32 devices in a mesh: half: 2 (over x), expert: 8 (over z, core), group: 2 (over y).
Axes of the slice: x: 2, y: 2, z: 4, core: 2. Of those that a mesh axis runs over, the one named last changes fastest.
Arguments:
- inputs: bfloat16 [2, 10240, 1024], P('half', ('expert', 'group')), may hold values from -6 to 6
- cotangent: bfloat16 [2, 10240, 1024], P('half', ('expert', 'group')), may hold values from -6 to 6
- enc_lengths: int32 [80], P(('expert', 'group')), may hold values from 32 to 512, as said below
- routes: int32 [2, 10240, 2], P('half', ('expert', 'group')), may hold values from 0 to 7, all different within a row; in each aligned block of 640 rows (0 to 639, 640 to 1279, ..., all dimensions but the last counted through in order) at most 200 rows name the same one
- norm_gains: float32 [2, 3, 1024], P('half'), may hold values from 0.25 to 1.75
- rel_bias: float32 [2, 16, 32], P('half'), may hold values from -4 to 4
- self_qkv: bfloat16 [2, 1024, 3072], P('half'), may hold values from -0.1875 to 0.1875
- self_out: bfloat16 [2, 1024, 1024], P('half'), may hold values from -1 to 1
- cross_proj: bfloat16 [2, 1024, 1024], P('half'), may hold values from -0.1875 to 0.1875
- cross_value: bfloat16 [2, 1024, 1024], P('half'), may hold values from -0.75 to 0.75
- router: float32 [2, 1024, 8], P('half'), may hold values from -0.125 to 0.125
- expert_in: bfloat16 [2, 8, 1024, 5632], P('half', 'expert'), may hold values from -0.1875 to 0.1875
- expert_out: bfloat16 [2, 8, 2816, 1024], P('half', 'expert'), may hold values from -0.15625 to 0.15625
Outputs:
- outputs: bfloat16 [2, 10240, 1024], P('half', ('expert', 'group'))
- grad_inputs: bfloat16 [2, 10240, 1024], P('half', ('expert', 'group'))
- grad_gains: float32 [2, 3, 1024], P('half', None, 'group')
- grad_bias: float32 [2, 16, 32], P('half', 'group')
- grad_qkv: float32 [2, 1024, 3072], P('half', 'group')
- grad_out: float32 [2, 1024, 1024], P('half', 'group')
- grad_cross_proj: float32 [2, 1024, 1024], P('half', 'group')
- grad_cross_value: float32 [2, 1024, 1024], P('half', 'group')
- grad_router: float32 [2, 1024, 8], P('half', 'group')
- grad_expert_in: float32 [2, 8, 1024, 5632], P('half', 'expert', None, 'group')
- grad_expert_out: float32 [2, 8, 2816, 1024], P('half', 'expert', 'group')
The draws below stay inside these ranges and needn't reach their ends.
Inputs may be any that keep to these rules, and one draw needn't show every extreme that they name: `enc_lengths`: each device's 5 encoder items, in order, fill its 640 rows exactly, and one item of each device is exactly 512 long. `routes`: each row names two different experts; among the rows of one device no expert is named more than 200 times.
All inputs are finite; a program needn't handle non-finite values.
Results may differ from the reference program's by a relative error of at most 0.025.
Values may be sent and summed in bfloat16 or wider, within the bound.
No kernel may reach another device: no remote copies, remote signals or barrier semaphores. Data moves between devices by JAX's collectives and lax.ppermute only.
A program may use at most 448 MiB of HBM per device.

```python
import math
from functools import reduce
import jax
import jax.numpy as jnp
import numpy as np
from jax import lax

D = 1024
H = 16
HD = 64
FF = 2816
NBKT = 32
DEC_SLOT = 128
DEC_LEN = 114
ENC_MOST = 512
ENC_MIN = 32
ITEMS = 5
E = 8
ROWS_DEV = 640
CAP = 200
DEVS_HALF = 16
TOK_HALF = 10240
N_EXPERT = 8
N_GROUP = 2


def draw_enc_lengths(key, part):
    key = jax.random.fold_in(key, 11)
    spare_rows = ROWS_DEV - ENC_MOST - (ITEMS - 1) * ENC_MIN
    key_cut, key_place = jax.random.split(key)
    cut_points = jnp.sort(jax.random.randint(key_cut, (DEVS_HALF, ITEMS - 2), 0, spare_rows + 1), axis=1)
    boundary = jnp.concatenate([jnp.zeros((DEVS_HALF, 1), jnp.int32), cut_points.astype(jnp.int32), jnp.full((DEVS_HALF, 1), spare_rows, jnp.int32)], axis=1)
    others = ENC_MIN + boundary[:, 1:] - boundary[:, :-1]
    long_place = jax.random.randint(key_place, (DEVS_HALF, 1), 0, ITEMS)
    columns = jnp.arange(ITEMS, dtype=jnp.int32)[None, :]
    shifted = jnp.where(columns > long_place, columns - 1, columns)
    picked = jnp.take_along_axis(others, jnp.minimum(shifted, ITEMS - 2), axis=1)
    lengths = jnp.where(columns == long_place, ENC_MOST, picked)
    return lengths.reshape(-1).astype(jnp.int32)


def block_scale(stream_key, dims, cuts, low, top_value):
    def one(axis_at, parts):
        draws = jax.random.uniform(jax.random.fold_in(jax.random.fold_in(stream_key, 6), axis_at), (parts,), jnp.float32, low / len(cuts), top_value / len(cuts))
        return jnp.repeat(jnp.exp(draws), dims[axis_at] // parts).reshape((-1,) + (1,) * (len(dims) - axis_at - 1))

    loudness = one(*cuts[0])
    for cut in cuts[1:]:
        loudness = loudness * one(*cut)
    return loudness


def shared_out(stream_key, own, number, rows, amount, top, reach, lean):
    ranking = jax.random.permutation(stream_key, amount)
    packed, ordinary = load_shares(amount, rows * top, reach, lean, True), load_shares(amount, rows * top, reach, lean, False)
    places = jnp.arange(amount)

    def named(sizes, offset_by):
        used = int((sizes > 0).sum())
        fixed = max(1, used // 4)
        passed = fixed + (places - fixed + offset_by * (used - fixed)) % max(1, amount - fixed)
        return jnp.zeros((amount,), jnp.int32).at[ranking[jnp.where(places < fixed, places, passed)]].set(jnp.asarray(sizes, jnp.int32))

    sizes = jnp.where(number % 4 == 0, named(packed, number // 4), named(ordinary, number - number // 4 - 1))
    mixed = jax.random.permutation(jax.random.fold_in(own, 3), amount)
    giver, receiver = mixed[0:amount // 2 * 2:2], mixed[1:amount // 2 * 2:2]
    margin = jnp.minimum(sizes[giver] - 1, reach - sizes[receiver]) // 2
    margin = jnp.where((giver == ranking[0]) | (receiver == ranking[0]) | (sizes[receiver] == 0), 0, jnp.maximum(margin, 0))
    passed = jax.random.randint(jax.random.fold_in(own, 4), (amount // 2,), 0, 1 << 20) % (margin + 1)
    sizes = sizes.at[giver].add(-passed).at[receiver].add(passed)
    items = jnp.searchsorted(jnp.cumsum(sizes), jnp.arange(rows * top), side="right").astype(jnp.int32)
    grid = items.reshape(top, rows).T
    grid = grid[jax.random.permutation(jax.random.fold_in(own, 1), rows)]
    offset_by = jax.random.randint(jax.random.fold_in(own, 2), (rows, 1), 0, top)
    return jnp.take_along_axis(grid, (jnp.arange(top)[None, :] + offset_by) % top, axis=1)


def load_shares(number_of, total, reach, slope, full):
    loads = [(1 << 20) // math.isqrt(standing ** slope) + 1 for standing in range(1, number_of + 1)]
    largest = reach if full else min(reach, max(-(-total // number_of), total * loads[0] // sum(loads)))
    least = 1 if total - largest >= number_of - 1 else 0
    given, spare = [largest] + [least] * (number_of - 1), total - largest - least * (number_of - 1)
    while spare > 0:
        candidates = [i for i in range(1, number_of) if given[i] < largest] or [i for i in range(1, number_of) if given[i] < reach]
        pool, remaining = sum([loads[i] for i in candidates]), spare
        for i in candidates:
            addition = min(reach - given[i], max(1, remaining * loads[i] // pool), spare)
            given[i] = given[i] + addition
            spare = spare - addition
    return np.array(given)


def normal_values(own_key, shape, width, reach, cuts=(), kind=jnp.bfloat16):
    result = jax.random.normal(own_key, shape, jnp.float32) * width
    if len(cuts) > 0:
        result = block_scale(own_key, shape, cuts, -0.22, 0.18) * result
    return jnp.clip(result, min=-reach, max=reach).astype(kind)


def setup_inputs(seed: int = 0) -> dict:
    key_list = jax.random.split(jax.random.key(seed), 14)
    inputs = normal_values(key_list[0], (2, TOK_HALF, D), 1.0, 6.0, ((0, 2), (1, 16)))
    cotangent = normal_values(key_list[1], (2, TOK_HALF, D), 1.0, 6.0, ((0, 2), (1, 16)))
    enc_lengths = draw_enc_lengths(jax.random.fold_in(key_list[13], 71), 0)
    routes_keys = jax.random.split(jax.random.fold_in(key_list[3], 1), 2 * TOK_HALF // ROWS_DEV)
    routes_turns = jax.random.permutation(jax.random.fold_in(key_list[3], 3), 2 * TOK_HALF // ROWS_DEV)
    routes = jax.vmap(lambda own, number: shared_out(jax.random.fold_in(key_list[3], 2), own, number, ROWS_DEV, E, 2, CAP, 2))(routes_keys, routes_turns).reshape((2, TOK_HALF, 2))
    norm_gains = jnp.clip(1.0 + 0.15 * jax.random.normal(key_list[4], (2, 3, D), jnp.float32), 0.25, 1.75)
    rel_bias = normal_values(key_list[5], (2, H, NBKT), 1.0, 4.0, ((0, 2),), jnp.float32)
    self_qkv = normal_values(key_list[6], (2, D, 3 * D), D ** -0.5, 0.1875, ((0, 2),))
    self_out = normal_values(key_list[7], (2, D, D), (D // 32) ** -0.5, 1.0, ((0, 2),))
    cross_proj = normal_values(key_list[8], (2, D, D), D ** -0.5, 0.1875, ((0, 2),))
    cross_value = normal_values(key_list[9], (2, D, D), (D // 16) ** -0.5, 0.75, ((0, 2),))
    router = normal_values(key_list[10], (2, D, E), (2 * D) ** -0.5, 0.125, ((0, 2),), jnp.float32)
    expert_in = normal_values(key_list[11], (2, E, D, 2 * FF), D ** -0.5, 0.1875, ((0, 2), (1, 8)))
    expert_out = normal_values(key_list[12], (2, E, FF, D), (FF // 2) ** -0.5, 0.15625, ((0, 2), (1, 8)))
    return {"inputs": inputs, "cotangent": cotangent, "enc_lengths": enc_lengths, "routes": routes, "norm_gains": norm_gains, "rel_bias": rel_bias, "self_qkv": self_qkv, "self_out": self_out, "cross_proj": cross_proj, "cross_value": cross_value, "router": router, "expert_in": expert_in, "expert_out": expert_out}


EPSILON = 1e-06
MASKED = -1e+30
HIGHEST = lax.Precision.HIGHEST

@jax.custom_vjp
def low(v):
    return lax.optimization_barrier(v.astype(jnp.bfloat16)).astype(jnp.float32)

@jax.custom_vjp
def low_back(v):
    return v

def low_keep(v):
    return (low(v), None)

def low_pass(kept, grad):
    return (grad,)

def back_keep(v):
    return (v, None)

def back_low(kept, grad):
    return (low(grad),)
low.defvjp(low_keep, low_pass)
low_back.defvjp(back_keep, back_low)

def bucket_limits(exact_range, growth, divisions):
    limits = []
    for number in range(1, divisions):
        candidate = exact_range
        while candidate ** divisions < exact_range ** divisions * growth ** number:
            candidate = candidate + 1
        limits.append(candidate)
    return limits

def rel_buckets(offset, causal):
    if causal:
        behind = jnp.maximum(-offset, 0)
        flags = [(behind >= threshold).astype(jnp.int32) for threshold in bucket_limits(16, 8, 16)]
        return jnp.minimum(behind, 16) + reduce(jnp.add, flags)
    distance = jnp.abs(offset)
    flags = [(distance >= threshold).astype(jnp.int32) for threshold in bucket_limits(8, 16, 8)]
    return (offset > 0).astype(jnp.int32) * 16 + jnp.minimum(distance, 8) + reduce(jnp.add, flags)

def rms_norm(values, gain_vec):
    return values * lax.rsqrt(lax.optimization_barrier(jnp.mean(values * values, axis=-1, keepdims=True)) + EPSILON) * gain_vec

def segment_ids(lengths, places):
    item_ends = jnp.cumsum(lengths)
    return lax.optimization_barrier(jnp.sum((places[:, None] >= item_ends[None, :]).astype(jnp.int32), axis=1))

def gate_values(normed, router_weight, routing):
    logits = jnp.dot(normed, router_weight, precision=HIGHEST)
    probabilities = jax.nn.softmax(logits, axis=-1)
    picked = jnp.take_along_axis(probabilities, routing, axis=1)
    return picked / lax.optimization_barrier(jnp.sum(picked, axis=1, keepdims=True))

def slot_targets(routing, experts, capacity):
    ordered = routing.T.reshape(-1)
    expert_hits = (ordered[:, None] == jnp.arange(experts, dtype=jnp.int32)[None, :]).astype(jnp.int32)
    earlier = jnp.cumsum(expert_hits, axis=0) - expert_hits
    slot_rank = lax.optimization_barrier(jnp.sum(earlier * expert_hits, axis=1))
    return (ordered * capacity + slot_rank).reshape(2, -1).T

def attention(queries, key_rows, value_rows, bias_part, allowed):
    scaling = queries.shape[-1] ** (-0.5)
    scores = low_back(jnp.einsum('qhd,khd->hqk', queries, key_rows, precision=HIGHEST) * scaling)
    scores = jnp.where(allowed[None], scores + bias_part, MASKED)
    highest = lax.optimization_barrier(jnp.max(scores, axis=-1, keepdims=True))
    exponent = jnp.exp(scores - highest)
    weights = exponent / lax.optimization_barrier(jnp.sum(exponent, axis=-1, keepdims=True))
    return jnp.einsum('hqk,khd->qhd', low(weights), value_rows, precision=HIGHEST)

def self_block(inputs_f, gain_vec, qkv_weight, out_weight, bias_part, allowed):
    row_count = inputs_f.shape[0]
    normed = low(rms_norm(inputs_f, gain_vec))
    project = low(low_back(jnp.dot(normed, qkv_weight, precision=HIGHEST))).reshape(row_count, 3, H, HD)
    context = attention(project[:, 0], project[:, 1], project[:, 2], bias_part, allowed)
    context = low(low_back(context)).reshape(row_count, D)
    return inputs_f + low_back(jnp.dot(context, out_weight, precision=HIGHEST))

def expert_block(inputs_f, gain_vec, router_weight, routing, expert_first, expert_second):
    normed = rms_norm(inputs_f, gain_vec)
    gate_rows = gate_values(normed, router_weight, routing)
    targets = slot_targets(routing, E, CAP)
    buffer = jnp.zeros((E * CAP, D), jnp.float32).at[targets[:, 0]].set(normed).at[targets[:, 1]].set(normed)
    buffer = low(low_back(buffer)).reshape(E, CAP, D)
    hidden = low_back(jnp.einsum('ecd,edf->ecf', buffer, expert_first, precision=HIGHEST))
    active = low(jax.nn.gelu(hidden[..., :FF]) * hidden[..., FF:])
    returned = jnp.einsum('ecf,efd->ecd', active, expert_second, precision=HIGHEST).reshape(E * CAP, D)
    returned = low(low_back(returned))
    return inputs_f + gate_rows[:, 0:1] * returned[targets[:, 0]] + gate_rows[:, 1:2] * returned[targets[:, 1]]

def pair_block(enc_in, dec_in, lengths, enc_route, dec_route, params):
    gains, bias_table, qkv_weight, out_weight, proj_weight, value_weight, router_weight, expert_first, expert_second = params
    row_count = enc_in.shape[0]
    places = jnp.arange(row_count, dtype=jnp.int32)
    offset = places[None, :] - places[:, None]
    segment = segment_ids(lengths, places)
    enc_allowed = segment[:, None] == segment[None, :]
    enc_bias = jnp.take(bias_table[0], rel_buckets(offset, False), axis=1)
    encoded = self_block(enc_in, gains[0, 0], qkv_weight[0], out_weight[0], enc_bias, enc_allowed)
    encoded = expert_block(encoded, gains[0, 1], router_weight[0], enc_route, expert_first[0], expert_second[0])
    memory = low(rms_norm(encoded, gains[0, 2]))
    key_rows = low(low_back(jnp.dot(memory, proj_weight[0], precision=HIGHEST))).reshape(row_count, H, HD)
    value_rows = low(low_back(jnp.dot(memory, value_weight[0], precision=HIGHEST))).reshape(row_count, H, HD)
    item_ids = places // DEC_SLOT
    dec_allowed = (item_ids[:, None] == item_ids[None, :]) & (offset <= 0) & (places[None, :] % DEC_SLOT < DEC_LEN)
    dec_bias = jnp.take(bias_table[1], rel_buckets(offset, True), axis=1)
    decoded = self_block(dec_in, gains[1, 0], qkv_weight[1], out_weight[1], dec_bias, dec_allowed)
    normed = low(rms_norm(decoded, gains[1, 1]))
    queries = low(low_back(jnp.dot(normed, proj_weight[1], precision=HIGHEST))).reshape(row_count, H, HD)
    cross_allowed = item_ids[:, None] == segment[None, :]
    context = attention(queries, key_rows, value_rows, 0.0, cross_allowed)
    context = low(low_back(context)).reshape(row_count, D)
    decoded = decoded + low_back(jnp.dot(context, value_weight[1], precision=HIGHEST))
    decoded = expert_block(decoded, gains[1, 2], router_weight[1], dec_route, expert_first[1], expert_second[1])
    return (encoded, decoded)

def reference(inputs, cotangent, enc_lengths, routes, norm_gains, rel_bias, self_qkv, self_out, cross_proj, cross_value, router, expert_in, expert_out):
    devices_half = N_EXPERT * N_GROUP
    starts = inputs.astype(jnp.float32).reshape(2, devices_half, ROWS_DEV, D)
    params = (norm_gains.astype(jnp.float32), rel_bias.astype(jnp.float32), self_qkv.astype(jnp.float32), self_out.astype(jnp.float32), cross_proj.astype(jnp.float32), cross_value.astype(jnp.float32), router.astype(jnp.float32), expert_in.astype(jnp.float32), expert_out.astype(jnp.float32))
    lengths = enc_lengths.reshape(devices_half, ITEMS)
    routing = routes.reshape(2, devices_half, ROWS_DEV, 2)
    checked = jax.checkpoint(pair_block)

    def forward(start_rows, weights_all):

        def one_device(pieces):
            return checked(pieces[0], pieces[1], pieces[2], pieces[3], pieces[4], weights_all)
        encoded, decoded = lax.map(one_device, (start_rows[0], start_rows[1], lengths, routing[0], routing[1]))
        return jnp.stack([encoded, decoded])
    outputs, pullback = jax.vjp(forward, starts, params)
    grad_starts, grad_params = pullback(cotangent.astype(jnp.float32).reshape(2, devices_half, ROWS_DEV, D))
    full_shape = (2, devices_half * ROWS_DEV, D)
    return (outputs.reshape(full_shape).astype(jnp.bfloat16), grad_starts.reshape(full_shape).astype(jnp.bfloat16), grad_params[0], grad_params[1], grad_params[2], grad_params[3], grad_params[4], grad_params[5], grad_params[6], grad_params[7], grad_params[8])
```

```python
from functools import partial

import jax
import jax.numpy as jnp
import numpy as np
from jax import lax
from jax.experimental import pallas as pl
from jax.experimental.pallas import tpu as pltpu
from jax.sharding import PartitionSpec as P

D = 1024
H = 16
HD = 64
FF = 2816
NBKT = 32
DEC_SLOT = 128
DEC_LEN = 114
ENC_MOST = 512
ENC_MIN = 32
ITEMS = 5

EPSILON = 1e-06
MASKED = -1e30
HIGHEST = lax.Precision.HIGHEST
BLOCK = 128
PAIRS = H // 2
DIAGONAL = ENC_MOST // BLOCK - 1
LINE = 2 * ENC_MOST
FF_TILE = 256
F32 = jnp.float32
BF16 = jnp.bfloat16
GELU_SCALE = float(np.sqrt(2.0 / np.pi))
GELU_CUBE = 0.044715
SWAP = ((0, 1), (1, 0))
VMEM_LIMIT = 60 * 1024 * 1024


def bucket_limits(exact_range, growth, divisions):
    limits = []
    for number in range(1, divisions):
        candidate = exact_range
        while candidate**divisions < exact_range**divisions * growth**number:
            candidate = candidate + 1
        limits.append(candidate)
    return limits


def rel_buckets(offset, causal):
    if causal:
        behind = np.maximum(-offset, 0)
        return np.minimum(behind, 16) + sum(
            (behind >= threshold).astype(np.int32) for threshold in bucket_limits(16, 8, 16)
        )
    distance = np.abs(offset)
    return (
        (offset > 0).astype(np.int32) * 16
        + np.minimum(distance, 8)
        + sum((distance >= threshold).astype(np.int32) for threshold in bucket_limits(8, 16, 8))
    )


def bucket_hits(offset, causal):
    return (rel_buckets(offset, causal)[:, None] == np.arange(NBKT)[None, :]).astype(np.float32)


def inverse_rms(values):
    return lax.rsqrt(jnp.mean(values * values, axis=-1, keepdims=True) + EPSILON)


def rms_norm(values, gain_vec):
    return values * inverse_rms(values) * gain_vec


def rms_back(grad_normed, values, gain_vec):
    scale = inverse_rms(values)
    unit = values * scale
    pulled = grad_normed * gain_vec
    grad_values = scale * (pulled - unit * jnp.mean(pulled * unit, axis=-1, keepdims=True))
    return grad_values, jnp.sum(grad_normed * unit, axis=0)


def dot(a, b):
    return jnp.dot(a, b, preferred_element_type=F32)


def dot_nt(a, b):
    return lax.dot_general(a, b, (((1,), (1,)), ((), ())), preferred_element_type=F32)


def dot_tn(a, b):
    return lax.dot_general(a, b, (((0,), (0,)), ((), ())), preferred_element_type=F32)


def skew(line, rows):
    width = line.shape[1]
    tile = jnp.broadcast_to(line, (8, width))
    row = lax.broadcasted_iota(jnp.int32, (8, width), 0)
    for step in (1, 2, 4):
        tile = jnp.where((row & step) != 0, pltpu.roll(tile, step, 1), tile)
    return jnp.concatenate(
        [pltpu.roll(tile, width - rows + first, 1) for first in range(0, rows, 8)], axis=0
    )


def unskew(total):
    rows, width = total.shape
    summed = None
    for first in range(0, rows, 8):
        moved = pltpu.roll(total[first : first + 8], rows - first, 1)
        summed = moved if summed is None else summed + moved
    row = lax.broadcasted_iota(jnp.int32, (8, width), 0)
    for step in (1, 2, 4):
        summed = jnp.where((row & step) != 0, pltpu.roll(summed, width - step, 1), summed)
    return jnp.sum(summed, axis=0, keepdims=True)


def own_lanes(head):
    return (lax.broadcasted_iota(jnp.int32, (1, 2 * HD), 1) // HD) == head


def head_lanes(head, value):
    return jnp.where(own_lanes(head), value, 0.0).astype(BF16)


def tile_places(keys, queries):
    key = lax.broadcasted_iota(jnp.int32, (keys, queries), 0)
    query = lax.broadcasted_iota(jnp.int32, (keys, queries), 1)
    return key, query


def causal_tile():
    key, query = tile_places(BLOCK, BLOCK)
    return (key <= query) & (key < DEC_LEN)


def short_tile():
    key, query = tile_places(BLOCK, BLOCK)
    return (key // ENC_MIN) == (query // ENC_MIN)


def bias_tiles(rows, queries, shares):
    return [
        (
            slice(block * BLOCK, (block + 1) * BLOCK),
            slice((DIAGONAL - block % (rows // BLOCK // shares)) * BLOCK, None),
            queries,
        )
        for block in range(rows // BLOCK)
    ]


def add_bias(scores, bias_ref, head, shares):
    rows, queries = scores.shape
    return joined(
        [
            scores[here] + bias_ref[head, :, lanes.start : lanes.start + queries]
            for here, lanes, queries in bias_tiles(rows, queries, shares)
        ]
    )


def add_bias_grad(dbias_ref, head, grad_scores, shares):
    rows, queries = grad_scores.shape
    sums = {}
    for here, lanes, queries in bias_tiles(rows, queries, shares):
        part = grad_scores[here]
        sums[lanes.start] = sums[lanes.start] + part if lanes.start in sums else part
    for first, part in sums.items():
        dbias_ref[head, :, first : first + queries] += part


def masked(scores, mask):
    return scores if mask is None else jnp.where(mask, scores, MASKED)


def key_parts(rows, shares):
    step = rows.shape[0] // shares
    return [rows[first : first + step] for first in range(0, rows.shape[0], step)]


def spread_max(values, shares):
    return [jnp.max(part, axis=0, keepdims=True) for part in key_parts(values, shares)]


def joined(parts):
    return parts[0] if len(parts) == 1 else jnp.concatenate(parts, axis=0)


def per_share(lines, rows):
    step = rows // len(lines)
    if len(lines) == 1:
        return lines[0]
    return jnp.concatenate(
        [jnp.broadcast_to(line, (step, line.shape[1])) for line in lines], axis=0
    )


def attend_groups(groups, bias_ref):
    units = [(group, head) for group in groups for head in range(2)]
    scores = []
    for (queries, keys, values, mask), head in units:
        scale = head_lanes(head, HD**-0.5)
        part = joined([dot_nt(key, query * scale) for query, key in zip(queries, keys)])
        scores.append(part)
    contexts = []
    log_sums = []
    for ((queries, keys, values, mask), head), part in zip(units, scores):
        shares = len(queries)
        if bias_ref is not None:
            part = add_bias(part, bias_ref, head, shares)
        part = masked(part, mask)
        highest = spread_max(part, shares)
        exponent = jnp.exp(part - per_share(highest, part.shape[0]))
        totals = [jnp.sum(rows, axis=0, keepdims=True) for rows in key_parts(exponent, shares)]
        log_sums.append([top + jnp.log(total) for top, total in zip(highest, totals)])
        rounded = key_parts(exponent.astype(BF16), shares)
        contexts.append(
            [
                dot_tn(rows, jnp.where(own_lanes(head), value, jnp.ones_like(value)))
                for rows, value in zip(rounded, values)
            ]
        )
    results = []
    for number in range(len(groups)):
        rows = []
        lines = []
        for share in range(len(groups[number][0])):
            first, second = contexts[2 * number][share], contexts[2 * number + 1][share]
            sums = jnp.where(own_lanes(0), second, first)
            context = jnp.where(own_lanes(0), first, second) / pltpu.roll(sums, HD, 1)
            rows.append(context.astype(BF16))
            lines.append(
                jnp.concatenate(
                    [log_sums[2 * number][share], log_sums[2 * number + 1][share]], axis=0
                )
            )
        results.append((rows, lines))
    return results


def attend_groups_back(groups, bias_ref, dbias_ref):
    units = [(group, head) for group in groups for head in range(2)]
    scores = []
    pulls = []
    for (queries, keys, values, mask, grads, lines), head in units:
        scale = head_lanes(head, HD**-0.5)
        own = head_lanes(head, 1.0)
        scores.append(joined([dot_nt(key, query * scale) for query, key in zip(queries, keys)]))
        pulls.append(joined([dot_nt(value, grad * own) for value, grad in zip(values, grads)]))
    totals = []
    for ((queries, keys, values, mask, grads, lines), head), part, pull in zip(units, scores, pulls):
        shares = len(queries)
        scale = head_lanes(head, HD**-0.5)
        own = head_lanes(head, 1.0)
        if bias_ref is not None:
            part = add_bias(part, bias_ref, head, shares)
        part = masked(part, mask)
        weights = jnp.exp(part - per_share([line[head : head + 1] for line in lines], part.shape[0]))
        product = weights * pull
        inner = [jnp.sum(rows, axis=0, keepdims=True) for rows in key_parts(product, shares)]
        grad_scores = product - weights * per_share(inner, part.shape[0])
        if dbias_ref is not None:
            add_bias_grad(dbias_ref, head, grad_scores, shares)
        rounded = key_parts(grad_scores.astype(BF16), shares)
        weights = key_parts(weights.astype(BF16), shares)
        totals.append(
            [
                [dot_tn(rows, key * scale) for rows, key in zip(rounded, keys)],
                [dot(rows, query * scale) for rows, query in zip(rounded, queries)],
                [dot(rows, grad * own) for rows, grad in zip(weights, grads)],
            ]
        )
    results = []
    for number in range(len(groups)):
        results.append(
            [
                [(one + two).astype(BF16) for one, two in zip(first, second)]
                for first, second in zip(totals[2 * number], totals[2 * number + 1])
            ]
        )
    return results


def short_places(place, item):
    later = (item >= place).astype(jnp.int32)
    return pl.multiple_of(item * ENC_MIN + later * ENC_MOST, ENC_MIN), item + later


def gather_short(ref, place):
    return jnp.concatenate(
        [ref[pl.ds(short_places(place, item)[0], ENC_MIN), :] for item in range(ITEMS - 1)], axis=0
    )


def scatter_short(ref, place, rows):
    for item in range(ITEMS - 1):
        ref[pl.ds(short_places(place, item)[0], ENC_MIN), :] = rows[
            item * ENC_MIN : (item + 1) * ENC_MIN
        ]


def block_rows(block):
    return slice(block * BLOCK, (block + 1) * BLOCK)


def self_attend_kernel(place_ref, q_ref, k_ref, v_ref, line_ref, out_ref, lse_ref, bias_ref):
    for head in range(2):
        bias_ref[head] = skew(line_ref[0, head : head + 1, :], BLOCK)
    place = place_ref[0]
    decoder = place_ref[1] == 1

    @pl.when(decoder)
    def _():
        blocks = [block_rows(block) for block in range(ITEMS)]
        shares = tuple([ref[here, :] for here in blocks] for ref in (q_ref, k_ref, v_ref))
        ((rows, lines),) = attend_groups([shares + (joined([causal_tile()] * ITEMS),)], bias_ref)
        for here, part, line in zip(blocks, rows, lines):
            out_ref[here, :] = part
            lse_ref[0, :, here] = line

    @pl.when(jnp.logical_not(decoder))
    def _():
        here = pl.ds(pl.multiple_of(place * ENC_MIN, ENC_MIN), ENC_MOST)
        groups = [
            ([q_ref[here, :]], [k_ref[here, :]], [v_ref[here, :]], None),
            tuple([gather_short(ref, place)] for ref in (q_ref, k_ref, v_ref)) + (short_tile(),),
        ]
        ((rows, lines),) = attend_groups(groups[:1], bias_ref)
        out_ref[here, :] = rows[0]
        lse_ref[0, :, :ENC_MOST] = lines[0]
        ((short_rows, short_lines),) = attend_groups(groups[1:], bias_ref)
        scatter_short(out_ref, place, short_rows[0])
        lse_ref[0, :, ENC_MOST:] = short_lines[0]


def self_attend_back_kernel(
    place_ref, q_ref, k_ref, v_ref, dc_ref, lse_ref, line_ref,
    dq_ref, dk_ref, dv_ref, dline_ref, bias_ref, dbias_ref,
):
    for head in range(2):
        bias_ref[head] = skew(line_ref[0, head : head + 1, :], BLOCK)
    dbias_ref[...] = jnp.zeros(dbias_ref.shape, F32)
    place = place_ref[0]
    decoder = place_ref[1] == 1
    outs = (dq_ref, dk_ref, dv_ref)

    @pl.when(decoder)
    def _():
        blocks = [block_rows(block) for block in range(ITEMS)]
        shares = tuple([ref[here, :] for here in blocks] for ref in (q_ref, k_ref, v_ref))
        shares += (
            joined([causal_tile()] * ITEMS),
            [dc_ref[here, :] for here in blocks],
            [lse_ref[0, :, here] for here in blocks],
        )
        (grads,) = attend_groups_back([shares], bias_ref, dbias_ref)
        for ref, rows in zip(outs, grads):
            for here, part in zip(blocks, rows):
                ref[here, :] = part

    @pl.when(jnp.logical_not(decoder))
    def _():
        here = pl.ds(pl.multiple_of(place * ENC_MIN, ENC_MIN), ENC_MOST)
        groups = [
            (
                [q_ref[here, :]],
                [k_ref[here, :]],
                [v_ref[here, :]],
                None,
                [dc_ref[here, :]],
                [lse_ref[0, :, :ENC_MOST]],
            ),
            (
                [gather_short(q_ref, place)],
                [gather_short(k_ref, place)],
                [gather_short(v_ref, place)],
                short_tile(),
                [gather_short(dc_ref, place)],
                [lse_ref[0, :, ENC_MOST:]],
            ),
        ]
        grads, short_grads = attend_groups_back(groups, bias_ref, dbias_ref)
        for ref, rows, short_rows in zip(outs, grads, short_grads):
            ref[here, :] = rows[0]
            scatter_short(ref, place, short_rows[0])

    for head in range(2):
        dline_ref[0, head : head + 1, :] = unskew(dbias_ref[head])


def cross_places(place):
    long_pair = (
        pl.ds(pl.multiple_of(place * BLOCK, BLOCK), BLOCK),
        pl.ds(pl.multiple_of(place * ENC_MIN, ENC_MIN), ENC_MOST),
    )
    pairs = []
    for item in range(ITEMS - 1):
        start, number = short_places(place, item)
        pairs.append(
            (pl.ds(pl.multiple_of(number * BLOCK, BLOCK), BLOCK), pl.ds(start, ENC_MIN))
        )
    return [[long_pair], pairs]


def cross_attend_kernel(place_ref, q_ref, k_ref, v_ref, out_ref, lse_ref):
    places = cross_places(place_ref[0])
    groups = [
        (
            [q_ref[here, :] for here, there in pairs],
            [k_ref[there, :] for here, there in pairs],
            [v_ref[there, :] for here, there in pairs],
            None,
        )
        for pairs in places
    ]
    number = 0
    for pairs, (rows, lines) in zip(places, attend_groups(groups, None)):
        for (here, there), part, line in zip(pairs, rows, lines):
            out_ref[here, :] = part
            lse_ref[0, :, block_rows(number)] = line
            number += 1


def cross_attend_back_kernel(
    place_ref, q_ref, k_ref, v_ref, dc_ref, lse_ref, dq_ref, dk_ref, dv_ref
):
    places = cross_places(place_ref[0])
    lines = [lse_ref[0, :, block_rows(number)] for number in range(ITEMS)]
    groups = [
        (
            [q_ref[here, :] for here, there in pairs],
            [k_ref[there, :] for here, there in pairs],
            [v_ref[there, :] for here, there in pairs],
            None,
            [dc_ref[here, :] for here, there in pairs],
            part,
        )
        for pairs, part in zip(places, (lines[:1], lines[1:]))
    ]
    for pairs, grads in zip(places, attend_groups_back(groups, None, None)):
        for number, (here, there) in enumerate(pairs):
            dq_ref[here, :] = grads[0][number]
            dk_ref[there, :] = grads[1][number]
            dv_ref[there, :] = grads[2][number]


def pair_spec(rows, first):
    return pl.BlockSpec((rows, 2 * HD), lambda pair, places: (0, first + pair))


def flat_spec(*shape):
    return pl.BlockSpec((1,) + shape, lambda pair, places: (pair, 0, 0))


def pair_call(kernel, places, operands, specs, out_specs, out_shape, scratch, work):
    rows = ITEMS * BLOCK
    return pl.pallas_call(
        kernel,
        grid_spec=pltpu.PrefetchScalarGridSpec(
            num_scalar_prefetch=1,
            grid=(PAIRS,),
            in_specs=specs,
            out_specs=out_specs,
            scratch_shapes=scratch,
        ),
        out_shape=out_shape,
        compiler_params=pltpu.CompilerParams(vmem_limit_bytes=VMEM_LIMIT),
        cost_estimate=pl.CostEstimate(
            flops=work * rows * rows * D, bytes_accessed=16 * rows * D, transcendentals=rows * rows * H
        ),
        name=kernel.__name__,
    )(places, *operands)


def attend(query, keys, values, places, lines):
    rows = query[0].shape[0]
    operands = [part[0] for part in (query, keys, values)]
    specs = [pair_spec(rows, part[1]) for part in (query, keys, values)]
    scratch = []
    if lines is not None:
        operands.append(lines)
        specs.append(flat_spec(2, LINE))
        scratch.append(pltpu.VMEM((2, BLOCK, LINE), F32))
    return pair_call(
        cross_attend_kernel if lines is None else self_attend_kernel,
        places,
        operands,
        specs,
        [pair_spec(rows, 0), flat_spec(2, rows)],
        [
            jax.ShapeDtypeStruct((rows, D), BF16),
            jax.ShapeDtypeStruct((PAIRS, 2, rows), F32),
        ],
        scratch,
        4,
    )


def attend_back(query, keys, values, grad_context, lse, places, lines):
    rows = query[0].shape[0]
    operands = [part[0] for part in (query, keys, values)] + [grad_context, lse]
    specs = [pair_spec(rows, part[1]) for part in (query, keys, values)]
    specs += [pair_spec(rows, 0), flat_spec(2, rows)]
    out_specs = [pair_spec(rows, 0)] * 3
    out_shape = [jax.ShapeDtypeStruct((rows, D), BF16)] * 3
    scratch = []
    if lines is not None:
        operands.append(lines)
        specs.append(flat_spec(2, LINE))
        out_specs.append(flat_spec(2, LINE))
        out_shape.append(jax.ShapeDtypeStruct((PAIRS, 2, LINE), F32))
        scratch += [pltpu.VMEM((2, BLOCK, LINE), F32)] * 2
    return pair_call(
        cross_attend_back_kernel if lines is None else self_attend_back_kernel,
        places,
        operands,
        specs,
        out_specs,
        out_shape,
        scratch,
        10,
    )


def exchange(rows, experts):
    parts = rows.reshape(experts, -1, rows.shape[-1])
    return lax.all_to_all(parts, "expert", split_axis=0, concat_axis=0, tiled=True).reshape(
        rows.shape
    )


def gelu_parts(value):
    square = value * value
    bend = jnp.tanh(value * (GELU_SCALE + GELU_SCALE * GELU_CUBE * square))
    half = 0.5 + 0.5 * bend
    slope = half + value * (half * (1.0 - bend)) * (
        GELU_SCALE + 3.0 * GELU_SCALE * GELU_CUBE * square
    )
    return value * half, slope


def row_blocks(rows):
    step = rows // 2
    return [slice(first, first + step) for first in range(0, rows, step)]


def expert_forward_kernel(x_ref, gate_ref, up_ref, down_ref, out_ref, total_ref):
    @pl.when(pl.program_id(0) == 0)
    def _():
        total_ref[...] = jnp.zeros(total_ref.shape, F32)

    for here in row_blocks(x_ref.shape[0]):
        rows = x_ref[here, :]
        value, _ = gelu_parts(dot(rows, gate_ref[...]))
        active = (value * dot(rows, up_ref[...])).astype(BF16)
        total_ref[here, :] += dot(active, down_ref[...])

    @pl.when(pl.program_id(0) == pl.num_programs(0) - 1)
    def _():
        out_ref[...] = total_ref[...].astype(BF16)


def hidden_grads(rows, grad_rows, gate_ref, up_ref, down_ref):
    gate = dot(rows, gate_ref[...])
    up = dot(rows, up_ref[...])
    grad_active = dot_nt(grad_rows, down_ref[...])
    value, slope = gelu_parts(gate)
    grad_gate = (grad_active * (up * slope)).astype(BF16)
    grad_up = (grad_active * value).astype(BF16)
    return value * up, grad_active, grad_gate, grad_up


def expert_both_kernel(
    x_ref, g_ref, gate_ref, up_ref, down_ref,
    dx_ref, out_ref, line_ref, dx_total, out_total, line_total,
):
    @pl.when(pl.program_id(0) == 0)
    def _():
        dx_total[...] = jnp.zeros(dx_total.shape, F32)
        out_total[...] = jnp.zeros(out_total.shape, F32)
        line_total[...] = jnp.zeros(line_total.shape, F32)

    for here in row_blocks(x_ref.shape[0]):
        active, grad_active, grad_gate, grad_up = hidden_grads(
            x_ref[here, :], g_ref[here, :], gate_ref, up_ref, down_ref
        )
        dx_total[here, :] += dot_nt(grad_gate, gate_ref[...]) + dot_nt(grad_up, up_ref[...])
        out_total[here, :] += dot(active.astype(BF16), down_ref[...])
        product = active * grad_active
        line_total[here, :] += sum(
            product[:, first : first + 128] for first in range(0, product.shape[1], 128)
        )

    @pl.when(pl.program_id(0) == pl.num_programs(0) - 1)
    def _():
        dx_ref[...] = dx_total[...].astype(BF16)
        out_ref[...] = out_total[...].astype(BF16)
        line_ref[...] = jnp.sum(line_total[...], axis=1, keepdims=True)


def expert_back_kernel(flags_ref, *refs, count):
    one_ref, two_ref, three_ref, scale_ref, gate_ref, up_ref, down_ref = refs[:7]
    dx_ref, x_ref, g_ref, active_ref, keep_ref, send_ref, dx_total, sems = refs[-8:]
    decoder = flags_ref[0] == 1
    first_group = flags_ref[1] == 0
    most = x_ref.shape[1]
    spare = slice(count, most)

    def load(rows, grads):
        copies = [
            pltpu.make_async_copy(rows, x_ref.at[0, pl.ds(0, count)], sems.at[0]),
            pltpu.make_async_copy(grads, g_ref.at[0, pl.ds(0, count)], sems.at[1]),
        ]
        for copy in copies:
            copy.start()
        for copy in copies:
            copy.wait()

    @pl.when(pl.program_id(0) == 0)
    def _():
        dx_total[...] = jnp.zeros(dx_total.shape, F32)

        @pl.when(decoder)
        def _():
            load(two_ref, one_ref)

        @pl.when(jnp.logical_not(decoder))
        def _():
            load(one_ref, three_ref)

        grads = g_ref[0, :count, :].astype(F32) * scale_ref[...]
        g_ref[0, :count, :] = grads.astype(BF16)
        if count < most:
            x_ref[0, spare, :] = jnp.zeros((most - count, D), BF16)
            g_ref[0, spare, :] = jnp.zeros((most - count, D), BF16)

    for here in row_blocks(count):
        active, _, grad_gate, grad_up = hidden_grads(
            x_ref[0, here, :], g_ref[0, here, :], gate_ref, up_ref, down_ref
        )
        dx_total[here, :] += dot_nt(grad_gate, gate_ref[...]) + dot_nt(grad_up, up_ref[...])
        active_ref[0, here, :] = active.astype(BF16)
        keep_ref[0, here, :] = jnp.where(first_group, grad_gate, grad_up)
        send_ref[0, here, :] = jnp.where(first_group, grad_up, grad_gate)
    if count < most:
        for ref in (active_ref, keep_ref, send_ref):
            ref[0, spare, :] = jnp.zeros((most - count, FF_TILE), BF16)

    @pl.when(pl.program_id(0) == pl.num_programs(0) - 1)
    def _():
        dx_ref[...] = dx_total[...].astype(BF16)


def expert_specs(rows):
    tiles = FF // FF_TILE
    whole = pl.BlockSpec((rows, D), lambda tile, *_: (0, 0))
    weight_specs = [
        pl.BlockSpec((D, FF_TILE), lambda tile, *_: (0, tile)),
        pl.BlockSpec((D, FF_TILE), lambda tile, *_: (0, tiles + tile)),
        pl.BlockSpec((FF_TILE, D), lambda tile, *_: (tile, 0)),
    ]
    return whole, weight_specs, tiles


def expert_cost(rows, products):
    return pl.CostEstimate(
        flops=2 * products * rows * D * FF, bytes_accessed=6 * D * FF, transcendentals=rows * FF
    )


def expert_forward(arrived, expert_first, expert_second):
    rows = arrived.shape[0]
    whole, weight_specs, tiles = expert_specs(rows)
    return pl.pallas_call(
        expert_forward_kernel,
        grid=(tiles,),
        in_specs=[whole] + weight_specs,
        out_specs=whole,
        out_shape=jax.ShapeDtypeStruct((rows, D), BF16),
        scratch_shapes=[pltpu.VMEM((rows, D), F32)],
        compiler_params=pltpu.CompilerParams(vmem_limit_bytes=VMEM_LIMIT),
        cost_estimate=expert_cost(rows, 3),
        name="expert_forward",
    )(arrived, expert_first, expert_first, expert_second)


def expert_both(arrived, grad_rows, expert_first, expert_second):
    rows = arrived.shape[0]
    whole, weight_specs, tiles = expert_specs(rows)
    row_shape = jax.ShapeDtypeStruct((rows, D), BF16)
    total = pltpu.VMEM((rows, D), F32)
    return pl.pallas_call(
        expert_both_kernel,
        grid=(tiles,),
        in_specs=[whole, whole] + weight_specs,
        out_specs=[whole, whole, pl.BlockSpec((rows, 1), lambda tile: (0, 0))],
        out_shape=[row_shape, row_shape, jax.ShapeDtypeStruct((rows, 1), F32)],
        scratch_shapes=[total, total, pltpu.VMEM((rows, 128), F32)],
        compiler_params=pltpu.CompilerParams(vmem_limit_bytes=VMEM_LIMIT),
        cost_estimate=expert_cost(rows, 6),
        name="expert_both",
    )(arrived, grad_rows, expert_first, expert_first, expert_second)


def expert_back(flags, one, two, three, scale, expert_first, expert_second, kept, number, most):
    rows = one.shape[0]
    whole, weight_specs, tiles = expert_specs(rows)
    part = pl.BlockSpec((1, most, D), lambda tile, *_: (number, 0, 0))
    strip = pl.BlockSpec((1, most, FF_TILE), lambda tile, *_: (number, 0, tile))
    kept_shapes = [jax.ShapeDtypeStruct((2, most, D), BF16)] * 2
    kept_shapes += [jax.ShapeDtypeStruct((2, most, FF), BF16)] * 3
    anywhere = pl.BlockSpec(memory_space=pl.ANY)
    in_specs = [anywhere] * 3 + [pl.BlockSpec((rows, 1), lambda tile, *_: (0, 0))] + weight_specs
    operands = [one, two, three, scale, expert_first, expert_first, expert_second]
    aliases = {}
    if kept is not None:
        aliases = {1 + len(operands) + place: 1 + place for place in range(len(kept))}
        in_specs += [anywhere] * len(kept)
        operands += kept
    dx, *kept = pl.pallas_call(
        partial(expert_back_kernel, count=rows),
        grid_spec=pltpu.PrefetchScalarGridSpec(
            num_scalar_prefetch=1,
            grid=(tiles,),
            in_specs=in_specs,
            out_specs=[whole, part, part, strip, strip, strip],
            scratch_shapes=[pltpu.VMEM((rows, D), F32), pltpu.SemaphoreType.DMA((2,))],
        ),
        out_shape=[jax.ShapeDtypeStruct((rows, D), BF16)] + kept_shapes,
        input_output_aliases=aliases,
        compiler_params=pltpu.CompilerParams(vmem_limit_bytes=VMEM_LIMIT),
        cost_estimate=expert_cost(rows, 5),
        name="expert_back",
    )(flags, *operands)
    return dx, list(kept)


def gate_pair(normed, router_weight, picked_first, picked_second):
    logits = jnp.dot(normed, router_weight, precision=HIGHEST)
    first = jnp.sum(logits * picked_first, axis=1, keepdims=True)
    second = jnp.sum(logits * picked_second, axis=1, keepdims=True)
    return jax.nn.sigmoid(first - second), jax.nn.sigmoid(second - first)


def group_swap(rows, group):
    half = rows.shape[0] // 2
    sent = lax.dynamic_slice_in_dim(rows, (1 - group) * half, half, 0)
    kept = lax.dynamic_slice_in_dim(rows, group * half, half, 0)
    return kept + lax.ppermute(sent, "group", SWAP)


def shard_rows(grad):
    rows, columns = grad.shape
    parts = grad.astype(BF16).reshape(2, lax.axis_size("expert"), -1, columns)
    return jnp.swapaxes(parts, 0, 1).reshape(rows, columns)


def expert_scatter(rows):
    return lax.psum_scatter(rows, "expert", scatter_dimension=0, tiled=True)


def expert_gather(rows):
    return lax.all_gather(rows, "expert", axis=0, tiled=True)


def together(*values):
    return lax.optimization_barrier(values)


def per_device(
    inputs,
    cotangent,
    enc_lengths,
    routes,
    norm_gains,
    rel_bias,
    self_qkv,
    self_out,
    cross_proj,
    cross_value,
    router,
    expert_in,
    expert_out,
):
    decoder = lax.axis_index("half") == 1
    group = lax.axis_index("group")
    start_rows = inputs[0].astype(F32)
    row_count = start_rows.shape[0]
    gain_rows = norm_gains[0]
    bias_table = rel_bias[0]
    qkv_weight = self_qkv[0]
    out_weight = self_out[0]
    proj_weight = cross_proj[0]
    value_weight = cross_value[0]
    router_weight = router[0]
    expert_first = expert_in[0, 0]
    expert_second = expert_out[0, 0]
    routing = routes[0]
    experts = router_weight.shape[1]
    cot = cotangent[0]
    cot_f = cot.astype(F32)

    forward = [(0, 1)]
    backward = [(1, 0)]
    half_rows = D // 2
    both_weights = jnp.concatenate([proj_weight, value_weight])
    pieces = [both_weights[first:last] for first, last in ((0, 384), (384, 960), (960, 1536), (1536, 2048))]

    long_place = jnp.sum(jnp.arange(ITEMS) * (enc_lengths == ENC_MOST)).astype(jnp.int32)
    places = jnp.stack([long_place, decoder.astype(jnp.int32)])
    offsets = ENC_MOST - np.arange(LINE)
    hits = jnp.where(decoder, bucket_hits(offsets, True), bucket_hits(offsets, False))
    lines = jnp.dot(bias_table, hits.T, precision=HIGHEST).reshape(PAIRS, 2, LINE)

    capacity = 5 * row_count // (2 * experts)
    padded = -(-capacity // 8) * 8
    first_chunk = padded // 16 * 8
    chunk_sizes = (first_chunk, padded - first_chunk)
    picked = [
        (routing[:, k : k + 1] == jnp.arange(experts, dtype=jnp.int32)[None, :]).astype(F32)
        for k in range(2)
    ]
    before = jnp.asarray(np.tril(np.ones((row_count, row_count)), -1), BF16)
    counts = dot(before, jnp.concatenate(picked, axis=1).astype(BF16))
    totals = jnp.sum(picked[0], axis=0, keepdims=True)
    slot_first = jnp.sum(picked[0] * counts[:, :experts], axis=1)
    slot_second = jnp.sum(picked[1] * (counts[:, experts:] + totals), axis=1)
    code_first = routing[:, 0] * padded + slot_first.astype(jnp.int32)
    code_second = routing[:, 1] * padded + slot_second.astype(jnp.int32)
    chunk_codes = []
    offset = 0
    for size in chunk_sizes:
        chunk_codes.append(
            (np.arange(experts)[:, None] * padded + offset + np.arange(size)[None, :])
            .reshape(-1)
            .astype(np.int32)
        )
        offset += size

    def spread(first_values, second_values):
        buffers = []
        for codes in chunk_codes:
            hit_first = (codes[:, None] == code_first[None, :]).astype(BF16)
            hit_second = (codes[:, None] == code_second[None, :]).astype(BF16)
            if first_values is second_values:
                buffers.append(dot(hit_first + hit_second, first_values).astype(BF16))
            else:
                buffers.append(
                    (dot(hit_first, first_values) + dot(hit_second, second_values)).astype(BF16)
                )
        return buffers

    def collect(buffers, code):
        total = None
        for codes, buffer in zip(chunk_codes, buffers):
            part = dot((code[:, None] == codes[None, :]).astype(BF16), buffer)
            total = part if total is None else total + part
        return total

    normed_in = rms_norm(start_rows, gain_rows[0]).astype(BF16)
    project = dot(normed_in, qkv_weight).astype(BF16)
    project, pieces[0] = together(project, pieces[0])
    query, keys, values = (project, 0), (project, PAIRS), (project, 2 * PAIRS)
    context, lse = attend(query, keys, values, places, lines)
    context, pieces[0] = together(context, lax.ppermute(pieces[0], "half", forward))
    first_half = start_rows + dot(context, out_weight)
    normed_half = rms_norm(first_half, gain_rows[1])
    rounded_half = normed_half.astype(BF16)

    first_rows = jnp.where(decoder, cot, rounded_half)
    sent = spread(first_rows, first_rows)
    arrived_one = [exchange(part, experts) for part in sent]
    returned_one = []
    for k in range(2):
        part, piece = together(arrived_one[k], pieces[1 + k])
        part = expert_forward(part, expert_first, expert_second)
        part, pieces[1 + k] = together(part, lax.ppermute(piece, "half", forward))
        if k == 1:
            part, pieces[3] = together(part, pieces[3])
        returned_one.append(exchange(part, experts))
    returned_one[1], pieces[3] = together(
        returned_one[1], lax.ppermute(pieces[3], "half", forward)
    )
    both_weights = jnp.concatenate(pieces)
    memory_proj, memory_value = both_weights[:D], both_weights[D:]
    enc_gates = gate_pair(normed_half, router_weight, *picked)
    enc_first = collect(returned_one, code_first)
    enc_second = collect(returned_one, code_second)
    encoded = first_half + enc_gates[0] * enc_first + enc_gates[1] * enc_second
    memory = rms_norm(encoded, gain_rows[2]).astype(BF16)
    memory_in = lax.ppermute(memory, "half", forward)

    cross_query = dot(rounded_half, proj_weight).astype(BF16)
    memory_keys = dot(memory_in, memory_proj).astype(BF16)
    memory_values = dot(memory_in, memory_value).astype(BF16)
    cross_context, cross_lse = attend(
        (cross_query, 0), (memory_keys, 0), (memory_values, 0), places, None
    )
    second_half = first_half + dot(cross_context, value_weight)
    normed_second = rms_norm(second_half, gain_rows[2])
    dec_gates = gate_pair(normed_second, router_weight, *picked)

    rounded_second = normed_second.astype(BF16)
    arrived_two = [exchange(part, experts) for part in spread(rounded_second, rounded_second)]
    all_codes = np.concatenate(chunk_codes)
    gate_rows = jnp.sum(
        jnp.where(all_codes[:, None] == code_first[None, :], dec_gates[0][:, 0][None, :], 0.0)
        + jnp.where(all_codes[:, None] == code_second[None, :], dec_gates[1][:, 0][None, :], 0.0),
        axis=1,
    )
    edge = experts * chunk_sizes[0]

    def exchange_line(line):
        parts = jnp.concatenate(
            [line[:edge].reshape(experts, -1), line[edge:].reshape(experts, -1)], axis=1
        )
        moved = lax.all_to_all(parts, "expert", split_axis=0, concat_axis=0, tiled=True)
        return jnp.concatenate(
            [moved[:, : chunk_sizes[0]].reshape(-1), moved[:, chunk_sizes[0] :].reshape(-1)]
        )

    produced_two = []
    returned_two = []
    gate_grads = []
    for part, grad_part in zip(arrived_two, arrived_one):
        grad_arrived, produced, line = expert_both(part, grad_part, expert_first, expert_second)
        gate_grads.append(line[:, 0])
        produced_two.append(produced)
        returned_two.append(exchange(grad_arrived, experts))
    returned_two[0], line_grads = together(returned_two[0], jnp.concatenate(gate_grads))
    line_grads = exchange_line(line_grads)

    def collect_line(line, code):
        return jnp.sum(
            jnp.where(code[:, None] == all_codes[None, :], line[None, :], 0.0), axis=1, keepdims=True
        )

    def router_back(gates, grad_first, grad_second):
        pulled = gates[0] * gates[1] * (grad_first - grad_second)
        grad_logits = pulled * (picked[0] - picked[1])
        return grad_logits, jnp.dot(grad_logits, router_weight.T, precision=HIGHEST)

    dec_logits, dec_normed = router_back(
        dec_gates, collect_line(line_grads, code_first), collect_line(line_grads, code_second)
    )
    dec_normed = (
        dec_normed
        + dec_gates[0] * collect(returned_two, code_first)
        + dec_gates[1] * collect(returned_two, code_second)
    )
    pulled_rows, gain_dec_moe = rms_back(dec_normed, second_half, gain_rows[2])
    grad_second_half = cot_f + pulled_rows

    rounded_grad = grad_second_half.astype(BF16)
    grad_cross_context = dot_nt(rounded_grad, value_weight).astype(BF16)
    grad_cross_query, grad_memory_keys, grad_memory_values = attend_back(
        (cross_query, 0),
        (memory_keys, 0),
        (memory_values, 0),
        grad_cross_context,
        cross_lse,
        places,
        None,
    )
    key_part = dot_nt(grad_memory_keys, memory_proj)
    value_part, key_part = together(dot_nt(grad_memory_values, memory_value), key_part)
    grad_memory, gate_rows = together((key_part + value_part).astype(BF16), gate_rows)
    arrived_gates = exchange_line(gate_rows)
    grad_memory, grad_memory_keys, grad_memory_values, arrived_gates = together(
        lax.ppermute(grad_memory, "half", backward),
        grad_memory_keys,
        grad_memory_values,
        arrived_gates,
    )
    back_keys = lax.ppermute(grad_memory_keys, "half", backward)
    back_values = lax.ppermute(grad_memory_values, "half", backward)
    grad_memory = grad_memory.astype(F32)
    pulled_rows, gain_cross = rms_back(
        dot_nt(grad_cross_query, proj_weight), first_half, gain_rows[1]
    )
    grad_first_dec = grad_second_half + pulled_rows

    pulled_rows, gain_memory = rms_back(grad_memory, encoded, gain_rows[2])
    grad_encoded = cot_f + pulled_rows
    grad_gate_first = jnp.sum(grad_encoded * enc_first, axis=1, keepdims=True)
    grad_gate_second = jnp.sum(grad_encoded * enc_second, axis=1, keepdims=True)
    sent = spread(
        (enc_gates[0] * grad_encoded).astype(BF16), (enc_gates[1] * grad_encoded).astype(BF16)
    )
    arrived_three = [
        exchange(jnp.where(decoder, produced, part), experts)
        for produced, part in zip(produced_two, sent)
    ]
    flags = jnp.stack([decoder.astype(jnp.int32), group])
    scales = jnp.where(decoder, arrived_gates, 1.0)[:, None]
    most = max(part.shape[0] for part in arrived_one)
    kept = None
    returned_three = []
    for k, scale in enumerate((scales[:edge], scales[edge:])):
        grad_arrived, kept = expert_back(
            flags,
            arrived_one[k],
            arrived_two[k],
            arrived_three[k],
            scale,
            expert_first,
            expert_second,
            kept,
            k,
            most,
        )
        if k == 0:
            grad_arrived, back_keys, back_values = together(grad_arrived, back_keys, back_values)
            grad_value = dot_tn(
                jnp.where(decoder, cross_context, memory),
                jnp.where(decoder, rounded_grad, back_values),
            )
            grad_proj = dot_tn(
                jnp.where(decoder, rounded_half, memory),
                jnp.where(decoder, grad_cross_query, back_keys),
            )
            early = group_swap(jnp.concatenate([grad_proj, grad_value], axis=1).astype(BF16), group)
            normed_sharded = jnp.swapaxes(
                normed_in.reshape(row_count, 2, lax.axis_size("expert"), -1), 1, 2
            ).reshape(row_count, D)
        else:
            grad_arrived, early, normed_sharded, kept, returned_three[0], arrived_three = together(
                grad_arrived, early, normed_sharded, kept, returned_three[0], arrived_three
            )
        returned_three.append(exchange(grad_arrived, experts))

    decoded = (
        second_half
        + dec_gates[0] * collect(arrived_three, code_first)
        + dec_gates[1] * collect(arrived_three, code_second)
    )
    result = jnp.where(decoder, decoded, encoded)

    expert_rows, expert_grad_rows, actives, keep_halves, send_halves = [
        part.reshape(2 * most, -1) for part in kept
    ]
    first_group = group == 0
    half_ff = FF // 2
    send_in = dot_tn(expert_rows, send_halves).astype(BF16)
    in_cuts = (0, 208, 496, 656, 816, D)
    out_cut = 320
    sends = [(send_in[first:last],) for first, last in zip(in_cuts[:-1], in_cuts[1:])]

    def swapped(parts):
        return [lax.ppermute(part, "group", SWAP) for part in parts]

    gots = [swapped(sends[0])]
    returned_three[1], sends, gots, early, result = together(
        returned_three[1], sends, gots, early, result.astype(BF16)
    )
    early = expert_scatter(early)

    enc_logits, enc_normed = router_back(enc_gates, grad_gate_first, grad_gate_second)
    enc_normed = enc_normed + collect(returned_three, code_first) + collect(returned_three, code_second)
    pulled_rows, gain_enc_moe = rms_back(enc_normed, first_half, gain_rows[1])
    grad_first = jnp.where(decoder, grad_first_dec, grad_encoded + pulled_rows)

    rounded_grad = grad_first.astype(BF16)
    grad_context = dot_nt(rounded_grad, out_weight).astype(BF16)
    middle = expert_scatter(shard_rows(dot_tn(context, rounded_grad)))
    grad_context, early, sends[1] = together(grad_context, early, sends[1])
    gots.append(swapped(sends[1]))
    early = expert_gather(early)
    grad_query, grad_keys, grad_values, grad_lines = attend_back(
        query, keys, values, grad_context, lse, places, lines
    )
    (grad_query, grad_keys, grad_values), gots, sends[2], middle, early, kept = together(
        (grad_query, grad_keys, grad_values),
        gots,
        sends[2],
        middle,
        early,
        (actives, expert_grad_rows),
    )
    late_first = dot_tn(normed_sharded, jnp.concatenate([grad_keys, grad_values], axis=1))
    late_first, (grad_query, grad_keys, grad_values), sends[2], kept = together(
        late_first.astype(BF16), (grad_query, grad_keys, grad_values), sends[2], kept
    )
    late_first = expert_scatter(late_first)
    actives, expert_grad_rows = kept
    send_out = dot_tn(
        jnp.where(first_group, actives[:, half_ff:], actives[:, :half_ff]), expert_grad_rows
    ).astype(BF16)
    gots.append(swapped(sends[2]))

    grad_table = jnp.dot(grad_lines.reshape(H, LINE), hits, precision=HIGHEST)
    grad_router = lax.dot_general(
        jnp.where(decoder, normed_second, normed_half),
        jnp.where(decoder, dec_logits, enc_logits),
        (((0,), (0,)), ((), ())),
        precision=HIGHEST,
    )
    grad_normed = dot_nt(jnp.concatenate([grad_query, grad_keys, grad_values], axis=1), qkv_weight)
    grad_normed, gots, sends[3] = together(grad_normed, gots, sends[3])
    gots.append(swapped(sends[3]))
    pulled_rows, gain_self = rms_back(grad_normed, start_rows, gain_rows[0])
    grad_starts = grad_first + pulled_rows
    gain_grads = jnp.stack(
        [
            gain_self,
            jnp.where(decoder, gain_cross, gain_enc_moe),
            jnp.where(decoder, gain_dec_moe, gain_memory),
        ]
    )
    table_rows = jnp.pad(grad_table.reshape(2, -1), ((0, 0), (0, (D - H * NBKT) // 2)))
    small = jnp.concatenate([grad_router, gain_grads.T, table_rows.reshape(D, 1)], axis=1)
    small = jnp.pad(small, ((0, 0), (0, 128 - small.shape[1])))
    late_second = jnp.concatenate(
        [dot_tn(normed_sharded, grad_query).astype(BF16), shard_rows(small)], axis=1
    )
    keep_in = dot_tn(expert_rows, keep_halves)
    late_second, late_first, gots, sends[4], keep_in = together(
        late_second, late_first, gots, sends[4] + (send_out[:out_cut],), keep_in
    )
    gots.append(swapped(sends[4]))
    late_second = expert_scatter(late_second)
    keep_out = dot_tn(
        jnp.where(first_group, actives[:, :half_ff], actives[:, half_ff:]), expert_grad_rows
    )
    late_first, late_second, keep_out, gots, send_out = together(
        late_first, late_second, keep_out, gots, send_out
    )
    late = group_swap(jnp.concatenate([late_first, late_second, middle], axis=1), group)
    late, send_out = together(late, send_out)
    late = expert_gather(late)
    gots.append(swapped([send_out[out_cut:]]))
    grad_expert_in = keep_in + jnp.concatenate([part[0] for part in gots[:5]]).astype(F32)
    grad_expert_out = keep_out + jnp.concatenate([gots[4][1], gots[5][0]]).astype(F32)
    grad_qkv = jnp.concatenate([late[:, 2 * D : 3 * D], late[:, : 2 * D]], axis=1).astype(F32)
    small = late[:, 3 * D : 3 * D + 128].astype(F32)
    small_table = small[: H * NBKT // 2, experts + 3].reshape(H // 2, NBKT)
    return (
        result[None],
        grad_starts.astype(BF16)[None],
        small[:, experts : experts + 3].T[None],
        small_table[None],
        grad_qkv[None],
        late[:, 3 * D + 128 :].astype(F32)[None],
        early[:, :D].astype(F32)[None],
        early[:, D:].astype(F32)[None],
        small[:, :experts][None],
        grad_expert_in[None, None],
        grad_expert_out[None, None],
    )


def solution(mesh):
    in_specs = (
        P("half", ("expert", "group"), None),
        P("half", ("expert", "group"), None),
        P(("expert", "group")),
        P("half", ("expert", "group"), None),
        P("half", None, None),
        P("half", None, None),
        P("half", None, None),
        P("half", None, None),
        P("half", None, None),
        P("half", None, None),
        P("half", None, None),
        P("half", "expert", None, None),
        P("half", "expert", None, None),
    )
    out_specs = (
        P("half", ("expert", "group"), None),
        P("half", ("expert", "group"), None),
        P("half", None, "group"),
        P("half", "group", None),
        P("half", "group", None),
        P("half", "group", None),
        P("half", "group", None),
        P("half", "group", None),
        P("half", "group", None),
        P("half", "expert", None, "group"),
        P("half", "expert", "group", None),
    )
    return jax.shard_map(
        per_device, mesh=mesh, in_specs=in_specs, out_specs=out_specs, check_vma=False
    )
```

```python
from functools import partial

import jax
import jax.numpy as jnp
import numpy as np
from jax import lax
from jax.experimental import pallas as pl
from jax.experimental.layout import Layout, with_layout_constraint
from jax.experimental.pallas import tpu as pltpu
from jax.sharding import PartitionSpec as P

D = 1024
H = 16
HD = 64
FF = 2816
NBKT = 32
DEC_SLOT = 128
DEC_LEN = 114
ENC_MOST = 512
ENC_MIN = 32
ITEMS = 5

EPSILON = 1e-06
MASKED = -1e30
HIGHEST = lax.Precision.HIGHEST
BLOCK = 128
PAIRS = H // 2
DIAGONAL = ENC_MOST // BLOCK - 1
LINE = 2 * ENC_MOST
FF_TILE = 256
F32 = jnp.float32
BF16 = jnp.bfloat16
GELU_SCALE = float(np.sqrt(2.0 / np.pi))
GELU_CUBE = 0.044715
SWAP = ((0, 1), (1, 0))
VMEM_LIMIT = 60 * 1024 * 1024


def bucket_limits(exact_range, growth, divisions):
    limits = []
    for number in range(1, divisions):
        candidate = exact_range
        while candidate**divisions < exact_range**divisions * growth**number:
            candidate = candidate + 1
        limits.append(candidate)
    return limits


def rel_buckets(offset, causal):
    if causal:
        behind = np.maximum(-offset, 0)
        return np.minimum(behind, 16) + sum(
            (behind >= threshold).astype(np.int32) for threshold in bucket_limits(16, 8, 16)
        )
    distance = np.abs(offset)
    return (
        (offset > 0).astype(np.int32) * 16
        + np.minimum(distance, 8)
        + sum((distance >= threshold).astype(np.int32) for threshold in bucket_limits(8, 16, 8))
    )


def bucket_hits(offset, causal):
    return (rel_buckets(offset, causal)[:, None] == np.arange(NBKT)[None, :]).astype(np.float32)


def inverse_rms(values):
    return lax.rsqrt(jnp.mean(values * values, axis=-1, keepdims=True) + EPSILON)


def rms_norm(values, gain_vec):
    return values * inverse_rms(values) * gain_vec


def rms_back(grad_normed, values, gain_vec):
    scale = inverse_rms(values)
    unit = values * scale
    pulled = grad_normed * gain_vec
    grad_values = scale * (pulled - unit * jnp.mean(pulled * unit, axis=-1, keepdims=True))
    return grad_values, jnp.sum(grad_normed * unit, axis=0)


def dot(a, b):
    return jnp.dot(a, b, preferred_element_type=F32)


def dot_nt(a, b):
    return lax.dot_general(a, b, (((1,), (1,)), ((), ())), preferred_element_type=F32)


def dot_tn(a, b):
    return lax.dot_general(a, b, (((0,), (0,)), ((), ())), preferred_element_type=F32)


def skew(line, rows):
    width = line.shape[1]
    tile = jnp.broadcast_to(line, (8, width))
    row = lax.broadcasted_iota(jnp.int32, (8, width), 0)
    for step in (1, 2, 4):
        tile = jnp.where((row & step) != 0, pltpu.roll(tile, step, 1), tile)
    return jnp.concatenate(
        [pltpu.roll(tile, width - rows + first, 1) for first in range(0, rows, 8)], axis=0
    )


def unskew(total):
    rows, width = total.shape
    summed = None
    for first in range(0, rows, 8):
        moved = pltpu.roll(total[first : first + 8], rows - first, 1)
        summed = moved if summed is None else summed + moved
    row = lax.broadcasted_iota(jnp.int32, (8, width), 0)
    for step in (1, 2, 4):
        summed = jnp.where((row & step) != 0, pltpu.roll(summed, width - step, 1), summed)
    return jnp.sum(summed, axis=0, keepdims=True)


def own_lanes(head):
    return (lax.broadcasted_iota(jnp.int32, (1, 2 * HD), 1) // HD) == head


def head_lanes(head, value):
    return jnp.where(own_lanes(head), value, 0.0).astype(BF16)


def tile_places(keys, queries):
    key = lax.broadcasted_iota(jnp.int32, (keys, queries), 0)
    query = lax.broadcasted_iota(jnp.int32, (keys, queries), 1)
    return key, query


def causal_tile():
    key, query = tile_places(BLOCK, BLOCK)
    return (key <= query) & (key < DEC_LEN)


def short_tile():
    key, query = tile_places(BLOCK, BLOCK)
    return (key // ENC_MIN) == (query // ENC_MIN)


def bias_tiles(rows, queries, shares):
    return [
        (
            slice(block * BLOCK, (block + 1) * BLOCK),
            slice((DIAGONAL - block % (rows // BLOCK // shares)) * BLOCK, None),
            queries,
        )
        for block in range(rows // BLOCK)
    ]


def add_bias(scores, bias_ref, head, shares):
    rows, queries = scores.shape
    return joined(
        [
            scores[here] + bias_ref[head, :, lanes.start : lanes.start + queries]
            for here, lanes, queries in bias_tiles(rows, queries, shares)
        ]
    )


def add_bias_grad(dbias_ref, head, grad_scores, shares):
    rows, queries = grad_scores.shape
    sums = {}
    for here, lanes, queries in bias_tiles(rows, queries, shares):
        part = grad_scores[here]
        sums[lanes.start] = sums[lanes.start] + part if lanes.start in sums else part
    for first, part in sums.items():
        dbias_ref[head, :, first : first + queries] += part


def masked(scores, mask):
    return scores if mask is None else jnp.where(mask, scores, MASKED)


def key_parts(rows, shares):
    step = rows.shape[0] // shares
    return [rows[first : first + step] for first in range(0, rows.shape[0], step)]


def spread_max(values, shares):
    return [jnp.max(part, axis=0, keepdims=True) for part in key_parts(values, shares)]


def joined(parts):
    return parts[0] if len(parts) == 1 else jnp.concatenate(parts, axis=0)


def per_share(lines, rows):
    step = rows // len(lines)
    if len(lines) == 1:
        return lines[0]
    return jnp.concatenate(
        [jnp.broadcast_to(line, (step, line.shape[1])) for line in lines], axis=0
    )


def attend_groups(groups, bias_ref):
    units = [(group, head) for group in groups for head in range(2)]
    scores = []
    for (queries, keys, values, mask), head in units:
        scale = head_lanes(head, HD**-0.5)
        part = joined([dot_nt(key, query * scale) for query, key in zip(queries, keys)])
        scores.append(part)
    contexts = []
    log_sums = []
    for ((queries, keys, values, mask), head), part in zip(units, scores):
        shares = len(queries)
        if bias_ref is not None:
            part = add_bias(part, bias_ref, head, shares)
        part = masked(part, mask)
        highest = spread_max(part, shares)
        exponent = jnp.exp(part - per_share(highest, part.shape[0]))
        totals = [jnp.sum(rows, axis=0, keepdims=True) for rows in key_parts(exponent, shares)]
        log_sums.append([top + jnp.log(total) for top, total in zip(highest, totals)])
        rounded = key_parts(exponent.astype(BF16), shares)
        contexts.append(
            [
                dot_tn(rows, jnp.where(own_lanes(head), value, jnp.ones_like(value)))
                for rows, value in zip(rounded, values)
            ]
        )
    results = []
    for number in range(len(groups)):
        rows = []
        lines = []
        for share in range(len(groups[number][0])):
            first, second = contexts[2 * number][share], contexts[2 * number + 1][share]
            sums = jnp.where(own_lanes(0), second, first)
            context = jnp.where(own_lanes(0), first, second) / pltpu.roll(sums, HD, 1)
            rows.append(context.astype(BF16))
            lines.append(
                jnp.concatenate(
                    [log_sums[2 * number][share], log_sums[2 * number + 1][share]], axis=0
                )
            )
        results.append((rows, lines))
    return results


def attend_groups_back(groups, bias_ref, dbias_ref):
    units = [(group, head) for group in groups for head in range(2)]
    scores = []
    pulls = []
    for (queries, keys, values, mask, grads, lines), head in units:
        scale = head_lanes(head, HD**-0.5)
        own = head_lanes(head, 1.0)
        scores.append(joined([dot_nt(key, query * scale) for query, key in zip(queries, keys)]))
        pulls.append(joined([dot_nt(value, grad * own) for value, grad in zip(values, grads)]))
    totals = []
    for ((queries, keys, values, mask, grads, lines), head), part, pull in zip(units, scores, pulls):
        shares = len(queries)
        scale = head_lanes(head, HD**-0.5)
        own = head_lanes(head, 1.0)
        if bias_ref is not None:
            part = add_bias(part, bias_ref, head, shares)
        part = masked(part, mask)
        weights = jnp.exp(part - per_share([line[head : head + 1] for line in lines], part.shape[0]))
        product = weights * pull
        inner = [jnp.sum(rows, axis=0, keepdims=True) for rows in key_parts(product, shares)]
        grad_scores = product - weights * per_share(inner, part.shape[0])
        if dbias_ref is not None:
            add_bias_grad(dbias_ref, head, grad_scores, shares)
        rounded = key_parts(grad_scores.astype(BF16), shares)
        weights = key_parts(weights.astype(BF16), shares)
        totals.append(
            [
                [dot_tn(rows, key * scale) for rows, key in zip(rounded, keys)],
                [dot(rows, query * scale) for rows, query in zip(rounded, queries)],
                [dot(rows, grad * own) for rows, grad in zip(weights, grads)],
            ]
        )
    results = []
    for number in range(len(groups)):
        results.append(
            [
                [(one + two).astype(BF16) for one, two in zip(first, second)]
                for first, second in zip(totals[2 * number], totals[2 * number + 1])
            ]
        )
    return results


def short_places(place, item):
    later = (item >= place).astype(jnp.int32)
    return pl.multiple_of(item * ENC_MIN + later * ENC_MOST, ENC_MIN), item + later


def gather_short(ref, place):
    return jnp.concatenate(
        [ref[pl.ds(short_places(place, item)[0], ENC_MIN), :] for item in range(ITEMS - 1)], axis=0
    )


def scatter_short(ref, place, rows):
    for item in range(ITEMS - 1):
        ref[pl.ds(short_places(place, item)[0], ENC_MIN), :] = rows[
            item * ENC_MIN : (item + 1) * ENC_MIN
        ]


def block_rows(block):
    return slice(block * BLOCK, (block + 1) * BLOCK)


def self_attend_kernel(place_ref, q_ref, k_ref, v_ref, line_ref, out_ref, lse_ref, bias_ref):
    for head in range(2):
        bias_ref[head] = skew(line_ref[0, head : head + 1, :], BLOCK)
    place = place_ref[0]
    decoder = place_ref[1] == 1

    @pl.when(decoder)
    def _():
        blocks = [block_rows(block) for block in range(ITEMS)]
        shares = tuple([ref[here, :] for here in blocks] for ref in (q_ref, k_ref, v_ref))
        ((rows, lines),) = attend_groups([shares + (joined([causal_tile()] * ITEMS),)], bias_ref)
        for here, part, line in zip(blocks, rows, lines):
            out_ref[here, :] = part
            lse_ref[0, :, here] = line

    @pl.when(jnp.logical_not(decoder))
    def _():
        here = pl.ds(pl.multiple_of(place * ENC_MIN, ENC_MIN), ENC_MOST)
        groups = [
            ([q_ref[here, :]], [k_ref[here, :]], [v_ref[here, :]], None),
            tuple([gather_short(ref, place)] for ref in (q_ref, k_ref, v_ref)) + (short_tile(),),
        ]
        ((rows, lines),) = attend_groups(groups[:1], bias_ref)
        out_ref[here, :] = rows[0]
        lse_ref[0, :, :ENC_MOST] = lines[0]
        ((short_rows, short_lines),) = attend_groups(groups[1:], bias_ref)
        scatter_short(out_ref, place, short_rows[0])
        lse_ref[0, :, ENC_MOST:] = short_lines[0]


def self_attend_back_kernel(
    place_ref, q_ref, k_ref, v_ref, dc_ref, lse_ref, line_ref,
    dq_ref, dk_ref, dv_ref, dline_ref, bias_ref, dbias_ref,
):
    for head in range(2):
        bias_ref[head] = skew(line_ref[0, head : head + 1, :], BLOCK)
    dbias_ref[...] = jnp.zeros(dbias_ref.shape, F32)
    place = place_ref[0]
    decoder = place_ref[1] == 1
    outs = (dq_ref, dk_ref, dv_ref)

    @pl.when(decoder)
    def _():
        blocks = [block_rows(block) for block in range(ITEMS)]
        shares = tuple([ref[here, :] for here in blocks] for ref in (q_ref, k_ref, v_ref))
        shares += (
            joined([causal_tile()] * ITEMS),
            [dc_ref[here, :] for here in blocks],
            [lse_ref[0, :, here] for here in blocks],
        )
        (grads,) = attend_groups_back([shares], bias_ref, dbias_ref)
        for ref, rows in zip(outs, grads):
            for here, part in zip(blocks, rows):
                ref[here, :] = part

    @pl.when(jnp.logical_not(decoder))
    def _():
        here = pl.ds(pl.multiple_of(place * ENC_MIN, ENC_MIN), ENC_MOST)
        groups = [
            (
                [q_ref[here, :]],
                [k_ref[here, :]],
                [v_ref[here, :]],
                None,
                [dc_ref[here, :]],
                [lse_ref[0, :, :ENC_MOST]],
            ),
            (
                [gather_short(q_ref, place)],
                [gather_short(k_ref, place)],
                [gather_short(v_ref, place)],
                short_tile(),
                [gather_short(dc_ref, place)],
                [lse_ref[0, :, ENC_MOST:]],
            ),
        ]
        grads, short_grads = attend_groups_back(groups, bias_ref, dbias_ref)
        for ref, rows, short_rows in zip(outs, grads, short_grads):
            ref[here, :] = rows[0]
            scatter_short(ref, place, short_rows[0])

    for head in range(2):
        dline_ref[0, head : head + 1, :] = unskew(dbias_ref[head])


def cross_places(place):
    long_pair = (
        pl.ds(pl.multiple_of(place * BLOCK, BLOCK), BLOCK),
        pl.ds(pl.multiple_of(place * ENC_MIN, ENC_MIN), ENC_MOST),
    )
    pairs = []
    for item in range(ITEMS - 1):
        start, number = short_places(place, item)
        pairs.append(
            (pl.ds(pl.multiple_of(number * BLOCK, BLOCK), BLOCK), pl.ds(start, ENC_MIN))
        )
    return [[long_pair], pairs]


def cross_attend_kernel(place_ref, q_ref, k_ref, v_ref, out_ref, lse_ref):
    places = cross_places(place_ref[0])
    groups = [
        (
            [q_ref[here, :] for here, there in pairs],
            [k_ref[there, :] for here, there in pairs],
            [v_ref[there, :] for here, there in pairs],
            None,
        )
        for pairs in places
    ]
    number = 0
    for pairs, (rows, lines) in zip(places, attend_groups(groups, None)):
        for (here, there), part, line in zip(pairs, rows, lines):
            out_ref[here, :] = part
            lse_ref[0, :, block_rows(number)] = line
            number += 1


def cross_attend_back_kernel(
    place_ref, q_ref, k_ref, v_ref, dc_ref, lse_ref, dq_ref, dk_ref, dv_ref
):
    places = cross_places(place_ref[0])
    lines = [lse_ref[0, :, block_rows(number)] for number in range(ITEMS)]
    groups = [
        (
            [q_ref[here, :] for here, there in pairs],
            [k_ref[there, :] for here, there in pairs],
            [v_ref[there, :] for here, there in pairs],
            None,
            [dc_ref[here, :] for here, there in pairs],
            part,
        )
        for pairs, part in zip(places, (lines[:1], lines[1:]))
    ]
    for pairs, grads in zip(places, attend_groups_back(groups, None, None)):
        for number, (here, there) in enumerate(pairs):
            dq_ref[here, :] = grads[0][number]
            dk_ref[there, :] = grads[1][number]
            dv_ref[there, :] = grads[2][number]


def pair_spec(rows, first):
    return pl.BlockSpec((rows, 2 * HD), lambda pair, places: (0, first + pair))


def flat_spec(first, *shape):
    return pl.BlockSpec((1,) + shape, lambda pair, places: (first + pair, 0, 0))


def pair_call(kernel, places, operands, specs, out_specs, out_shape, scratch, work, pairs=PAIRS):
    rows = ITEMS * BLOCK
    share = rows * rows * D * pairs // PAIRS
    return pl.pallas_call(
        kernel,
        grid_spec=pltpu.PrefetchScalarGridSpec(
            num_scalar_prefetch=1,
            grid=(pairs,),
            in_specs=specs,
            out_specs=out_specs,
            scratch_shapes=scratch,
        ),
        out_shape=out_shape,
        compiler_params=pltpu.CompilerParams(vmem_limit_bytes=VMEM_LIMIT),
        cost_estimate=pl.CostEstimate(
            flops=work * share, bytes_accessed=16 * rows * D, transcendentals=share // HD
        ),
        name=kernel.__name__,
    )(places, *operands)


def attend(query, keys, values, places, lines):
    rows = query[0].shape[0]
    operands = [part[0] for part in (query, keys, values)]
    specs = [pair_spec(rows, part[1]) for part in (query, keys, values)]
    scratch = []
    if lines is not None:
        operands.append(lines)
        specs.append(flat_spec(0, 2, LINE))
        scratch.append(pltpu.VMEM((2, BLOCK, LINE), F32))
    return pair_call(
        cross_attend_kernel if lines is None else self_attend_kernel,
        places,
        operands,
        specs,
        [pair_spec(rows, 0), flat_spec(0, 2, rows)],
        [
            jax.ShapeDtypeStruct((rows, D), BF16),
            jax.ShapeDtypeStruct((PAIRS, 2, rows), F32),
        ],
        scratch,
        4,
    )


def attend_back(query, keys, values, grad_context, lse, places, lines, first=0, pairs=PAIRS):
    rows = query[0].shape[0]
    operands = [part[0] for part in (query, keys, values)] + [grad_context, lse]
    specs = [pair_spec(rows, part[1] + first) for part in (query, keys, values)]
    specs += [pair_spec(rows, first), flat_spec(first, 2, rows)]
    out_specs = [pair_spec(rows, 0)] * 3
    out_shape = [jax.ShapeDtypeStruct((rows, pairs * 2 * HD), BF16)] * 3
    scratch = []
    if lines is not None:
        operands.append(lines)
        specs.append(flat_spec(first, 2, LINE))
        out_specs.append(flat_spec(0, 2, LINE))
        out_shape.append(jax.ShapeDtypeStruct((pairs, 2, LINE), F32))
        scratch += [pltpu.VMEM((2, BLOCK, LINE), F32)] * 2
    return pair_call(
        cross_attend_back_kernel if lines is None else self_attend_back_kernel,
        places,
        operands,
        specs,
        out_specs,
        out_shape,
        scratch,
        10,
        pairs,
    )


def exchange(rows, experts):
    parts = rows.reshape(experts, -1, rows.shape[-1])
    return lax.all_to_all(parts, "expert", split_axis=0, concat_axis=0, tiled=True).reshape(
        rows.shape
    )


def gelu_parts(value):
    square = value * value
    bend = jnp.tanh(value * (GELU_SCALE + GELU_SCALE * GELU_CUBE * square))
    half = 0.5 + 0.5 * bend
    slope = half + value * (half * (1.0 - bend)) * (
        GELU_SCALE + 3.0 * GELU_SCALE * GELU_CUBE * square
    )
    return value * half, slope


def row_blocks(rows):
    step = rows // 2
    return [slice(first, first + step) for first in range(0, rows, step)]


def expert_forward_kernel(x_ref, gate_ref, up_ref, down_ref, out_ref, total_ref):
    @pl.when(pl.program_id(0) == 0)
    def _():
        total_ref[...] = jnp.zeros(total_ref.shape, F32)

    for here in row_blocks(x_ref.shape[0]):
        rows = x_ref[here, :]
        value, _ = gelu_parts(dot(rows, gate_ref[...]))
        active = (value * dot(rows, up_ref[...])).astype(BF16)
        total_ref[here, :] += dot(active, down_ref[...])

    @pl.when(pl.program_id(0) == pl.num_programs(0) - 1)
    def _():
        out_ref[...] = total_ref[...].astype(BF16)


def hidden_grads(rows, grad_rows, gate_ref, up_ref, down_ref):
    gate = dot(rows, gate_ref[...])
    up = dot(rows, up_ref[...])
    grad_active = dot_nt(grad_rows, down_ref[...])
    value, slope = gelu_parts(gate)
    grad_gate = (grad_active * (up * slope)).astype(BF16)
    grad_up = (grad_active * value).astype(BF16)
    return value * up, grad_active, grad_gate, grad_up


def expert_both_kernel(
    x_ref, g_ref, gate_ref, up_ref, down_ref, dx_ref, active_ref, line_ref, dx_total, line_total
):
    @pl.when(pl.program_id(0) == 0)
    def _():
        dx_total[...] = jnp.zeros(dx_total.shape, F32)
        line_total[...] = jnp.zeros(line_total.shape, F32)

    for here in row_blocks(x_ref.shape[0]):
        active, grad_active, grad_gate, grad_up = hidden_grads(
            x_ref[here, :], g_ref[here, :], gate_ref, up_ref, down_ref
        )
        dx_total[here, :] += dot_nt(grad_gate, gate_ref[...]) + dot_nt(grad_up, up_ref[...])
        active_ref[here, :] = active.astype(BF16)
        product = active * grad_active
        line_total[here, :] += sum(
            product[:, first : first + 128] for first in range(0, product.shape[1], 128)
        )

    @pl.when(pl.program_id(0) == pl.num_programs(0) - 1)
    def _():
        dx_ref[...] = dx_total[...].astype(BF16)
        line_ref[...] = jnp.sum(line_total[...], axis=1, keepdims=True)


def expert_back_kernel(flags_ref, *refs, count):
    one_ref, two_ref, three_ref, scale_ref, gate_ref, up_ref, down_ref = refs[:7]
    dx_ref, x_ref, g_ref, active_ref, keep_ref, send_ref, dx_total, sems = refs[-8:]
    decoder = flags_ref[0] == 1
    first_group = flags_ref[1] == 0
    most = x_ref.shape[1]
    spare = slice(count, most)

    def load(rows, grads):
        copies = [
            pltpu.make_async_copy(rows, x_ref.at[0, pl.ds(0, count)], sems.at[0]),
            pltpu.make_async_copy(grads, g_ref.at[0, pl.ds(0, count)], sems.at[1]),
        ]
        for copy in copies:
            copy.start()
        for copy in copies:
            copy.wait()

    @pl.when(pl.program_id(0) == 0)
    def _():
        dx_total[...] = jnp.zeros(dx_total.shape, F32)

        @pl.when(decoder)
        def _():
            load(two_ref, one_ref)

        @pl.when(jnp.logical_not(decoder))
        def _():
            load(one_ref, three_ref)

        grads = g_ref[0, :count, :].astype(F32) * scale_ref[...]
        g_ref[0, :count, :] = grads.astype(BF16)
        if count < most:
            x_ref[0, spare, :] = jnp.zeros((most - count, D), BF16)
            g_ref[0, spare, :] = jnp.zeros((most - count, D), BF16)

    for here in row_blocks(count):
        active, _, grad_gate, grad_up = hidden_grads(
            x_ref[0, here, :], g_ref[0, here, :], gate_ref, up_ref, down_ref
        )
        dx_total[here, :] += dot_nt(grad_gate, gate_ref[...]) + dot_nt(grad_up, up_ref[...])
        active_ref[0, here, :] = active.astype(BF16)
        keep_ref[0, here, :] = jnp.where(first_group, grad_gate, grad_up)
        send_ref[0, here, :] = jnp.where(first_group, grad_up, grad_gate)
    if count < most:
        for ref in (active_ref, keep_ref, send_ref):
            ref[0, spare, :] = jnp.zeros((most - count, FF_TILE), BF16)

    @pl.when(pl.program_id(0) == pl.num_programs(0) - 1)
    def _():
        dx_ref[...] = dx_total[...].astype(BF16)


def expert_specs(rows):
    tiles = FF // FF_TILE
    whole = pl.BlockSpec((rows, D), lambda tile, *_: (0, 0))
    weight_specs = [
        pl.BlockSpec((D, FF_TILE), lambda tile, *_: (0, tile)),
        pl.BlockSpec((D, FF_TILE), lambda tile, *_: (0, tiles + tile)),
        pl.BlockSpec((FF_TILE, D), lambda tile, *_: (tile, 0)),
    ]
    return whole, weight_specs, tiles


def expert_cost(rows, products):
    return pl.CostEstimate(
        flops=2 * products * rows * D * FF, bytes_accessed=6 * D * FF, transcendentals=rows * FF
    )


def expert_forward(arrived, expert_first, expert_second):
    rows = arrived.shape[0]
    whole, weight_specs, tiles = expert_specs(rows)
    return pl.pallas_call(
        expert_forward_kernel,
        grid=(tiles,),
        in_specs=[whole] + weight_specs,
        out_specs=whole,
        out_shape=jax.ShapeDtypeStruct((rows, D), BF16),
        scratch_shapes=[pltpu.VMEM((rows, D), F32)],
        compiler_params=pltpu.CompilerParams(vmem_limit_bytes=VMEM_LIMIT),
        cost_estimate=expert_cost(rows, 3),
        name="expert_forward",
    )(arrived, expert_first, expert_first, expert_second)


def expert_both(arrived, grad_rows, expert_first, expert_second):
    rows = arrived.shape[0]
    whole, weight_specs, tiles = expert_specs(rows)
    row_shape = jax.ShapeDtypeStruct((rows, D), BF16)
    total = pltpu.VMEM((rows, D), F32)
    return pl.pallas_call(
        expert_both_kernel,
        grid=(tiles,),
        in_specs=[whole, whole] + weight_specs,
        out_specs=[
            whole,
            pl.BlockSpec((rows, FF_TILE), lambda tile: (0, tile)),
            pl.BlockSpec((rows, 1), lambda tile: (0, 0)),
        ],
        out_shape=[
            row_shape,
            jax.ShapeDtypeStruct((rows, FF), BF16),
            jax.ShapeDtypeStruct((rows, 1), F32),
        ],
        scratch_shapes=[total, pltpu.VMEM((rows, 128), F32)],
        compiler_params=pltpu.CompilerParams(vmem_limit_bytes=VMEM_LIMIT),
        cost_estimate=expert_cost(rows, 5),
        name="expert_both",
    )(arrived, grad_rows, expert_first, expert_first, expert_second)


def expert_back(flags, one, two, three, scale, expert_first, expert_second, kept, number, most):
    rows = one.shape[0]
    whole, weight_specs, tiles = expert_specs(rows)
    part = pl.BlockSpec((1, most, D), lambda tile, *_: (number, 0, 0))
    strip = pl.BlockSpec((1, most, FF_TILE), lambda tile, *_: (number, 0, tile))
    kept_shapes = [jax.ShapeDtypeStruct((2, most, D), BF16)] * 2
    kept_shapes += [jax.ShapeDtypeStruct((2, most, FF), BF16)] * 3
    anywhere = pl.BlockSpec(memory_space=pl.ANY)
    in_specs = [anywhere] * 3 + [pl.BlockSpec((rows, 1), lambda tile, *_: (0, 0))] + weight_specs
    operands = [one, two, three, scale, expert_first, expert_first, expert_second]
    aliases = {}
    if kept is not None:
        aliases = {1 + len(operands) + place: 1 + place for place in range(len(kept))}
        in_specs += [anywhere] * len(kept)
        operands += kept
    dx, *kept = pl.pallas_call(
        partial(expert_back_kernel, count=rows),
        grid_spec=pltpu.PrefetchScalarGridSpec(
            num_scalar_prefetch=1,
            grid=(tiles,),
            in_specs=in_specs,
            out_specs=[whole, part, part, strip, strip, strip],
            scratch_shapes=[pltpu.VMEM((rows, D), F32), pltpu.SemaphoreType.DMA((2,))],
        ),
        out_shape=[jax.ShapeDtypeStruct((rows, D), BF16)] + kept_shapes,
        input_output_aliases=aliases,
        compiler_params=pltpu.CompilerParams(vmem_limit_bytes=VMEM_LIMIT),
        cost_estimate=expert_cost(rows, 5),
        name="expert_back",
    )(flags, *operands)
    return dx, list(kept)


def gate_pair(normed, router_weight, picked_first, picked_second):
    logits = jnp.dot(normed, router_weight, precision=HIGHEST)
    first = jnp.sum(logits * picked_first, axis=1, keepdims=True)
    second = jnp.sum(logits * picked_second, axis=1, keepdims=True)
    return jax.nn.sigmoid(first - second), jax.nn.sigmoid(second - first)


def group_parts(rows, group):
    half = rows.shape[0] // 2
    sent = lax.dynamic_slice_in_dim(rows, (1 - group) * half, half, 0)
    kept = lax.dynamic_slice_in_dim(rows, group * half, half, 0)
    return kept, lax.ppermute(sent, "group", SWAP)


def group_swap(rows, group):
    kept, got = group_parts(rows, group)
    return kept + got


def shard_rows(grad):
    rows, columns = grad.shape
    parts = grad.astype(BF16).reshape(2, lax.axis_size("expert"), -1, columns)
    return jnp.swapaxes(parts, 0, 1).reshape(rows, columns)


def expert_scatter(rows):
    return lax.psum_scatter(rows, "expert", scatter_dimension=0, tiled=True)


def expert_gather(rows):
    return lax.all_gather(rows, "expert", axis=0, tiled=True)


def together(*values):
    return lax.optimization_barrier(values)


def per_device(
    inputs,
    cotangent,
    enc_lengths,
    routes,
    norm_gains,
    rel_bias,
    self_qkv,
    self_out,
    cross_proj,
    cross_value,
    router,
    expert_in,
    expert_out,
):
    decoder = lax.axis_index("half") == 1
    group = lax.axis_index("group")
    start_rows = inputs[0].astype(F32)
    row_count = start_rows.shape[0]
    gain_rows = norm_gains[0]
    bias_table = rel_bias[0]
    qkv_weight = self_qkv[0]
    out_weight = self_out[0]
    proj_weight = cross_proj[0]
    value_weight = cross_value[0]
    router_weight = router[0]
    expert_first = expert_in[0, 0]
    expert_second = expert_out[0, 0]
    routing = routes[0]
    experts = router_weight.shape[1]
    cot = cotangent[0]
    cot_f = cot.astype(F32)

    forward = [(0, 1)]
    backward = [(1, 0)]
    half_rows = D // 2
    both_weights = jnp.concatenate([proj_weight, value_weight], axis=1)
    pieces = [both_weights[first:last] for first, last in ((0, 352), (352, 704), (704, D))]

    long_place = jnp.sum(jnp.arange(ITEMS) * (enc_lengths == ENC_MOST)).astype(jnp.int32)
    places = jnp.stack([long_place, decoder.astype(jnp.int32)])
    offsets = ENC_MOST - np.arange(LINE)
    hits = jnp.where(decoder, bucket_hits(offsets, True), bucket_hits(offsets, False))
    lines = jnp.dot(bias_table, hits.T, precision=HIGHEST).reshape(PAIRS, 2, LINE)

    capacity = 5 * row_count // (2 * experts)
    padded = -(-capacity // 8) * 8
    first_chunk = padded // 16 * 8
    chunk_sizes = (first_chunk, padded - first_chunk)
    picked = [
        (routing[:, k : k + 1] == jnp.arange(experts, dtype=jnp.int32)[None, :]).astype(F32)
        for k in range(2)
    ]
    before = jnp.asarray(np.tril(np.ones((row_count, row_count)), -1), BF16)
    counts = dot(before, jnp.concatenate(picked, axis=1).astype(BF16))
    totals = jnp.sum(picked[0], axis=0, keepdims=True)
    slot_first = jnp.sum(picked[0] * counts[:, :experts], axis=1)
    slot_second = jnp.sum(picked[1] * (counts[:, experts:] + totals), axis=1)
    code_first = routing[:, 0] * padded + slot_first.astype(jnp.int32)
    code_second = routing[:, 1] * padded + slot_second.astype(jnp.int32)
    chunk_codes = []
    offset = 0
    for size in chunk_sizes:
        chunk_codes.append(
            (np.arange(experts)[:, None] * padded + offset + np.arange(size)[None, :])
            .reshape(-1)
            .astype(np.int32)
        )
        offset += size

    def spread(first_values, second_values):
        buffers = []
        for codes in chunk_codes:
            hit_first = (codes[:, None] == code_first[None, :]).astype(BF16)
            hit_second = (codes[:, None] == code_second[None, :]).astype(BF16)
            if first_values is second_values:
                buffers.append(dot(hit_first + hit_second, first_values).astype(BF16))
            else:
                buffers.append(
                    (dot(hit_first, first_values) + dot(hit_second, second_values)).astype(BF16)
                )
        return buffers

    def collect(buffers, code, first=0):
        total = None
        for codes, buffer in zip(chunk_codes[first:], buffers):
            part = dot((code[:, None] == codes[None, :]).astype(BF16), buffer)
            total = part if total is None else total + part
        return total

    normed_in = rms_norm(start_rows, gain_rows[0]).astype(BF16)
    project = dot(normed_in, qkv_weight).astype(BF16)
    query, keys, values = (project, 0), (project, PAIRS), (project, 2 * PAIRS)
    context, lse = attend(query, keys, values, places, lines)
    first_half = start_rows + dot(context, out_weight)
    normed_half = rms_norm(first_half, gain_rows[1])
    rounded_half = normed_half.astype(BF16)

    first_rows = jnp.where(decoder, cot, rounded_half)
    sent = spread(first_rows, first_rows)
    arrived_one = [exchange(part, experts) for part in sent]
    returned_one = []
    for k in range(2):
        part, piece = together(arrived_one[k], pieces[k])
        part = expert_forward(part, expert_first, expert_second)
        part, pieces[k] = together(part, lax.ppermute(piece, "half", forward))
        if k == 1:
            part, pieces[2] = together(part, pieces[2])
        returned_one.append(exchange(part, experts))
    returned_one[1], pieces[2] = together(
        returned_one[1], lax.ppermute(pieces[2], "half", forward)
    )
    both_weights = jnp.concatenate(pieces)
    memory_proj, memory_value = both_weights[:, :D], both_weights[:, D:]
    enc_gates = gate_pair(normed_half, router_weight, *picked)
    enc_first = collect(returned_one, code_first)
    enc_second = collect(returned_one, code_second)
    encoded = first_half + enc_gates[0] * enc_first + enc_gates[1] * enc_second
    memory = rms_norm(encoded, gain_rows[2]).astype(BF16)
    memory_in = lax.ppermute(memory, "half", forward)

    cross_query = dot(rounded_half, proj_weight).astype(BF16)
    memory_both = dot(memory_in, both_weights).astype(BF16)
    memory_keys, memory_values = (memory_both, 0), (memory_both, PAIRS)
    cross_context, cross_lse = attend(
        (cross_query, 0), memory_keys, memory_values, places, None
    )
    second_half = first_half + dot(cross_context, value_weight)
    normed_second = rms_norm(second_half, gain_rows[2])
    dec_gates = gate_pair(normed_second, router_weight, *picked)

    rounded_second = normed_second.astype(BF16)
    arrived_two = [exchange(part, experts) for part in spread(rounded_second, rounded_second)]
    all_codes = np.concatenate(chunk_codes)
    gate_rows = jnp.sum(
        jnp.where(all_codes[:, None] == code_first[None, :], dec_gates[0][:, 0][None, :], 0.0)
        + jnp.where(all_codes[:, None] == code_second[None, :], dec_gates[1][:, 0][None, :], 0.0),
        axis=1,
    )
    edge = experts * chunk_sizes[0]

    def exchange_lines(lines):
        parts = []
        for line in lines:
            parts += [line[:edge].reshape(experts, -1), line[edge:].reshape(experts, -1)]
        moved = lax.all_gather(jnp.concatenate(parts, axis=1), "expert", axis=0)
        moved = lax.dynamic_index_in_dim(moved, lax.axis_index("expert"), 1, keepdims=False)
        results = []
        first = 0
        for _ in lines:
            halves = []
            for size in chunk_sizes:
                halves.append(moved[:, first : first + size].reshape(-1))
                first += size
            results.append(jnp.concatenate(halves))
        return results

    actives_two = []
    returned_two = []
    gate_grads = []
    for part, grad_part in zip(arrived_two, arrived_one):
        grad_arrived, active, line = expert_both(part, grad_part, expert_first, expert_second)
        gate_grads.append(line[:, 0])
        actives_two.append(active)
        returned_two.append(exchange(grad_arrived, experts))
    first_parts, line_grads = together(
        [collect(returned_two[:1], code) for code in (code_first, code_second)],
        jnp.concatenate(gate_grads),
    )
    line_grads, arrived_gates = exchange_lines([line_grads, gate_rows])

    def collect_line(line, code):
        return jnp.sum(
            jnp.where(code[:, None] == all_codes[None, :], line[None, :], 0.0), axis=1, keepdims=True
        )

    def router_back(gates, grad_first, grad_second):
        pulled = gates[0] * gates[1] * (grad_first - grad_second)
        grad_logits = pulled * (picked[0] - picked[1])
        return grad_logits, jnp.dot(grad_logits, router_weight.T, precision=HIGHEST)

    dec_logits, dec_normed = router_back(
        dec_gates, collect_line(line_grads, code_first), collect_line(line_grads, code_second)
    )
    dec_normed = (
        dec_normed
        + dec_gates[0] * (first_parts[0] + collect(returned_two[1:], code_first, 1))
        + dec_gates[1] * (first_parts[1] + collect(returned_two[1:], code_second, 1))
    )
    pulled_rows, gain_dec_moe = rms_back(dec_normed, second_half, gain_rows[2])
    grad_second_half = cot_f + pulled_rows

    rounded_grad = grad_second_half.astype(BF16)
    grad_cross_context = dot_nt(rounded_grad, value_weight).astype(BF16)
    grad_cross_query, grad_memory_keys, grad_memory_values = attend_back(
        (cross_query, 0),
        memory_keys,
        memory_values,
        grad_cross_context,
        cross_lse,
        places,
        None,
    )
    key_part = dot_nt(grad_memory_keys, memory_proj)
    value_part, key_part = together(dot_nt(grad_memory_values, memory_value), key_part)
    grad_memory, actives_two = together((key_part + value_part).astype(BF16), actives_two)
    produced_two = [dot(active, expert_second).astype(BF16) for active in actives_two]
    grad_memory, grad_memory_keys, grad_memory_values, produced_two = together(
        lax.ppermute(grad_memory, "half", backward),
        grad_memory_keys,
        grad_memory_values,
        produced_two,
    )
    back_keys = lax.ppermute(grad_memory_keys, "half", backward)
    grad_memory = grad_memory.astype(F32)
    pulled_rows, gain_cross = rms_back(
        dot_nt(grad_cross_query, proj_weight), first_half, gain_rows[1]
    )
    grad_first_dec = grad_second_half + pulled_rows

    pulled_rows, gain_memory = rms_back(grad_memory, encoded, gain_rows[2])
    grad_encoded = cot_f + pulled_rows
    grad_gate_first = jnp.sum(grad_encoded * enc_first, axis=1, keepdims=True)
    grad_gate_second = jnp.sum(grad_encoded * enc_second, axis=1, keepdims=True)
    sent = spread(
        (enc_gates[0] * grad_encoded).astype(BF16), (enc_gates[1] * grad_encoded).astype(BF16)
    )
    arrived_three = [
        exchange(jnp.where(decoder, produced, part), experts)
        for produced, part in zip(produced_two, sent)
    ]
    normed_sharded = jnp.swapaxes(
        normed_in.reshape(row_count, 2, lax.axis_size("expert"), -1), 1, 2
    ).reshape(row_count, D)
    back_keys, grad_memory_values = together(back_keys, grad_memory_values)
    back_values = lax.ppermute(grad_memory_values, "half", backward)
    grad_proj = dot_tn(
        jnp.where(decoder, rounded_half, memory), jnp.where(decoder, grad_cross_query, back_keys)
    ).astype(BF16)
    arrived_three[0], normed_sharded, grad_proj = together(
        arrived_three[0], normed_sharded, grad_proj
    )
    flags = jnp.stack([decoder.astype(jnp.int32), group])
    scales = jnp.where(decoder, arrived_gates, 1.0)[:, None]
    most = max(part.shape[0] for part in arrived_one)
    kept = None
    returned_three = []
    for k, scale in enumerate((scales[:edge], scales[edge:])):
        grad_arrived, kept = expert_back(
            flags,
            arrived_one[k],
            arrived_two[k],
            arrived_three[k],
            scale,
            expert_first,
            expert_second,
            kept,
            k,
            most,
        )
        if k == 0:
            grad_arrived, back_values = together(grad_arrived, back_values)
            arrived_three[1], back_values = together(arrived_three[1], back_values)
            grad_value = dot_tn(
                jnp.where(decoder, cross_context, memory),
                jnp.where(decoder, rounded_grad, back_values),
            )
            early = jnp.concatenate([grad_proj, grad_value.astype(BF16)], axis=1)
            early = group_parts(early, group)
        else:
            grad_arrived, early, kept, returned_three[0], arrived_three = together(
                grad_arrived, early, kept, returned_three[0], arrived_three
            )
        returned_three.append(exchange(grad_arrived, experts))

    expert_rows, expert_grad_rows, actives, keep_halves, send_halves = [
        part.reshape(2 * most, -1) for part in kept
    ]
    first_group = group == 0
    half_ff = FF // 2
    in_cuts = (0, 256, 512, 656, 832, 960, D)
    out_cuts = (0, 352, 736, half_ff)

    def cut(values, cuts):
        return [[values[first:last]] for first, last in zip(cuts[:-1], cuts[1:])]

    first_in = dot_tn(expert_rows[:, : in_cuts[1]], send_halves).astype(BF16)
    rest_in = dot_tn(expert_rows[:, in_cuts[1] :], send_halves).astype(BF16)
    sends = [[first_in]] + cut(rest_in, [place - in_cuts[1] for place in in_cuts[1:]])

    def swapped(parts):
        return [lax.ppermute(part, "group", SWAP) for part in parts]

    gots = [swapped(sends[0])]
    early = with_layout_constraint(early[0] + early[1], Layout((0, 1)))
    returned_three[1], sends, gots, early = together(returned_three[1], sends, gots, early)
    early = expert_scatter(early)

    enc_logits, enc_normed = router_back(enc_gates, grad_gate_first, grad_gate_second)
    enc_normed = enc_normed + collect(returned_three, code_first) + collect(returned_three, code_second)
    pulled_rows, gain_enc_moe = rms_back(enc_normed, first_half, gain_rows[1])
    grad_first = jnp.where(decoder, grad_first_dec, grad_encoded + pulled_rows)

    rounded_grad = grad_first.astype(BF16)
    grad_context = dot_nt(rounded_grad, out_weight).astype(BF16)
    gots.append(swapped(sends[1]))
    halves = [
        attend_back(query, keys, values, grad_context, lse, places, lines, 0, PAIRS // 2)
    ]
    halves[0], gots, sends[2], early, grad_context = together(
        halves[0], gots, sends[2], early, grad_context
    )
    early = expert_gather(early)
    gots.append(swapped(sends[2]))
    halves.append(
        attend_back(query, keys, values, grad_context, lse, places, lines, PAIRS // 2, PAIRS // 2)
    )
    halves, gots, kept, arrived_three = together(
        halves, gots, (actives, expert_grad_rows), arrived_three
    )
    late_first = dot_tn(normed_sharded, jnp.concatenate(halves[0][:3], axis=1))
    late_first, halves, sends[3], kept, rounded_grad, early = together(
        late_first.astype(BF16), halves, sends[3], kept, rounded_grad, early
    )
    late_first = expert_scatter(late_first)
    gots.append(swapped(sends[3]))
    grad_project = jnp.concatenate(
        [half[part] for part in range(3) for half in halves], axis=1
    )
    grad_lines = jnp.concatenate([half[3] for half in halves])

    grad_table = jnp.dot(grad_lines.reshape(H, LINE), hits, precision=HIGHEST)
    grad_router = lax.dot_general(
        jnp.where(decoder, normed_second, normed_half),
        jnp.where(decoder, dec_logits, enc_logits),
        (((0,), (0,)), ((), ())),
        precision=HIGHEST,
    )
    grad_normed = dot_nt(grad_project, qkv_weight)
    grad_normed, gots, sends[4] = together(grad_normed, gots, sends[4])
    gots.append(swapped(sends[4]))
    pulled_rows, gain_self = rms_back(grad_normed, start_rows, gain_rows[0])
    grad_starts = grad_first + pulled_rows
    gain_grads = jnp.stack(
        [
            gain_self,
            jnp.where(decoder, gain_cross, gain_enc_moe),
            jnp.where(decoder, gain_dec_moe, gain_memory),
        ]
    )
    table_rows = jnp.pad(grad_table.reshape(2, -1), ((0, 0), (0, (D - H * NBKT) // 2)))
    small = jnp.concatenate([grad_router, gain_grads.T, table_rows.reshape(D, 1)], axis=1)
    small = jnp.pad(small, ((0, 0), (0, 128 - small.shape[1])))
    late_second = jnp.concatenate(
        [
            dot_tn(normed_sharded, jnp.concatenate(halves[1][:3], axis=1)).astype(BF16),
            shard_rows(small),
            shard_rows(dot_tn(context, rounded_grad)),
        ],
        axis=1,
    )
    late_second = expert_scatter(late_second)
    keep_in = dot_tn(expert_rows, keep_halves)
    keep_in, gots, sends[5], kept, arrived_three = together(
        keep_in, gots, sends[5], kept, arrived_three
    )
    actives, expert_grad_rows = kept
    send_out = dot_tn(
        jnp.where(first_group, actives[:, half_ff:], actives[:, :half_ff]), expert_grad_rows
    ).astype(BF16)
    out_sends = cut(send_out, out_cuts)
    sends[5], out_sends[0] = together(sends[5], out_sends[0])
    gots.append(swapped(sends[5] + out_sends[0]))
    decoded = (
        second_half
        + dec_gates[0] * collect(arrived_three, code_first)
        + dec_gates[1] * collect(arrived_three, code_second)
    )
    result = jnp.where(decoder, decoded, encoded)

    result, gots, out_sends, kept = together(result.astype(BF16), gots, out_sends, kept)
    gots.append(swapped(out_sends[1]))
    actives, expert_grad_rows = kept
    keep_out = dot_tn(
        jnp.where(first_group, actives[:, :half_ff], actives[:, half_ff:]), expert_grad_rows
    )
    late_first, keep_out, gots = together(late_first, keep_out, gots)
    late_first, late_second, gots, out_sends = together(late_first, late_second, gots, out_sends)
    late = group_swap(jnp.concatenate([late_first, late_second], axis=1), group)
    late, out_sends = together(late, out_sends)
    late = expert_gather(late)
    gots.append(swapped(out_sends[2]))
    got_in = [part[0] for part in gots[: len(sends)]]
    got_out = [gots[5][1], gots[6][0], gots[7][0]]
    grad_expert_in = keep_in + jnp.concatenate(got_in).astype(F32)
    grad_expert_out = keep_out + jnp.concatenate(got_out).astype(F32)
    half_columns = D // 2
    grad_qkv = jnp.concatenate(
        [
            late[:, first + half * part : first + half * part + half_columns]
            for part in range(3)
            for first, half in ((0, half_columns), (3 * half_columns, half_columns))
        ],
        axis=1,
    ).astype(F32)
    small = late[:, 3 * D : 3 * D + 128].astype(F32)
    small_table = small[: H * NBKT // 2, experts + 3].reshape(H // 2, NBKT)
    return (
        result[None],
        grad_starts.astype(BF16)[None],
        small[:, experts : experts + 3].T[None],
        small_table[None],
        grad_qkv[None],
        late[:, 3 * D + 128 :].astype(F32)[None],
        early[:, :D].astype(F32)[None],
        early[:, D:].astype(F32)[None],
        small[:, :experts][None],
        grad_expert_in[None, None],
        grad_expert_out[None, None],
    )


def solution(mesh):
    in_specs = (
        P("half", ("expert", "group"), None),
        P("half", ("expert", "group"), None),
        P(("expert", "group")),
        P("half", ("expert", "group"), None),
        P("half", None, None),
        P("half", None, None),
        P("half", None, None),
        P("half", None, None),
        P("half", None, None),
        P("half", None, None),
        P("half", None, None),
        P("half", "expert", None, None),
        P("half", "expert", None, None),
    )
    out_specs = (
        P("half", ("expert", "group"), None),
        P("half", ("expert", "group"), None),
        P("half", None, "group"),
        P("half", "group", None),
        P("half", "group", None),
        P("half", "group", None),
        P("half", "group", None),
        P("half", "group", None),
        P("half", "group", None),
        P("half", "expert", None, "group"),
        P("half", "expert", "group", None),
    )
    return jax.shard_map(
        per_device, mesh=mesh, in_specs=in_specs, out_specs=out_specs, check_vma=False
    )
```

```python
from functools import partial

import jax
import jax.numpy as jnp
import numpy as np
from jax import lax
from jax.experimental import pallas as pl
from jax.experimental.layout import Layout, with_layout_constraint
from jax.experimental.pallas import tpu as pltpu
from jax.sharding import PartitionSpec as P

D = 1024
H = 16
HD = 64
FF = 2816
NBKT = 32
DEC_SLOT = 128
DEC_LEN = 114
ENC_MOST = 512
ENC_MIN = 32
ITEMS = 5

EPSILON = 1e-06
MASKED = -1e30
HIGHEST = lax.Precision.HIGHEST
BLOCK = 128
PAIRS = H // 2
DIAGONAL = ENC_MOST // BLOCK - 1
LINE = 2 * ENC_MOST
FF_TILE = 256
F32 = jnp.float32
BF16 = jnp.bfloat16
GELU_SCALE = float(np.sqrt(2.0 / np.pi))
GELU_CUBE = 0.044715
SWAP = ((0, 1), (1, 0))
VMEM_LIMIT = 60 * 1024 * 1024


def bucket_limits(exact_range, growth, divisions):
    limits = []
    for number in range(1, divisions):
        candidate = exact_range
        while candidate**divisions < exact_range**divisions * growth**number:
            candidate = candidate + 1
        limits.append(candidate)
    return limits


def rel_buckets(offset, causal):
    if causal:
        behind = np.maximum(-offset, 0)
        return np.minimum(behind, 16) + sum(
            (behind >= threshold).astype(np.int32) for threshold in bucket_limits(16, 8, 16)
        )
    distance = np.abs(offset)
    return (
        (offset > 0).astype(np.int32) * 16
        + np.minimum(distance, 8)
        + sum((distance >= threshold).astype(np.int32) for threshold in bucket_limits(8, 16, 8))
    )


def bucket_hits(offset, causal):
    return (rel_buckets(offset, causal)[:, None] == np.arange(NBKT)[None, :]).astype(np.float32)


def inverse_rms(values):
    return lax.rsqrt(jnp.mean(values * values, axis=-1, keepdims=True) + EPSILON)


def rms_norm(values, gain_vec):
    return values * inverse_rms(values) * gain_vec


def rms_back(grad_normed, values, gain_vec):
    scale = inverse_rms(values)
    unit = values * scale
    pulled = grad_normed * gain_vec
    grad_values = scale * (pulled - unit * jnp.mean(pulled * unit, axis=-1, keepdims=True))
    return grad_values, jnp.sum(grad_normed * unit, axis=0)


def dot(a, b):
    return jnp.dot(a, b, preferred_element_type=F32)


def dot_nt(a, b):
    return lax.dot_general(a, b, (((1,), (1,)), ((), ())), preferred_element_type=F32)


def dot_tn(a, b):
    return lax.dot_general(a, b, (((0,), (0,)), ((), ())), preferred_element_type=F32)


def skew(line, rows):
    width = line.shape[1]
    tile = jnp.broadcast_to(line, (8, width))
    row = lax.broadcasted_iota(jnp.int32, (8, width), 0)
    for step in (1, 2, 4):
        tile = jnp.where((row & step) != 0, pltpu.roll(tile, step, 1), tile)
    return jnp.concatenate(
        [pltpu.roll(tile, width - rows + first, 1) for first in range(0, rows, 8)], axis=0
    )


def unskew(total):
    rows, width = total.shape
    summed = None
    for first in range(0, rows, 8):
        moved = pltpu.roll(total[first : first + 8], rows - first, 1)
        summed = moved if summed is None else summed + moved
    row = lax.broadcasted_iota(jnp.int32, (8, width), 0)
    for step in (1, 2, 4):
        summed = jnp.where((row & step) != 0, pltpu.roll(summed, width - step, 1), summed)
    return jnp.sum(summed, axis=0, keepdims=True)


def own_lanes(head):
    return (lax.broadcasted_iota(jnp.int32, (1, 2 * HD), 1) // HD) == head


def head_lanes(head, value):
    return jnp.where(own_lanes(head), value, 0.0).astype(BF16)


def tile_places(keys, queries):
    key = lax.broadcasted_iota(jnp.int32, (keys, queries), 0)
    query = lax.broadcasted_iota(jnp.int32, (keys, queries), 1)
    return key, query


def causal_tile():
    key, query = tile_places(BLOCK, BLOCK)
    return (key <= query) & (key < DEC_LEN)


def short_tile():
    key, query = tile_places(BLOCK, BLOCK)
    return (key // ENC_MIN) == (query // ENC_MIN)


def bias_tiles(rows, queries, shares):
    return [
        (
            slice(block * BLOCK, (block + 1) * BLOCK),
            slice((DIAGONAL - block % (rows // BLOCK // shares)) * BLOCK, None),
            queries,
        )
        for block in range(rows // BLOCK)
    ]


def add_bias(scores, bias_ref, head, shares):
    rows, queries = scores.shape
    return joined(
        [
            scores[here] + bias_ref[head, :, lanes.start : lanes.start + queries]
            for here, lanes, queries in bias_tiles(rows, queries, shares)
        ]
    )


def add_bias_grad(dbias_ref, head, grad_scores, shares):
    rows, queries = grad_scores.shape
    sums = {}
    for here, lanes, queries in bias_tiles(rows, queries, shares):
        part = grad_scores[here]
        sums[lanes.start] = sums[lanes.start] + part if lanes.start in sums else part
    for first, part in sums.items():
        dbias_ref[head, :, first : first + queries] += part


def masked(scores, mask):
    return scores if mask is None else jnp.where(mask, scores, MASKED)


def key_parts(rows, shares):
    step = rows.shape[0] // shares
    return [rows[first : first + step] for first in range(0, rows.shape[0], step)]


def spread_max(values, shares):
    return [jnp.max(part, axis=0, keepdims=True) for part in key_parts(values, shares)]


def joined(parts):
    return parts[0] if len(parts) == 1 else jnp.concatenate(parts, axis=0)


def per_share(lines, rows):
    step = rows // len(lines)
    if len(lines) == 1:
        return lines[0]
    return jnp.concatenate(
        [jnp.broadcast_to(line, (step, line.shape[1])) for line in lines], axis=0
    )


def attend_groups(groups, bias_ref):
    units = [(group, head) for group in groups for head in range(2)]
    scores = []
    for (queries, keys, values, mask), head in units:
        scale = head_lanes(head, HD**-0.5)
        part = joined([dot_nt(key, query * scale) for query, key in zip(queries, keys)])
        scores.append(part)
    contexts = []
    log_sums = []
    for ((queries, keys, values, mask), head), part in zip(units, scores):
        shares = len(queries)
        if bias_ref is not None:
            part = add_bias(part, bias_ref, head, shares)
        part = masked(part, mask)
        highest = spread_max(part, shares)
        exponent = jnp.exp(part - per_share(highest, part.shape[0]))
        totals = [jnp.sum(rows, axis=0, keepdims=True) for rows in key_parts(exponent, shares)]
        log_sums.append([top + jnp.log(total) for top, total in zip(highest, totals)])
        rounded = key_parts(exponent.astype(BF16), shares)
        contexts.append(
            [
                dot_tn(rows, jnp.where(own_lanes(head), value, jnp.ones_like(value)))
                for rows, value in zip(rounded, values)
            ]
        )
    results = []
    for number in range(len(groups)):
        rows = []
        lines = []
        for share in range(len(groups[number][0])):
            first, second = contexts[2 * number][share], contexts[2 * number + 1][share]
            sums = jnp.where(own_lanes(0), second, first)
            context = jnp.where(own_lanes(0), first, second) / pltpu.roll(sums, HD, 1)
            rows.append(context.astype(BF16))
            lines.append(
                jnp.concatenate(
                    [log_sums[2 * number][share], log_sums[2 * number + 1][share]], axis=0
                )
            )
        results.append((rows, lines))
    return results


def attend_groups_back(groups, bias_ref, dbias_ref):
    units = [(group, head) for group in groups for head in range(2)]
    scores = []
    pulls = []
    for (queries, keys, values, mask, grads, lines), head in units:
        scale = head_lanes(head, HD**-0.5)
        own = head_lanes(head, 1.0)
        scores.append(joined([dot_nt(key, query * scale) for query, key in zip(queries, keys)]))
        pulls.append(joined([dot_nt(value, grad * own) for value, grad in zip(values, grads)]))
    totals = []
    for ((queries, keys, values, mask, grads, lines), head), part, pull in zip(units, scores, pulls):
        shares = len(queries)
        scale = head_lanes(head, HD**-0.5)
        own = head_lanes(head, 1.0)
        if bias_ref is not None:
            part = add_bias(part, bias_ref, head, shares)
        part = masked(part, mask)
        weights = jnp.exp(part - per_share([line[head : head + 1] for line in lines], part.shape[0]))
        product = weights * pull
        inner = [jnp.sum(rows, axis=0, keepdims=True) for rows in key_parts(product, shares)]
        grad_scores = product - weights * per_share(inner, part.shape[0])
        if dbias_ref is not None:
            add_bias_grad(dbias_ref, head, grad_scores, shares)
        rounded = key_parts(grad_scores.astype(BF16), shares)
        weights = key_parts(weights.astype(BF16), shares)
        totals.append(
            [
                [dot_tn(rows, key * scale) for rows, key in zip(rounded, keys)],
                [dot(rows, query * scale) for rows, query in zip(rounded, queries)],
                [dot(rows, grad * own) for rows, grad in zip(weights, grads)],
            ]
        )
    results = []
    for number in range(len(groups)):
        results.append(
            [
                [(one + two).astype(BF16) for one, two in zip(first, second)]
                for first, second in zip(totals[2 * number], totals[2 * number + 1])
            ]
        )
    return results


def short_places(place, item):
    later = (item >= place).astype(jnp.int32)
    return pl.multiple_of(item * ENC_MIN + later * ENC_MOST, ENC_MIN), item + later


def gather_short(ref, place):
    return jnp.concatenate(
        [ref[pl.ds(short_places(place, item)[0], ENC_MIN), :] for item in range(ITEMS - 1)], axis=0
    )


def scatter_short(ref, place, rows):
    for item in range(ITEMS - 1):
        ref[pl.ds(short_places(place, item)[0], ENC_MIN), :] = rows[
            item * ENC_MIN : (item + 1) * ENC_MIN
        ]


def block_rows(block):
    return slice(block * BLOCK, (block + 1) * BLOCK)


def self_attend_kernel(place_ref, q_ref, k_ref, v_ref, line_ref, out_ref, lse_ref, bias_ref):
    for head in range(2):
        bias_ref[head] = skew(line_ref[0, head : head + 1, :], BLOCK)
    place = place_ref[0]
    decoder = place_ref[1] == 1

    @pl.when(decoder)
    def _():
        blocks = [block_rows(block) for block in range(ITEMS)]
        shares = tuple([ref[here, :] for here in blocks] for ref in (q_ref, k_ref, v_ref))
        ((rows, lines),) = attend_groups([shares + (joined([causal_tile()] * ITEMS),)], bias_ref)
        for here, part, line in zip(blocks, rows, lines):
            out_ref[here, :] = part
            lse_ref[0, :, here] = line

    @pl.when(jnp.logical_not(decoder))
    def _():
        here = pl.ds(pl.multiple_of(place * ENC_MIN, ENC_MIN), ENC_MOST)
        groups = [
            ([q_ref[here, :]], [k_ref[here, :]], [v_ref[here, :]], None),
            tuple([gather_short(ref, place)] for ref in (q_ref, k_ref, v_ref)) + (short_tile(),),
        ]
        ((rows, lines),) = attend_groups(groups[:1], bias_ref)
        out_ref[here, :] = rows[0]
        lse_ref[0, :, :ENC_MOST] = lines[0]
        ((short_rows, short_lines),) = attend_groups(groups[1:], bias_ref)
        scatter_short(out_ref, place, short_rows[0])
        lse_ref[0, :, ENC_MOST:] = short_lines[0]


def self_attend_back_kernel(
    place_ref, q_ref, k_ref, v_ref, dc_ref, lse_ref, line_ref,
    dq_ref, dk_ref, dv_ref, dline_ref, bias_ref, dbias_ref,
):
    for head in range(2):
        bias_ref[head] = skew(line_ref[0, head : head + 1, :], BLOCK)
    dbias_ref[...] = jnp.zeros(dbias_ref.shape, F32)
    place = place_ref[0]
    decoder = place_ref[1] == 1
    outs = (dq_ref, dk_ref, dv_ref)

    @pl.when(decoder)
    def _():
        blocks = [block_rows(block) for block in range(ITEMS)]
        shares = tuple([ref[here, :] for here in blocks] for ref in (q_ref, k_ref, v_ref))
        shares += (
            joined([causal_tile()] * ITEMS),
            [dc_ref[here, :] for here in blocks],
            [lse_ref[0, :, here] for here in blocks],
        )
        (grads,) = attend_groups_back([shares], bias_ref, dbias_ref)
        for ref, rows in zip(outs, grads):
            for here, part in zip(blocks, rows):
                ref[here, :] = part

    @pl.when(jnp.logical_not(decoder))
    def _():
        here = pl.ds(pl.multiple_of(place * ENC_MIN, ENC_MIN), ENC_MOST)
        groups = [
            (
                [q_ref[here, :]],
                [k_ref[here, :]],
                [v_ref[here, :]],
                None,
                [dc_ref[here, :]],
                [lse_ref[0, :, :ENC_MOST]],
            ),
            (
                [gather_short(q_ref, place)],
                [gather_short(k_ref, place)],
                [gather_short(v_ref, place)],
                short_tile(),
                [gather_short(dc_ref, place)],
                [lse_ref[0, :, ENC_MOST:]],
            ),
        ]
        grads, short_grads = attend_groups_back(groups, bias_ref, dbias_ref)
        for ref, rows, short_rows in zip(outs, grads, short_grads):
            ref[here, :] = rows[0]
            scatter_short(ref, place, short_rows[0])

    for head in range(2):
        dline_ref[0, head : head + 1, :] = unskew(dbias_ref[head])


def cross_places(place):
    long_pair = (
        pl.ds(pl.multiple_of(place * BLOCK, BLOCK), BLOCK),
        pl.ds(pl.multiple_of(place * ENC_MIN, ENC_MIN), ENC_MOST),
    )
    pairs = []
    for item in range(ITEMS - 1):
        start, number = short_places(place, item)
        pairs.append(
            (pl.ds(pl.multiple_of(number * BLOCK, BLOCK), BLOCK), pl.ds(start, ENC_MIN))
        )
    return [[long_pair], pairs]


def cross_attend_kernel(place_ref, q_ref, k_ref, v_ref, out_ref, lse_ref):
    places = cross_places(place_ref[0])
    groups = [
        (
            [q_ref[here, :] for here, there in pairs],
            [k_ref[there, :] for here, there in pairs],
            [v_ref[there, :] for here, there in pairs],
            None,
        )
        for pairs in places
    ]
    number = 0
    for pairs, (rows, lines) in zip(places, attend_groups(groups, None)):
        for (here, there), part, line in zip(pairs, rows, lines):
            out_ref[here, :] = part
            lse_ref[0, :, block_rows(number)] = line
            number += 1


def cross_attend_back_kernel(
    place_ref, q_ref, k_ref, v_ref, dc_ref, lse_ref, dq_ref, dk_ref, dv_ref
):
    places = cross_places(place_ref[0])
    lines = [lse_ref[0, :, block_rows(number)] for number in range(ITEMS)]
    groups = [
        (
            [q_ref[here, :] for here, there in pairs],
            [k_ref[there, :] for here, there in pairs],
            [v_ref[there, :] for here, there in pairs],
            None,
            [dc_ref[here, :] for here, there in pairs],
            part,
        )
        for pairs, part in zip(places, (lines[:1], lines[1:]))
    ]
    for pairs, grads in zip(places, attend_groups_back(groups, None, None)):
        for number, (here, there) in enumerate(pairs):
            dq_ref[here, :] = grads[0][number]
            dk_ref[there, :] = grads[1][number]
            dv_ref[there, :] = grads[2][number]


def pair_spec(rows, first):
    return pl.BlockSpec((rows, 2 * HD), lambda pair, places: (0, first + pair))


def flat_spec(first, *shape):
    return pl.BlockSpec((1,) + shape, lambda pair, places: (first + pair, 0, 0))


def pair_call(kernel, places, operands, specs, out_specs, out_shape, scratch, work, pairs=PAIRS):
    rows = ITEMS * BLOCK
    share = rows * rows * D * pairs // PAIRS
    return pl.pallas_call(
        kernel,
        grid_spec=pltpu.PrefetchScalarGridSpec(
            num_scalar_prefetch=1,
            grid=(pairs,),
            in_specs=specs,
            out_specs=out_specs,
            scratch_shapes=scratch,
        ),
        out_shape=out_shape,
        compiler_params=pltpu.CompilerParams(vmem_limit_bytes=VMEM_LIMIT),
        cost_estimate=pl.CostEstimate(
            flops=work * share, bytes_accessed=16 * rows * D, transcendentals=share // HD
        ),
        name=kernel.__name__,
    )(places, *operands)


def attend(query, keys, values, places, lines):
    rows = query[0].shape[0]
    operands = [part[0] for part in (query, keys, values)]
    specs = [pair_spec(rows, part[1]) for part in (query, keys, values)]
    scratch = []
    if lines is not None:
        operands.append(lines)
        specs.append(flat_spec(0, 2, LINE))
        scratch.append(pltpu.VMEM((2, BLOCK, LINE), F32))
    return pair_call(
        cross_attend_kernel if lines is None else self_attend_kernel,
        places,
        operands,
        specs,
        [pair_spec(rows, 0), flat_spec(0, 2, rows)],
        [
            jax.ShapeDtypeStruct((rows, D), BF16),
            jax.ShapeDtypeStruct((PAIRS, 2, rows), F32),
        ],
        scratch,
        4,
    )


def attend_back(query, keys, values, grad_context, lse, places, lines, first=0, pairs=PAIRS):
    rows = query[0].shape[0]
    operands = [part[0] for part in (query, keys, values)] + [grad_context, lse]
    specs = [pair_spec(rows, part[1] + first) for part in (query, keys, values)]
    specs += [pair_spec(rows, first), flat_spec(first, 2, rows)]
    out_specs = [pair_spec(rows, 0)] * 3
    out_shape = [jax.ShapeDtypeStruct((rows, pairs * 2 * HD), BF16)] * 3
    scratch = []
    if lines is not None:
        operands.append(lines)
        specs.append(flat_spec(first, 2, LINE))
        out_specs.append(flat_spec(0, 2, LINE))
        out_shape.append(jax.ShapeDtypeStruct((pairs, 2, LINE), F32))
        scratch += [pltpu.VMEM((2, BLOCK, LINE), F32)] * 2
    return pair_call(
        cross_attend_back_kernel if lines is None else self_attend_back_kernel,
        places,
        operands,
        specs,
        out_specs,
        out_shape,
        scratch,
        10,
        pairs,
    )


def exchange(rows, experts):
    parts = rows.reshape(experts, -1, rows.shape[-1])
    return lax.all_to_all(parts, "expert", split_axis=0, concat_axis=0, tiled=True).reshape(
        rows.shape
    )


def gelu_parts(value):
    square = value * value
    bend = jnp.tanh(value * (GELU_SCALE + GELU_SCALE * GELU_CUBE * square))
    half = 0.5 + 0.5 * bend
    slope = half + value * (half * (1.0 - bend)) * (
        GELU_SCALE + 3.0 * GELU_SCALE * GELU_CUBE * square
    )
    return value * half, slope


def row_blocks(rows):
    step = rows // 2
    return [slice(first, first + step) for first in range(0, rows, step)]


def expert_forward_kernel(x_ref, gate_ref, up_ref, down_ref, out_ref, total_ref):
    @pl.when(pl.program_id(0) == 0)
    def _():
        total_ref[...] = jnp.zeros(total_ref.shape, F32)

    for here in row_blocks(x_ref.shape[0]):
        rows = x_ref[here, :]
        value, _ = gelu_parts(dot(rows, gate_ref[...]))
        active = (value * dot(rows, up_ref[...])).astype(BF16)
        total_ref[here, :] += dot(active, down_ref[...])

    @pl.when(pl.program_id(0) == pl.num_programs(0) - 1)
    def _():
        out_ref[...] = total_ref[...].astype(BF16)


def hidden_grads(rows, grad_rows, gate_ref, up_ref, down_ref):
    gate = dot(rows, gate_ref[...])
    up = dot(rows, up_ref[...])
    grad_active = dot_nt(grad_rows, down_ref[...])
    value, slope = gelu_parts(gate)
    grad_gate = (grad_active * (up * slope)).astype(BF16)
    grad_up = (grad_active * value).astype(BF16)
    return value * up, grad_active, grad_gate, grad_up


def expert_both_kernel(
    x_ref, g_ref, gate_ref, up_ref, down_ref, dx_ref, active_ref, line_ref, dx_total, line_total
):
    @pl.when(pl.program_id(0) == 0)
    def _():
        dx_total[...] = jnp.zeros(dx_total.shape, F32)
        line_total[...] = jnp.zeros(line_total.shape, F32)

    for here in row_blocks(x_ref.shape[0]):
        active, grad_active, grad_gate, grad_up = hidden_grads(
            x_ref[here, :], g_ref[here, :], gate_ref, up_ref, down_ref
        )
        dx_total[here, :] += dot_nt(grad_gate, gate_ref[...]) + dot_nt(grad_up, up_ref[...])
        active_ref[here, :] = active.astype(BF16)
        product = active * grad_active
        line_total[here, :] += sum(
            product[:, first : first + 128] for first in range(0, product.shape[1], 128)
        )

    @pl.when(pl.program_id(0) == pl.num_programs(0) - 1)
    def _():
        dx_ref[...] = dx_total[...].astype(BF16)
        line_ref[...] = jnp.sum(line_total[...], axis=1, keepdims=True)


def expert_back_kernel(flags_ref, *refs, count):
    one_ref, two_ref, three_ref, scale_ref, gate_ref, up_ref, down_ref = refs[:7]
    dx_ref, x_ref, g_ref, active_ref, keep_ref, send_ref, dx_total, sems = refs[-8:]
    decoder = flags_ref[0] == 1
    first_group = flags_ref[1] == 0
    most = x_ref.shape[1]
    spare = slice(count, most)

    def load(rows, grads):
        copies = [
            pltpu.make_async_copy(rows, x_ref.at[0, pl.ds(0, count)], sems.at[0]),
            pltpu.make_async_copy(grads, g_ref.at[0, pl.ds(0, count)], sems.at[1]),
        ]
        for copy in copies:
            copy.start()
        for copy in copies:
            copy.wait()

    @pl.when(pl.program_id(0) == 0)
    def _():
        dx_total[...] = jnp.zeros(dx_total.shape, F32)

        @pl.when(decoder)
        def _():
            load(two_ref, one_ref)

        @pl.when(jnp.logical_not(decoder))
        def _():
            load(one_ref, three_ref)

        grads = g_ref[0, :count, :].astype(F32) * scale_ref[...]
        g_ref[0, :count, :] = grads.astype(BF16)
        if count < most:
            x_ref[0, spare, :] = jnp.zeros((most - count, D), BF16)
            g_ref[0, spare, :] = jnp.zeros((most - count, D), BF16)

    for here in row_blocks(count):
        active, _, grad_gate, grad_up = hidden_grads(
            x_ref[0, here, :], g_ref[0, here, :], gate_ref, up_ref, down_ref
        )
        dx_total[here, :] += dot_nt(grad_gate, gate_ref[...]) + dot_nt(grad_up, up_ref[...])
        active_ref[0, here, :] = active.astype(BF16)
        keep_ref[0, here, :] = jnp.where(first_group, grad_gate, grad_up)
        send_ref[0, here, :] = jnp.where(first_group, grad_up, grad_gate)
    if count < most:
        for ref in (active_ref, keep_ref, send_ref):
            ref[0, spare, :] = jnp.zeros((most - count, FF_TILE), BF16)

    @pl.when(pl.program_id(0) == pl.num_programs(0) - 1)
    def _():
        dx_ref[...] = dx_total[...].astype(BF16)


def expert_specs(rows):
    tiles = FF // FF_TILE
    whole = pl.BlockSpec((rows, D), lambda tile, *_: (0, 0))
    weight_specs = [
        pl.BlockSpec((D, FF_TILE), lambda tile, *_: (0, tile)),
        pl.BlockSpec((D, FF_TILE), lambda tile, *_: (0, tiles + tile)),
        pl.BlockSpec((FF_TILE, D), lambda tile, *_: (tile, 0)),
    ]
    return whole, weight_specs, tiles


def expert_cost(rows, products):
    return pl.CostEstimate(
        flops=2 * products * rows * D * FF, bytes_accessed=6 * D * FF, transcendentals=rows * FF
    )


def expert_forward(arrived, expert_first, expert_second):
    rows = arrived.shape[0]
    whole, weight_specs, tiles = expert_specs(rows)
    return pl.pallas_call(
        expert_forward_kernel,
        grid=(tiles,),
        in_specs=[whole] + weight_specs,
        out_specs=whole,
        out_shape=jax.ShapeDtypeStruct((rows, D), BF16),
        scratch_shapes=[pltpu.VMEM((rows, D), F32)],
        compiler_params=pltpu.CompilerParams(vmem_limit_bytes=VMEM_LIMIT),
        cost_estimate=expert_cost(rows, 3),
        name="expert_forward",
    )(arrived, expert_first, expert_first, expert_second)


def expert_both(arrived, grad_rows, expert_first, expert_second):
    rows = arrived.shape[0]
    whole, weight_specs, tiles = expert_specs(rows)
    row_shape = jax.ShapeDtypeStruct((rows, D), BF16)
    total = pltpu.VMEM((rows, D), F32)
    return pl.pallas_call(
        expert_both_kernel,
        grid=(tiles,),
        in_specs=[whole, whole] + weight_specs,
        out_specs=[
            whole,
            pl.BlockSpec((rows, FF_TILE), lambda tile: (0, tile)),
            pl.BlockSpec((rows, 1), lambda tile: (0, 0)),
        ],
        out_shape=[
            row_shape,
            jax.ShapeDtypeStruct((rows, FF), BF16),
            jax.ShapeDtypeStruct((rows, 1), F32),
        ],
        scratch_shapes=[total, pltpu.VMEM((rows, 128), F32)],
        compiler_params=pltpu.CompilerParams(vmem_limit_bytes=VMEM_LIMIT),
        cost_estimate=expert_cost(rows, 5),
        name="expert_both",
    )(arrived, grad_rows, expert_first, expert_first, expert_second)


def expert_back(flags, one, two, three, scale, expert_first, expert_second, kept, number, most):
    rows = one.shape[0]
    whole, weight_specs, tiles = expert_specs(rows)
    part = pl.BlockSpec((1, most, D), lambda tile, *_: (number, 0, 0))
    strip = pl.BlockSpec((1, most, FF_TILE), lambda tile, *_: (number, 0, tile))
    kept_shapes = [jax.ShapeDtypeStruct((2, most, D), BF16)] * 2
    kept_shapes += [jax.ShapeDtypeStruct((2, most, FF), BF16)] * 3
    anywhere = pl.BlockSpec(memory_space=pl.ANY)
    in_specs = [anywhere] * 3 + [pl.BlockSpec((rows, 1), lambda tile, *_: (0, 0))] + weight_specs
    operands = [one, two, three, scale, expert_first, expert_first, expert_second]
    aliases = {}
    if kept is not None:
        aliases = {1 + len(operands) + place: 1 + place for place in range(len(kept))}
        in_specs += [anywhere] * len(kept)
        operands += kept
    dx, *kept = pl.pallas_call(
        partial(expert_back_kernel, count=rows),
        grid_spec=pltpu.PrefetchScalarGridSpec(
            num_scalar_prefetch=1,
            grid=(tiles,),
            in_specs=in_specs,
            out_specs=[whole, part, part, strip, strip, strip],
            scratch_shapes=[pltpu.VMEM((rows, D), F32), pltpu.SemaphoreType.DMA((2,))],
        ),
        out_shape=[jax.ShapeDtypeStruct((rows, D), BF16)] + kept_shapes,
        input_output_aliases=aliases,
        compiler_params=pltpu.CompilerParams(vmem_limit_bytes=VMEM_LIMIT),
        cost_estimate=expert_cost(rows, 5),
        name="expert_back",
    )(flags, *operands)
    return dx, list(kept)


def gate_pair(normed, router_weight, picked_first, picked_second):
    logits = jnp.dot(normed, router_weight, precision=HIGHEST)
    first = jnp.sum(logits * picked_first, axis=1, keepdims=True)
    second = jnp.sum(logits * picked_second, axis=1, keepdims=True)
    return jax.nn.sigmoid(first - second), jax.nn.sigmoid(second - first)


def group_parts(rows, group):
    half = rows.shape[0] // 2
    sent = lax.dynamic_slice_in_dim(rows, (1 - group) * half, half, 0)
    kept = lax.dynamic_slice_in_dim(rows, group * half, half, 0)
    return kept, lax.ppermute(sent, "group", SWAP)


def group_swap(rows, group):
    kept, got = group_parts(rows, group)
    return kept + got


def shard_rows(grad):
    rows, columns = grad.shape
    parts = grad.astype(BF16).reshape(2, lax.axis_size("expert"), -1, columns)
    return jnp.swapaxes(parts, 0, 1).reshape(rows, columns)


def expert_scatter(rows):
    return lax.psum_scatter(rows, "expert", scatter_dimension=0, tiled=True)


def expert_gather(rows):
    return lax.all_gather(rows, "expert", axis=0, tiled=True)


def widen_kernel(part_ref, *refs):
    refs[-1][...] = part_ref[...].astype(F32)


def interleave(part, place, whole=None):
    rows = part.shape[0]
    half = D // 2
    operands = [part] if whole is None else [part, whole]
    specs = [pl.BlockSpec((rows, half), lambda step: (0, step))]
    if whole is not None:
        specs.append(pl.BlockSpec(memory_space=pl.ANY))
    return pl.pallas_call(
        widen_kernel,
        grid=(3,),
        in_specs=specs,
        out_specs=pl.BlockSpec((rows, half), lambda step: (0, 2 * step + place)),
        out_shape=jax.ShapeDtypeStruct((rows, 3 * D), F32),
        input_output_aliases={} if whole is None else {1: 0},
        compiler_params=pltpu.CompilerParams(vmem_limit_bytes=VMEM_LIMIT),
        cost_estimate=pl.CostEstimate(flops=0, bytes_accessed=9 * rows * D, transcendentals=0),
        name="interleave",
    )(*operands)


def together(*values):
    return lax.optimization_barrier(values)


def per_device(
    inputs,
    cotangent,
    enc_lengths,
    routes,
    norm_gains,
    rel_bias,
    self_qkv,
    self_out,
    cross_proj,
    cross_value,
    router,
    expert_in,
    expert_out,
):
    decoder = lax.axis_index("half") == 1
    group = lax.axis_index("group")
    start_rows = inputs[0].astype(F32)
    row_count = start_rows.shape[0]
    gain_rows = norm_gains[0]
    bias_table = rel_bias[0]
    qkv_weight = self_qkv[0]
    out_weight = self_out[0]
    proj_weight = cross_proj[0]
    value_weight = cross_value[0]
    router_weight = router[0]
    expert_first = expert_in[0, 0]
    expert_second = expert_out[0, 0]
    routing = routes[0]
    experts = router_weight.shape[1]
    cot = cotangent[0]
    cot_f = cot.astype(F32)

    forward = [(0, 1)]
    backward = [(1, 0)]
    half_rows = D // 2
    both_weights = jnp.concatenate([proj_weight, value_weight], axis=1)
    pieces = [both_weights[first:last] for first, last in ((0, 352), (352, 704), (704, D))]

    long_place = jnp.sum(jnp.arange(ITEMS) * (enc_lengths == ENC_MOST)).astype(jnp.int32)
    places = jnp.stack([long_place, decoder.astype(jnp.int32)])
    offsets = ENC_MOST - np.arange(LINE)
    hits = jnp.where(decoder, bucket_hits(offsets, True), bucket_hits(offsets, False))
    lines = jnp.dot(bias_table, hits.T, precision=HIGHEST).reshape(PAIRS, 2, LINE)

    capacity = 5 * row_count // (2 * experts)
    padded = -(-capacity // 8) * 8
    first_chunk = padded // 16 * 8
    chunk_sizes = (first_chunk, padded - first_chunk)
    picked = [
        (routing[:, k : k + 1] == jnp.arange(experts, dtype=jnp.int32)[None, :]).astype(F32)
        for k in range(2)
    ]
    before = jnp.asarray(np.tril(np.ones((row_count, row_count)), -1), BF16)
    counts = dot(before, jnp.concatenate(picked, axis=1).astype(BF16))
    totals = jnp.sum(picked[0], axis=0, keepdims=True)
    slot_first = jnp.sum(picked[0] * counts[:, :experts], axis=1)
    slot_second = jnp.sum(picked[1] * (counts[:, experts:] + totals), axis=1)
    code_first = routing[:, 0] * padded + slot_first.astype(jnp.int32)
    code_second = routing[:, 1] * padded + slot_second.astype(jnp.int32)
    chunk_codes = []
    offset = 0
    for size in chunk_sizes:
        chunk_codes.append(
            (np.arange(experts)[:, None] * padded + offset + np.arange(size)[None, :])
            .reshape(-1)
            .astype(np.int32)
        )
        offset += size

    def spread(first_values, second_values):
        buffers = []
        for codes in chunk_codes:
            hit_first = (codes[:, None] == code_first[None, :]).astype(BF16)
            hit_second = (codes[:, None] == code_second[None, :]).astype(BF16)
            if first_values is second_values:
                buffers.append(dot(hit_first + hit_second, first_values).astype(BF16))
            else:
                buffers.append(
                    (dot(hit_first, first_values) + dot(hit_second, second_values)).astype(BF16)
                )
        return buffers

    def collect(buffers, code, first=0):
        total = None
        for codes, buffer in zip(chunk_codes[first:], buffers):
            part = dot((code[:, None] == codes[None, :]).astype(BF16), buffer)
            total = part if total is None else total + part
        return total

    normed_in = rms_norm(start_rows, gain_rows[0]).astype(BF16)
    project = dot(normed_in, qkv_weight).astype(BF16)
    query, keys, values = (project, 0), (project, PAIRS), (project, 2 * PAIRS)
    context, lse = attend(query, keys, values, places, lines)
    first_half = start_rows + dot(context, out_weight)
    normed_half = rms_norm(first_half, gain_rows[1])
    rounded_half = normed_half.astype(BF16)

    first_rows = jnp.where(decoder, cot, rounded_half)
    sent = spread(first_rows, first_rows)
    arrived_one = [exchange(part, experts) for part in sent]
    returned_one = []
    for k in range(2):
        part, piece = together(arrived_one[k], pieces[k])
        part = expert_forward(part, expert_first, expert_second)
        part, pieces[k] = together(part, lax.ppermute(piece, "half", forward))
        if k == 1:
            part, pieces[2] = together(part, pieces[2])
        returned_one.append(exchange(part, experts))
    returned_one[1], pieces[2] = together(
        returned_one[1], lax.ppermute(pieces[2], "half", forward)
    )
    both_weights = jnp.concatenate(pieces)
    memory_proj, memory_value = both_weights[:, :D], both_weights[:, D:]
    enc_gates = gate_pair(normed_half, router_weight, *picked)
    enc_first = collect(returned_one, code_first)
    enc_second = collect(returned_one, code_second)
    encoded = first_half + enc_gates[0] * enc_first + enc_gates[1] * enc_second
    memory = rms_norm(encoded, gain_rows[2]).astype(BF16)
    memory_in = lax.ppermute(memory, "half", forward)

    cross_query = dot(rounded_half, proj_weight).astype(BF16)
    memory_both = dot(memory_in, both_weights).astype(BF16)
    memory_keys, memory_values = (memory_both, 0), (memory_both, PAIRS)
    cross_context, cross_lse = attend(
        (cross_query, 0), memory_keys, memory_values, places, None
    )
    second_half = first_half + dot(cross_context, value_weight)
    normed_second = rms_norm(second_half, gain_rows[2])
    dec_gates = gate_pair(normed_second, router_weight, *picked)

    rounded_second = normed_second.astype(BF16)
    arrived_two = [exchange(part, experts) for part in spread(rounded_second, rounded_second)]
    all_codes = np.concatenate(chunk_codes)
    gate_rows = jnp.sum(
        jnp.where(all_codes[:, None] == code_first[None, :], dec_gates[0][:, 0][None, :], 0.0)
        + jnp.where(all_codes[:, None] == code_second[None, :], dec_gates[1][:, 0][None, :], 0.0),
        axis=1,
    )
    edge = experts * chunk_sizes[0]

    def exchange_lines(lines):
        parts = []
        for line in lines:
            parts += [line[:edge].reshape(experts, -1), line[edge:].reshape(experts, -1)]
        moved = lax.all_gather(jnp.concatenate(parts, axis=1), "expert", axis=0)
        moved = lax.dynamic_index_in_dim(moved, lax.axis_index("expert"), 1, keepdims=False)
        results = []
        first = 0
        for _ in lines:
            halves = []
            for size in chunk_sizes:
                halves.append(moved[:, first : first + size].reshape(-1))
                first += size
            results.append(jnp.concatenate(halves))
        return results

    actives_two = []
    returned_two = []
    gate_grads = []
    for part, grad_part in zip(arrived_two, arrived_one):
        grad_arrived, active, line = expert_both(part, grad_part, expert_first, expert_second)
        gate_grads.append(line[:, 0])
        actives_two.append(active)
        returned_two.append(exchange(grad_arrived, experts))
    first_parts, line_grads = together(
        [collect(returned_two[:1], code) for code in (code_first, code_second)],
        jnp.concatenate(gate_grads),
    )
    line_grads, arrived_gates = exchange_lines([line_grads, gate_rows])

    def collect_line(line, code):
        return jnp.sum(
            jnp.where(code[:, None] == all_codes[None, :], line[None, :], 0.0), axis=1, keepdims=True
        )

    def router_back(gates, grad_first, grad_second):
        pulled = gates[0] * gates[1] * (grad_first - grad_second)
        grad_logits = pulled * (picked[0] - picked[1])
        return grad_logits, jnp.dot(grad_logits, router_weight.T, precision=HIGHEST)

    dec_logits, dec_normed = router_back(
        dec_gates, collect_line(line_grads, code_first), collect_line(line_grads, code_second)
    )
    dec_normed = (
        dec_normed
        + dec_gates[0] * (first_parts[0] + collect(returned_two[1:], code_first, 1))
        + dec_gates[1] * (first_parts[1] + collect(returned_two[1:], code_second, 1))
    )
    pulled_rows, gain_dec_moe = rms_back(dec_normed, second_half, gain_rows[2])
    grad_second_half = cot_f + pulled_rows

    rounded_grad = grad_second_half.astype(BF16)
    grad_cross_context = dot_nt(rounded_grad, value_weight).astype(BF16)
    grad_cross_query, grad_memory_keys, grad_memory_values = attend_back(
        (cross_query, 0),
        memory_keys,
        memory_values,
        grad_cross_context,
        cross_lse,
        places,
        None,
    )
    key_part = dot_nt(grad_memory_keys, memory_proj)
    value_part, key_part = together(dot_nt(grad_memory_values, memory_value), key_part)
    grad_memory, actives_two = together((key_part + value_part).astype(BF16), actives_two)
    produced_two = [dot(active, expert_second).astype(BF16) for active in actives_two]
    grad_memory, grad_memory_keys, grad_memory_values, produced_two = together(
        lax.ppermute(grad_memory, "half", backward),
        grad_memory_keys,
        grad_memory_values,
        produced_two,
    )
    back_keys = lax.ppermute(grad_memory_keys, "half", backward)
    grad_memory = grad_memory.astype(F32)
    pulled_rows, gain_cross = rms_back(
        dot_nt(grad_cross_query, proj_weight), first_half, gain_rows[1]
    )
    grad_first_dec = grad_second_half + pulled_rows

    pulled_rows, gain_memory = rms_back(grad_memory, encoded, gain_rows[2])
    grad_encoded = cot_f + pulled_rows
    grad_gate_first = jnp.sum(grad_encoded * enc_first, axis=1, keepdims=True)
    grad_gate_second = jnp.sum(grad_encoded * enc_second, axis=1, keepdims=True)
    sent = spread(
        (enc_gates[0] * grad_encoded).astype(BF16), (enc_gates[1] * grad_encoded).astype(BF16)
    )
    normed_sharded = jnp.swapaxes(
        normed_in.reshape(row_count, 2, lax.axis_size("expert"), -1), 1, 2
    ).reshape(row_count, D)
    back_keys, grad_memory_values = together(back_keys, grad_memory_values)
    back_values = lax.ppermute(grad_memory_values, "half", backward)
    grad_proj = dot_tn(
        jnp.where(decoder, rounded_half, memory), jnp.where(decoder, grad_cross_query, back_keys)
    ).astype(BF16)
    sent = [jnp.where(decoder, produced, part) for produced, part in zip(produced_two, sent)]
    sent[1], normed_sharded, grad_proj = together(sent[1], normed_sharded, grad_proj)
    arrived_three = [exchange(part, experts) for part in sent]
    flags = jnp.stack([decoder.astype(jnp.int32), group])
    scales = jnp.where(decoder, arrived_gates, 1.0)[:, None]
    most = max(part.shape[0] for part in arrived_one)
    kept = None
    returned_three = []
    for k, scale in enumerate((scales[:edge], scales[edge:])):
        grad_arrived, kept = expert_back(
            flags,
            arrived_one[k],
            arrived_two[k],
            arrived_three[k],
            scale,
            expert_first,
            expert_second,
            kept,
            k,
            most,
        )
        if k == 0:
            grad_arrived, back_values = together(grad_arrived, back_values)
            arrived_three[1], back_values = together(arrived_three[1], back_values)
            grad_value = dot_tn(
                jnp.where(decoder, cross_context, memory),
                jnp.where(decoder, rounded_grad, back_values),
            )
            early = jnp.concatenate([grad_proj, grad_value.astype(BF16)], axis=1)
            early = group_parts(early, group)
        else:
            grad_arrived, early, kept, returned_three[0], arrived_three = together(
                grad_arrived, early, kept, returned_three[0], arrived_three
            )
        returned_three.append(exchange(grad_arrived, experts))

    expert_rows, expert_grad_rows, actives, keep_halves, send_halves = [
        part.reshape(2 * most, -1) for part in kept
    ]
    first_group = group == 0
    half_ff = FF // 2
    in_cuts = (0, 208, 464, 608, 784, 928, D)
    out_cuts = (0, 256, 608, half_ff)

    def cut(values, cuts):
        return [[values[first:last]] for first, last in zip(cuts[:-1], cuts[1:])]

    first_in = dot_tn(expert_rows[:, : in_cuts[1]], send_halves).astype(BF16)
    rest_in = dot_tn(expert_rows[:, in_cuts[1] :], send_halves).astype(BF16)
    sends = [[first_in]] + cut(rest_in, [place - in_cuts[1] for place in in_cuts[1:]])

    def swapped(parts):
        return [lax.ppermute(part, "group", SWAP) for part in parts]

    gots = [swapped(sends[0])]
    early = with_layout_constraint(early[0] + early[1], Layout((0, 1)))
    returned_three[1], sends, gots, early = together(returned_three[1], sends, gots, early)
    early = expert_scatter(early)

    enc_logits, enc_normed = router_back(enc_gates, grad_gate_first, grad_gate_second)
    enc_normed = enc_normed + collect(returned_three, code_first) + collect(returned_three, code_second)
    pulled_rows, gain_enc_moe = rms_back(enc_normed, first_half, gain_rows[1])
    grad_first = jnp.where(decoder, grad_first_dec, grad_encoded + pulled_rows)

    rounded_grad = grad_first.astype(BF16)
    grad_context = dot_nt(rounded_grad, out_weight).astype(BF16)
    gots.append(swapped(sends[1]))
    halves = [
        attend_back(query, keys, values, grad_context, lse, places, lines, 0, PAIRS // 2)
    ]
    halves[0], gots, sends[2], early, grad_context = together(
        halves[0], gots, sends[2], early, grad_context
    )
    early = expert_gather(early)
    gots.append(swapped(sends[2]))
    halves.append(
        attend_back(query, keys, values, grad_context, lse, places, lines, PAIRS // 2, PAIRS // 2)
    )
    halves, gots, kept, arrived_three = together(
        halves, gots, (actives, expert_grad_rows), arrived_three
    )
    late_first = dot_tn(normed_sharded, jnp.concatenate(halves[0][:3], axis=1))
    late_first, halves, sends[3], kept, rounded_grad, early = together(
        late_first.astype(BF16), halves, sends[3], kept, rounded_grad, early
    )
    late_first = expert_scatter(late_first)
    gots.append(swapped(sends[3]))
    grad_project = jnp.concatenate(
        [half[part] for part in range(3) for half in halves], axis=1
    )
    grad_lines = jnp.concatenate([half[3] for half in halves])

    grad_table = jnp.dot(grad_lines.reshape(H, LINE), hits, precision=HIGHEST)
    grad_router = lax.dot_general(
        jnp.where(decoder, normed_second, normed_half),
        jnp.where(decoder, dec_logits, enc_logits),
        (((0,), (0,)), ((), ())),
        precision=HIGHEST,
    )
    grad_normed = dot_nt(grad_project, qkv_weight)
    grad_normed, gots, sends[4] = together(grad_normed, gots, sends[4])
    gots.append(swapped(sends[4]))
    pulled_rows, gain_self = rms_back(grad_normed, start_rows, gain_rows[0])
    grad_starts = grad_first + pulled_rows
    gain_grads = jnp.stack(
        [
            gain_self,
            jnp.where(decoder, gain_cross, gain_enc_moe),
            jnp.where(decoder, gain_dec_moe, gain_memory),
        ]
    )
    table_rows = jnp.pad(grad_table.reshape(2, -1), ((0, 0), (0, (D - H * NBKT) // 2)))
    small = jnp.concatenate([grad_router, gain_grads.T, table_rows.reshape(D, 1)], axis=1)
    small = jnp.pad(small, ((0, 0), (0, 128 - small.shape[1])))
    late_second = jnp.concatenate(
        [
            dot_tn(normed_sharded, jnp.concatenate(halves[1][:3], axis=1)).astype(BF16),
            shard_rows(small),
            shard_rows(dot_tn(context, rounded_grad)),
        ],
        axis=1,
    )
    late_second = expert_scatter(late_second)
    keep_in = dot_tn(expert_rows, keep_halves)
    keep_in, gots, late_first, sends[5], kept, arrived_three = together(
        keep_in, gots, late_first, sends[5], kept, arrived_three
    )
    late_first = group_swap(late_first, group)
    actives, expert_grad_rows = kept
    send_out = dot_tn(
        jnp.where(first_group, actives[:, half_ff:], actives[:, :half_ff]), expert_grad_rows
    ).astype(BF16)
    out_sends = cut(send_out, out_cuts)
    sends[5], out_sends[0], late_first = together(sends[5], out_sends[0], late_first)
    late_first = expert_gather(late_first)
    gots.append(swapped(sends[5] + out_sends[0]))
    decoded = (
        second_half
        + dec_gates[0] * collect(arrived_three, code_first)
        + dec_gates[1] * collect(arrived_three, code_second)
    )
    result = jnp.where(decoder, decoded, encoded)

    result, gots, out_sends, kept = together(result.astype(BF16), gots, out_sends, kept)
    gots.append(swapped(out_sends[1]))
    actives, expert_grad_rows = kept
    keep_out = dot_tn(
        jnp.where(first_group, actives[:, :half_ff], actives[:, half_ff:]), expert_grad_rows
    )
    late_second, keep_out, gots, out_sends = together(late_second, keep_out, gots, out_sends)
    late_second = group_swap(late_second, group)
    late_second, out_sends = together(late_second, out_sends)
    late_second = expert_gather(late_second)
    gots.append(swapped(out_sends[2]))
    got_in = [part[0] for part in gots[: len(sends)]]
    got_out = [gots[5][1], gots[6][0], gots[7][0]]
    grad_expert_in = keep_in + jnp.concatenate(got_in).astype(F32)
    grad_expert_out = keep_out + jnp.concatenate(got_out).astype(F32)
    small = late_second[:, 3 * D // 2 : 3 * D // 2 + 128].astype(F32)
    small_table = small[: H * NBKT // 2, experts + 3].reshape(H // 2, NBKT)
    return (
        result[None],
        grad_starts.astype(BF16)[None],
        small[:, experts : experts + 3].T[None],
        small_table[None],
        interleave(late_second, 1, interleave(late_first, 0))[None],
        late_second[:, 3 * D // 2 + 128 :].astype(F32)[None],
        early[:, :D].astype(F32)[None],
        early[:, D:].astype(F32)[None],
        small[:, :experts][None],
        grad_expert_in[None, None],
        grad_expert_out[None, None],
    )


def solution(mesh):
    in_specs = (
        P("half", ("expert", "group"), None),
        P("half", ("expert", "group"), None),
        P(("expert", "group")),
        P("half", ("expert", "group"), None),
        P("half", None, None),
        P("half", None, None),
        P("half", None, None),
        P("half", None, None),
        P("half", None, None),
        P("half", None, None),
        P("half", None, None),
        P("half", "expert", None, None),
        P("half", "expert", None, None),
    )
    out_specs = (
        P("half", ("expert", "group"), None),
        P("half", ("expert", "group"), None),
        P("half", None, "group"),
        P("half", "group", None),
        P("half", "group", None),
        P("half", "group", None),
        P("half", "group", None),
        P("half", "group", None),
        P("half", "group", None),
        P("half", "expert", None, "group"),
        P("half", "expert", "group", None),
    )
    return jax.shard_map(
        per_device, mesh=mesh, in_specs=in_specs, out_specs=out_specs, check_vma=False
    )
```

```python
from functools import partial

import jax
import jax.numpy as jnp
import numpy as np
from jax import lax
from jax.experimental import pallas as pl
from jax.experimental.layout import Layout, with_layout_constraint
from jax.experimental.pallas import tpu as pltpu
from jax.sharding import PartitionSpec as P

D = 1024
H = 16
HD = 64
FF = 2816
NBKT = 32
DEC_SLOT = 128
DEC_LEN = 114
ENC_MOST = 512
ENC_MIN = 32
ITEMS = 5

EPSILON = 1e-06
MASKED = -1e30
HIGHEST = lax.Precision.HIGHEST
BLOCK = 128
PAIRS = H // 2
DIAGONAL = ENC_MOST // BLOCK - 1
LINE = 2 * ENC_MOST
FF_TILE = 256
F32 = jnp.float32
BF16 = jnp.bfloat16
GELU_SCALE = float(np.sqrt(2.0 / np.pi))
GELU_CUBE = 0.044715
SWAP = ((0, 1), (1, 0))
VMEM_LIMIT = 60 * 1024 * 1024


def bucket_limits(exact_range, growth, divisions):
    limits = []
    for number in range(1, divisions):
        candidate = exact_range
        while candidate**divisions < exact_range**divisions * growth**number:
            candidate = candidate + 1
        limits.append(candidate)
    return limits


def rel_buckets(offset, causal):
    if causal:
        behind = np.maximum(-offset, 0)
        return np.minimum(behind, 16) + sum(
            (behind >= threshold).astype(np.int32) for threshold in bucket_limits(16, 8, 16)
        )
    distance = np.abs(offset)
    return (
        (offset > 0).astype(np.int32) * 16
        + np.minimum(distance, 8)
        + sum((distance >= threshold).astype(np.int32) for threshold in bucket_limits(8, 16, 8))
    )


def bucket_hits(offset, causal):
    return (rel_buckets(offset, causal)[:, None] == np.arange(NBKT)[None, :]).astype(np.float32)


def inverse_rms(values):
    return lax.rsqrt(jnp.mean(values * values, axis=-1, keepdims=True) + EPSILON)


def rms_norm(values, gain_vec):
    return values * inverse_rms(values) * gain_vec


def rms_back(grad_normed, values, gain_vec):
    scale = inverse_rms(values)
    unit = values * scale
    pulled = grad_normed * gain_vec
    grad_values = scale * (pulled - unit * jnp.mean(pulled * unit, axis=-1, keepdims=True))
    return grad_values, jnp.sum(grad_normed * unit, axis=0)


def dot(a, b):
    return jnp.dot(a, b, preferred_element_type=F32)


def dot_nt(a, b):
    return lax.dot_general(a, b, (((1,), (1,)), ((), ())), preferred_element_type=F32)


def dot_tn(a, b):
    return lax.dot_general(a, b, (((0,), (0,)), ((), ())), preferred_element_type=F32)


def skew(line, rows):
    width = line.shape[1]
    tile = jnp.broadcast_to(line, (8, width))
    row = lax.broadcasted_iota(jnp.int32, (8, width), 0)
    for step in (1, 2, 4):
        tile = jnp.where((row & step) != 0, pltpu.roll(tile, step, 1), tile)
    return jnp.concatenate(
        [pltpu.roll(tile, width - rows + first, 1) for first in range(0, rows, 8)], axis=0
    )


def unskew(total):
    rows, width = total.shape
    summed = None
    for first in range(0, rows, 8):
        moved = pltpu.roll(total[first : first + 8], rows - first, 1)
        summed = moved if summed is None else summed + moved
    row = lax.broadcasted_iota(jnp.int32, (8, width), 0)
    for step in (1, 2, 4):
        summed = jnp.where((row & step) != 0, pltpu.roll(summed, width - step, 1), summed)
    return jnp.sum(summed, axis=0, keepdims=True)


def own_lanes(head):
    return (lax.broadcasted_iota(jnp.int32, (1, 2 * HD), 1) // HD) == head


def head_lanes(head, value):
    return jnp.where(own_lanes(head), value, 0.0).astype(BF16)


def tile_places(keys, queries):
    key = lax.broadcasted_iota(jnp.int32, (keys, queries), 0)
    query = lax.broadcasted_iota(jnp.int32, (keys, queries), 1)
    return key, query


def causal_tile():
    key, query = tile_places(BLOCK, BLOCK)
    return (key <= query) & (key < DEC_LEN)


def short_tile():
    key, query = tile_places(BLOCK, BLOCK)
    return (key // ENC_MIN) == (query // ENC_MIN)


def bias_tiles(rows, queries, shares):
    return [
        (
            slice(block * BLOCK, (block + 1) * BLOCK),
            slice((DIAGONAL - block % (rows // BLOCK // shares)) * BLOCK, None),
            queries,
        )
        for block in range(rows // BLOCK)
    ]


def add_bias(scores, bias_ref, head, shares):
    rows, queries = scores.shape
    return joined(
        [
            scores[here] + bias_ref[head, :, lanes.start : lanes.start + queries]
            for here, lanes, queries in bias_tiles(rows, queries, shares)
        ]
    )


def add_bias_grad(dbias_ref, head, grad_scores, shares):
    rows, queries = grad_scores.shape
    sums = {}
    for here, lanes, queries in bias_tiles(rows, queries, shares):
        part = grad_scores[here]
        sums[lanes.start] = sums[lanes.start] + part if lanes.start in sums else part
    for first, part in sums.items():
        dbias_ref[head, :, first : first + queries] += part


def masked(scores, mask):
    return scores if mask is None else jnp.where(mask, scores, MASKED)


def key_parts(rows, shares):
    step = rows.shape[0] // shares
    return [rows[first : first + step] for first in range(0, rows.shape[0], step)]


def spread_max(values, shares):
    return [jnp.max(part, axis=0, keepdims=True) for part in key_parts(values, shares)]


def joined(parts):
    return parts[0] if len(parts) == 1 else jnp.concatenate(parts, axis=0)


def per_share(lines, rows):
    step = rows // len(lines)
    if len(lines) == 1:
        return lines[0]
    return jnp.concatenate(
        [jnp.broadcast_to(line, (step, line.shape[1])) for line in lines], axis=0
    )


def attend_groups(groups, bias_ref):
    units = [(group, head) for group in groups for head in range(2)]
    scores = []
    for (queries, keys, values, mask), head in units:
        scale = head_lanes(head, HD**-0.5)
        part = joined([dot_nt(key, query * scale) for query, key in zip(queries, keys)])
        scores.append(part)
    contexts = []
    log_sums = []
    for ((queries, keys, values, mask), head), part in zip(units, scores):
        shares = len(queries)
        if bias_ref is not None:
            part = add_bias(part, bias_ref, head, shares)
        part = masked(part, mask)
        highest = spread_max(part, shares)
        exponent = jnp.exp(part - per_share(highest, part.shape[0]))
        totals = [jnp.sum(rows, axis=0, keepdims=True) for rows in key_parts(exponent, shares)]
        log_sums.append([top + jnp.log(total) for top, total in zip(highest, totals)])
        rounded = key_parts(exponent.astype(BF16), shares)
        contexts.append(
            [
                dot_tn(rows, jnp.where(own_lanes(head), value, jnp.ones_like(value)))
                for rows, value in zip(rounded, values)
            ]
        )
    results = []
    for number in range(len(groups)):
        rows = []
        lines = []
        for share in range(len(groups[number][0])):
            first, second = contexts[2 * number][share], contexts[2 * number + 1][share]
            sums = jnp.where(own_lanes(0), second, first)
            context = jnp.where(own_lanes(0), first, second) / pltpu.roll(sums, HD, 1)
            rows.append(context.astype(BF16))
            lines.append(
                jnp.concatenate(
                    [log_sums[2 * number][share], log_sums[2 * number + 1][share]], axis=0
                )
            )
        results.append((rows, lines))
    return results


def attend_groups_back(groups, bias_ref, dbias_ref):
    units = [(group, head) for group in groups for head in range(2)]
    scores = []
    pulls = []
    for (queries, keys, values, mask, grads, lines), head in units:
        scale = head_lanes(head, HD**-0.5)
        own = head_lanes(head, 1.0)
        scores.append(joined([dot_nt(key, query * scale) for query, key in zip(queries, keys)]))
        pulls.append(joined([dot_nt(value, grad * own) for value, grad in zip(values, grads)]))
    totals = []
    for ((queries, keys, values, mask, grads, lines), head), part, pull in zip(units, scores, pulls):
        shares = len(queries)
        scale = head_lanes(head, HD**-0.5)
        own = head_lanes(head, 1.0)
        if bias_ref is not None:
            part = add_bias(part, bias_ref, head, shares)
        part = masked(part, mask)
        weights = jnp.exp(part - per_share([line[head : head + 1] for line in lines], part.shape[0]))
        product = weights * pull
        inner = [jnp.sum(rows, axis=0, keepdims=True) for rows in key_parts(product, shares)]
        grad_scores = product - weights * per_share(inner, part.shape[0])
        if dbias_ref is not None:
            add_bias_grad(dbias_ref, head, grad_scores, shares)
        rounded = key_parts(grad_scores.astype(BF16), shares)
        weights = key_parts(weights.astype(BF16), shares)
        totals.append(
            [
                [dot_tn(rows, key * scale) for rows, key in zip(rounded, keys)],
                [dot(rows, query * scale) for rows, query in zip(rounded, queries)],
                [dot(rows, grad * own) for rows, grad in zip(weights, grads)],
            ]
        )
    results = []
    for number in range(len(groups)):
        results.append(
            [
                [(one + two).astype(BF16) for one, two in zip(first, second)]
                for first, second in zip(totals[2 * number], totals[2 * number + 1])
            ]
        )
    return results


def short_places(place, item):
    later = (item >= place).astype(jnp.int32)
    return pl.multiple_of(item * ENC_MIN + later * ENC_MOST, ENC_MIN), item + later


def gather_short(ref, place):
    return jnp.concatenate(
        [ref[pl.ds(short_places(place, item)[0], ENC_MIN), :] for item in range(ITEMS - 1)], axis=0
    )


def scatter_short(ref, place, rows):
    for item in range(ITEMS - 1):
        ref[pl.ds(short_places(place, item)[0], ENC_MIN), :] = rows[
            item * ENC_MIN : (item + 1) * ENC_MIN
        ]


def block_rows(block):
    return slice(block * BLOCK, (block + 1) * BLOCK)


def self_attend_kernel(place_ref, q_ref, k_ref, v_ref, line_ref, out_ref, lse_ref, bias_ref):
    for head in range(2):
        bias_ref[head] = skew(line_ref[0, head : head + 1, :], BLOCK)
    place = place_ref[0]
    decoder = place_ref[1] == 1

    @pl.when(decoder)
    def _():
        blocks = [block_rows(block) for block in range(ITEMS)]
        shares = tuple([ref[here, :] for here in blocks] for ref in (q_ref, k_ref, v_ref))
        ((rows, lines),) = attend_groups([shares + (joined([causal_tile()] * ITEMS),)], bias_ref)
        for here, part, line in zip(blocks, rows, lines):
            out_ref[here, :] = part
            lse_ref[0, :, here] = line

    @pl.when(jnp.logical_not(decoder))
    def _():
        here = pl.ds(pl.multiple_of(place * ENC_MIN, ENC_MIN), ENC_MOST)
        groups = [
            ([q_ref[here, :]], [k_ref[here, :]], [v_ref[here, :]], None),
            tuple([gather_short(ref, place)] for ref in (q_ref, k_ref, v_ref)) + (short_tile(),),
        ]
        ((rows, lines),) = attend_groups(groups[:1], bias_ref)
        out_ref[here, :] = rows[0]
        lse_ref[0, :, :ENC_MOST] = lines[0]
        ((short_rows, short_lines),) = attend_groups(groups[1:], bias_ref)
        scatter_short(out_ref, place, short_rows[0])
        lse_ref[0, :, ENC_MOST:] = short_lines[0]


def self_attend_back_kernel(
    place_ref, q_ref, k_ref, v_ref, dc_ref, lse_ref, line_ref,
    dq_ref, dk_ref, dv_ref, dline_ref, bias_ref, dbias_ref,
):
    for head in range(2):
        bias_ref[head] = skew(line_ref[0, head : head + 1, :], BLOCK)
    dbias_ref[...] = jnp.zeros(dbias_ref.shape, F32)
    place = place_ref[0]
    decoder = place_ref[1] == 1
    outs = (dq_ref, dk_ref, dv_ref)

    @pl.when(decoder)
    def _():
        blocks = [block_rows(block) for block in range(ITEMS)]
        shares = tuple([ref[here, :] for here in blocks] for ref in (q_ref, k_ref, v_ref))
        shares += (
            joined([causal_tile()] * ITEMS),
            [dc_ref[here, :] for here in blocks],
            [lse_ref[0, :, here] for here in blocks],
        )
        (grads,) = attend_groups_back([shares], bias_ref, dbias_ref)
        for ref, rows in zip(outs, grads):
            for here, part in zip(blocks, rows):
                ref[here, :] = part

    @pl.when(jnp.logical_not(decoder))
    def _():
        here = pl.ds(pl.multiple_of(place * ENC_MIN, ENC_MIN), ENC_MOST)
        groups = [
            (
                [q_ref[here, :]],
                [k_ref[here, :]],
                [v_ref[here, :]],
                None,
                [dc_ref[here, :]],
                [lse_ref[0, :, :ENC_MOST]],
            ),
            (
                [gather_short(q_ref, place)],
                [gather_short(k_ref, place)],
                [gather_short(v_ref, place)],
                short_tile(),
                [gather_short(dc_ref, place)],
                [lse_ref[0, :, ENC_MOST:]],
            ),
        ]
        grads, short_grads = attend_groups_back(groups, bias_ref, dbias_ref)
        for ref, rows, short_rows in zip(outs, grads, short_grads):
            ref[here, :] = rows[0]
            scatter_short(ref, place, short_rows[0])

    for head in range(2):
        dline_ref[0, head : head + 1, :] = unskew(dbias_ref[head])


def cross_places(place):
    long_pair = (
        pl.ds(pl.multiple_of(place * BLOCK, BLOCK), BLOCK),
        pl.ds(pl.multiple_of(place * ENC_MIN, ENC_MIN), ENC_MOST),
    )
    pairs = []
    for item in range(ITEMS - 1):
        start, number = short_places(place, item)
        pairs.append(
            (pl.ds(pl.multiple_of(number * BLOCK, BLOCK), BLOCK), pl.ds(start, ENC_MIN))
        )
    return [[long_pair], pairs]


def cross_attend_kernel(place_ref, q_ref, k_ref, v_ref, out_ref, lse_ref):
    places = cross_places(place_ref[0])
    groups = [
        (
            [q_ref[here, :] for here, there in pairs],
            [k_ref[there, :] for here, there in pairs],
            [v_ref[there, :] for here, there in pairs],
            None,
        )
        for pairs in places
    ]
    number = 0
    for pairs, (rows, lines) in zip(places, attend_groups(groups, None)):
        for (here, there), part, line in zip(pairs, rows, lines):
            out_ref[here, :] = part
            lse_ref[0, :, block_rows(number)] = line
            number += 1


def cross_attend_back_kernel(
    place_ref, q_ref, k_ref, v_ref, dc_ref, lse_ref, dq_ref, dk_ref, dv_ref
):
    places = cross_places(place_ref[0])
    lines = [lse_ref[0, :, block_rows(number)] for number in range(ITEMS)]
    groups = [
        (
            [q_ref[here, :] for here, there in pairs],
            [k_ref[there, :] for here, there in pairs],
            [v_ref[there, :] for here, there in pairs],
            None,
            [dc_ref[here, :] for here, there in pairs],
            part,
        )
        for pairs, part in zip(places, (lines[:1], lines[1:]))
    ]
    for pairs, grads in zip(places, attend_groups_back(groups, None, None)):
        for number, (here, there) in enumerate(pairs):
            dq_ref[here, :] = grads[0][number]
            dk_ref[there, :] = grads[1][number]
            dv_ref[there, :] = grads[2][number]


def pair_spec(rows, first):
    return pl.BlockSpec((rows, 2 * HD), lambda pair, places: (0, first + pair))


def flat_spec(first, *shape):
    return pl.BlockSpec((1,) + shape, lambda pair, places: (first + pair, 0, 0))


def pair_call(kernel, places, operands, specs, out_specs, out_shape, scratch, work, pairs=PAIRS):
    rows = ITEMS * BLOCK
    share = rows * rows * D * pairs // PAIRS
    return pl.pallas_call(
        kernel,
        grid_spec=pltpu.PrefetchScalarGridSpec(
            num_scalar_prefetch=1,
            grid=(pairs,),
            in_specs=specs,
            out_specs=out_specs,
            scratch_shapes=scratch,
        ),
        out_shape=out_shape,
        compiler_params=pltpu.CompilerParams(vmem_limit_bytes=VMEM_LIMIT),
        cost_estimate=pl.CostEstimate(
            flops=work * share, bytes_accessed=16 * rows * D, transcendentals=share // HD
        ),
        name=kernel.__name__,
    )(places, *operands)


def attend(query, keys, values, places, lines):
    rows = query[0].shape[0]
    operands = [part[0] for part in (query, keys, values)]
    specs = [pair_spec(rows, part[1]) for part in (query, keys, values)]
    scratch = []
    if lines is not None:
        operands.append(lines)
        specs.append(flat_spec(0, 2, LINE))
        scratch.append(pltpu.VMEM((2, BLOCK, LINE), F32))
    return pair_call(
        cross_attend_kernel if lines is None else self_attend_kernel,
        places,
        operands,
        specs,
        [pair_spec(rows, 0), flat_spec(0, 2, rows)],
        [
            jax.ShapeDtypeStruct((rows, D), BF16),
            jax.ShapeDtypeStruct((PAIRS, 2, rows), F32),
        ],
        scratch,
        4,
    )


def attend_back(query, keys, values, grad_context, lse, places, lines, first=0, pairs=PAIRS):
    rows = query[0].shape[0]
    operands = [part[0] for part in (query, keys, values)] + [grad_context, lse]
    specs = [pair_spec(rows, part[1] + first) for part in (query, keys, values)]
    specs += [pair_spec(rows, first), flat_spec(first, 2, rows)]
    out_specs = [pair_spec(rows, 0)] * 3
    out_shape = [jax.ShapeDtypeStruct((rows, pairs * 2 * HD), BF16)] * 3
    scratch = []
    if lines is not None:
        operands.append(lines)
        specs.append(flat_spec(first, 2, LINE))
        out_specs.append(flat_spec(0, 2, LINE))
        out_shape.append(jax.ShapeDtypeStruct((pairs, 2, LINE), F32))
        scratch += [pltpu.VMEM((2, BLOCK, LINE), F32)] * 2
    return pair_call(
        cross_attend_back_kernel if lines is None else self_attend_back_kernel,
        places,
        operands,
        specs,
        out_specs,
        out_shape,
        scratch,
        10,
        pairs,
    )


def exchange(rows, experts):
    parts = rows.reshape(experts, -1, rows.shape[-1])
    return lax.all_to_all(parts, "expert", split_axis=0, concat_axis=0, tiled=True).reshape(
        rows.shape
    )


def gelu_parts(value):
    square = value * value
    bend = jnp.tanh(value * (GELU_SCALE + GELU_SCALE * GELU_CUBE * square))
    half = 0.5 + 0.5 * bend
    slope = half + value * (half * (1.0 - bend)) * (
        GELU_SCALE + 3.0 * GELU_SCALE * GELU_CUBE * square
    )
    return value * half, slope


def row_blocks(rows):
    step = rows // 2
    return [slice(first, first + step) for first in range(0, rows, step)]


def expert_forward_kernel(x_ref, gate_ref, up_ref, down_ref, out_ref, total_ref):
    @pl.when(pl.program_id(0) == 0)
    def _():
        total_ref[...] = jnp.zeros(total_ref.shape, F32)

    for here in row_blocks(x_ref.shape[0]):
        rows = x_ref[here, :]
        value, _ = gelu_parts(dot(rows, gate_ref[...]))
        active = (value * dot(rows, up_ref[...])).astype(BF16)
        total_ref[here, :] += dot(active, down_ref[...])

    @pl.when(pl.program_id(0) == pl.num_programs(0) - 1)
    def _():
        out_ref[...] = total_ref[...].astype(BF16)


def hidden_grads(rows, grad_rows, gate_ref, up_ref, down_ref):
    gate = dot(rows, gate_ref[...])
    up = dot(rows, up_ref[...])
    grad_active = dot_nt(grad_rows, down_ref[...])
    value, slope = gelu_parts(gate)
    grad_gate = (grad_active * (up * slope)).astype(BF16)
    grad_up = (grad_active * value).astype(BF16)
    return value * up, grad_active, grad_gate, grad_up


def expert_both_kernel(
    x_ref, g_ref, gate_ref, up_ref, down_ref, dx_ref, active_ref, line_ref, dx_total, line_total
):
    @pl.when(pl.program_id(0) == 0)
    def _():
        dx_total[...] = jnp.zeros(dx_total.shape, F32)
        line_total[...] = jnp.zeros(line_total.shape, F32)

    for here in row_blocks(x_ref.shape[0]):
        active, grad_active, grad_gate, grad_up = hidden_grads(
            x_ref[here, :], g_ref[here, :], gate_ref, up_ref, down_ref
        )
        dx_total[here, :] += dot_nt(grad_gate, gate_ref[...]) + dot_nt(grad_up, up_ref[...])
        active_ref[here, :] = active.astype(BF16)
        product = active * grad_active
        line_total[here, :] += sum(
            product[:, first : first + 128] for first in range(0, product.shape[1], 128)
        )

    @pl.when(pl.program_id(0) == pl.num_programs(0) - 1)
    def _():
        dx_ref[...] = dx_total[...].astype(BF16)
        line_ref[...] = jnp.sum(line_total[...], axis=1, keepdims=True)


def expert_back_kernel(flags_ref, *refs, count):
    one_ref, two_ref, three_ref, scale_ref, gate_ref, up_ref, down_ref = refs[:7]
    dx_ref, x_ref, g_ref, active_ref, keep_ref, send_ref, dx_total, sems = refs[-8:]
    decoder = flags_ref[0] == 1
    first_group = flags_ref[1] == 0
    most = x_ref.shape[1]
    spare = slice(count, most)

    def load(rows, grads):
        copies = [
            pltpu.make_async_copy(rows, x_ref.at[0, pl.ds(0, count)], sems.at[0]),
            pltpu.make_async_copy(grads, g_ref.at[0, pl.ds(0, count)], sems.at[1]),
        ]
        for copy in copies:
            copy.start()
        for copy in copies:
            copy.wait()

    @pl.when(pl.program_id(0) == 0)
    def _():
        dx_total[...] = jnp.zeros(dx_total.shape, F32)

        @pl.when(decoder)
        def _():
            load(two_ref, one_ref)

        @pl.when(jnp.logical_not(decoder))
        def _():
            load(one_ref, three_ref)

        grads = g_ref[0, :count, :].astype(F32) * scale_ref[...]
        g_ref[0, :count, :] = grads.astype(BF16)
        if count < most:
            x_ref[0, spare, :] = jnp.zeros((most - count, D), BF16)
            g_ref[0, spare, :] = jnp.zeros((most - count, D), BF16)

    for here in row_blocks(count):
        active, _, grad_gate, grad_up = hidden_grads(
            x_ref[0, here, :], g_ref[0, here, :], gate_ref, up_ref, down_ref
        )
        dx_total[here, :] += dot_nt(grad_gate, gate_ref[...]) + dot_nt(grad_up, up_ref[...])
        active_ref[0, here, :] = active.astype(BF16)
        keep_ref[0, here, :] = jnp.where(first_group, grad_gate, grad_up)
        send_ref[0, here, :] = jnp.where(first_group, grad_up, grad_gate)
    if count < most:
        for ref in (active_ref, keep_ref, send_ref):
            ref[0, spare, :] = jnp.zeros((most - count, FF_TILE), BF16)

    @pl.when(pl.program_id(0) == pl.num_programs(0) - 1)
    def _():
        dx_ref[...] = dx_total[...].astype(BF16)


def expert_specs(rows):
    tiles = FF // FF_TILE
    whole = pl.BlockSpec((rows, D), lambda tile, *_: (0, 0))
    weight_specs = [
        pl.BlockSpec((D, FF_TILE), lambda tile, *_: (0, tile)),
        pl.BlockSpec((D, FF_TILE), lambda tile, *_: (0, tiles + tile)),
        pl.BlockSpec((FF_TILE, D), lambda tile, *_: (tile, 0)),
    ]
    return whole, weight_specs, tiles


def expert_cost(rows, products):
    return pl.CostEstimate(
        flops=2 * products * rows * D * FF, bytes_accessed=6 * D * FF, transcendentals=rows * FF
    )


def expert_forward(arrived, expert_first, expert_second):
    rows = arrived.shape[0]
    whole, weight_specs, tiles = expert_specs(rows)
    return pl.pallas_call(
        expert_forward_kernel,
        grid=(tiles,),
        in_specs=[whole] + weight_specs,
        out_specs=whole,
        out_shape=jax.ShapeDtypeStruct((rows, D), BF16),
        scratch_shapes=[pltpu.VMEM((rows, D), F32)],
        compiler_params=pltpu.CompilerParams(vmem_limit_bytes=VMEM_LIMIT),
        cost_estimate=expert_cost(rows, 3),
        name="expert_forward",
    )(arrived, expert_first, expert_first, expert_second)


def expert_both(arrived, grad_rows, expert_first, expert_second):
    rows = arrived.shape[0]
    whole, weight_specs, tiles = expert_specs(rows)
    row_shape = jax.ShapeDtypeStruct((rows, D), BF16)
    total = pltpu.VMEM((rows, D), F32)
    return pl.pallas_call(
        expert_both_kernel,
        grid=(tiles,),
        in_specs=[whole, whole] + weight_specs,
        out_specs=[
            whole,
            pl.BlockSpec((rows, FF_TILE), lambda tile: (0, tile)),
            pl.BlockSpec((rows, 1), lambda tile: (0, 0)),
        ],
        out_shape=[
            row_shape,
            jax.ShapeDtypeStruct((rows, FF), BF16),
            jax.ShapeDtypeStruct((rows, 1), F32),
        ],
        scratch_shapes=[total, pltpu.VMEM((rows, 128), F32)],
        compiler_params=pltpu.CompilerParams(vmem_limit_bytes=VMEM_LIMIT),
        cost_estimate=expert_cost(rows, 5),
        name="expert_both",
    )(arrived, grad_rows, expert_first, expert_first, expert_second)


def expert_back(flags, one, two, three, scale, expert_first, expert_second, kept, number, most):
    rows = one.shape[0]
    whole, weight_specs, tiles = expert_specs(rows)
    part = pl.BlockSpec((1, most, D), lambda tile, *_: (number, 0, 0))
    strip = pl.BlockSpec((1, most, FF_TILE), lambda tile, *_: (number, 0, tile))
    kept_shapes = [jax.ShapeDtypeStruct((2, most, D), BF16)] * 2
    kept_shapes += [jax.ShapeDtypeStruct((2, most, FF), BF16)] * 3
    anywhere = pl.BlockSpec(memory_space=pl.ANY)
    in_specs = [anywhere] * 3 + [pl.BlockSpec((rows, 1), lambda tile, *_: (0, 0))] + weight_specs
    operands = [one, two, three, scale, expert_first, expert_first, expert_second]
    aliases = {}
    if kept is not None:
        aliases = {1 + len(operands) + place: 1 + place for place in range(len(kept))}
        in_specs += [anywhere] * len(kept)
        operands += kept
    dx, *kept = pl.pallas_call(
        partial(expert_back_kernel, count=rows),
        grid_spec=pltpu.PrefetchScalarGridSpec(
            num_scalar_prefetch=1,
            grid=(tiles,),
            in_specs=in_specs,
            out_specs=[whole, part, part, strip, strip, strip],
            scratch_shapes=[pltpu.VMEM((rows, D), F32), pltpu.SemaphoreType.DMA((2,))],
        ),
        out_shape=[jax.ShapeDtypeStruct((rows, D), BF16)] + kept_shapes,
        input_output_aliases=aliases,
        compiler_params=pltpu.CompilerParams(vmem_limit_bytes=VMEM_LIMIT),
        cost_estimate=expert_cost(rows, 5),
        name="expert_back",
    )(flags, *operands)
    return dx, list(kept)


def gate_pair(normed, router_weight, picked_first, picked_second):
    logits = jnp.dot(normed, router_weight, precision=HIGHEST)
    first = jnp.sum(logits * picked_first, axis=1, keepdims=True)
    second = jnp.sum(logits * picked_second, axis=1, keepdims=True)
    return jax.nn.sigmoid(first - second), jax.nn.sigmoid(second - first)


def group_parts(rows, group):
    half = rows.shape[0] // 2
    sent = lax.dynamic_slice_in_dim(rows, (1 - group) * half, half, 0)
    kept = lax.dynamic_slice_in_dim(rows, group * half, half, 0)
    return kept, lax.ppermute(sent, "group", SWAP)


def group_swap(rows, group):
    kept, got = group_parts(rows, group)
    return kept + got


def shard_rows(grad):
    rows, columns = grad.shape
    parts = grad.astype(BF16).reshape(2, lax.axis_size("expert"), -1, columns)
    return jnp.swapaxes(parts, 0, 1).reshape(rows, columns)


def expert_scatter(rows):
    return lax.psum_scatter(rows, "expert", scatter_dimension=0, tiled=True)


def expert_gather(rows):
    return lax.all_gather(rows, "expert", axis=0, tiled=True)


def widen_kernel(part_ref, *refs):
    refs[-1][...] = part_ref[...].astype(F32)


def interleave(part, place, whole=None):
    rows = part.shape[0]
    half = D // 2
    operands = [part] if whole is None else [part, whole]
    specs = [pl.BlockSpec((rows, half), lambda step: (0, step))]
    if whole is not None:
        specs.append(pl.BlockSpec(memory_space=pl.ANY))
    return pl.pallas_call(
        widen_kernel,
        grid=(3,),
        in_specs=specs,
        out_specs=pl.BlockSpec((rows, half), lambda step: (0, 2 * step + place)),
        out_shape=jax.ShapeDtypeStruct((rows, 3 * D), F32),
        input_output_aliases={} if whole is None else {1: 0},
        compiler_params=pltpu.CompilerParams(vmem_limit_bytes=VMEM_LIMIT),
        cost_estimate=pl.CostEstimate(flops=0, bytes_accessed=9 * rows * D, transcendentals=0),
        name="interleave",
    )(*operands)


def add_pieces_kernel(kept_ref, *refs, spans):
    step = pl.program_id(0)
    for piece_ref, (first, last) in zip(refs[:-1], spans):

        @pl.when((step >= first) & (step < last))
        def _():
            refs[-1][...] = kept_ref[...] + piece_ref[...].astype(F32)


def add_pieces(kept, pieces):
    rows, columns = kept.shape
    spans = []
    specs = [pl.BlockSpec((BLOCK, columns), lambda step: (step, 0))]
    for piece in pieces:
        first = spans[-1][1] if spans else 0
        last = first + piece.shape[0] // BLOCK
        spans.append((first, last))

        def place(step, first=first, last=last):
            return jnp.clip(step - first, 0, last - first - 1), 0

        specs.append(pl.BlockSpec((BLOCK, columns), place))
    return pl.pallas_call(
        partial(add_pieces_kernel, spans=spans),
        grid=(rows // BLOCK,),
        in_specs=specs,
        out_specs=specs[0],
        out_shape=jax.ShapeDtypeStruct((rows, columns), F32),
        compiler_params=pltpu.CompilerParams(vmem_limit_bytes=VMEM_LIMIT),
        cost_estimate=pl.CostEstimate(
            flops=rows * columns, bytes_accessed=10 * rows * columns, transcendentals=0
        ),
        name="add_pieces",
    )(kept, *pieces)


def together(*values):
    return lax.optimization_barrier(values)


def per_device(
    inputs,
    cotangent,
    enc_lengths,
    routes,
    norm_gains,
    rel_bias,
    self_qkv,
    self_out,
    cross_proj,
    cross_value,
    router,
    expert_in,
    expert_out,
):
    decoder = lax.axis_index("half") == 1
    group = lax.axis_index("group")
    start_rows = inputs[0].astype(F32)
    row_count = start_rows.shape[0]
    gain_rows = norm_gains[0]
    bias_table = rel_bias[0]
    qkv_weight = self_qkv[0]
    out_weight = self_out[0]
    proj_weight = cross_proj[0]
    value_weight = cross_value[0]
    router_weight = router[0]
    expert_first = expert_in[0, 0]
    expert_second = expert_out[0, 0]
    routing = routes[0]
    experts = router_weight.shape[1]
    cot = cotangent[0]
    cot_f = cot.astype(F32)

    forward = [(0, 1)]
    backward = [(1, 0)]
    half_rows = D // 2
    both_weights = jnp.concatenate([proj_weight, value_weight], axis=1)
    pieces = [both_weights[first:last] for first, last in ((0, 352), (352, 704), (704, D))]

    long_place = jnp.sum(jnp.arange(ITEMS) * (enc_lengths == ENC_MOST)).astype(jnp.int32)
    places = jnp.stack([long_place, decoder.astype(jnp.int32)])
    offsets = ENC_MOST - np.arange(LINE)
    hits = jnp.where(decoder, bucket_hits(offsets, True), bucket_hits(offsets, False))
    lines = jnp.dot(bias_table, hits.T, precision=HIGHEST).reshape(PAIRS, 2, LINE)

    capacity = 5 * row_count // (2 * experts)
    padded = -(-capacity // 8) * 8
    first_chunk = padded // 16 * 8
    chunk_sizes = (first_chunk, padded - first_chunk)
    picked = [
        (routing[:, k : k + 1] == jnp.arange(experts, dtype=jnp.int32)[None, :]).astype(F32)
        for k in range(2)
    ]
    before = jnp.asarray(np.tril(np.ones((row_count, row_count)), -1), BF16)
    counts = dot(before, jnp.concatenate(picked, axis=1).astype(BF16))
    totals = jnp.sum(picked[0], axis=0, keepdims=True)
    slot_first = jnp.sum(picked[0] * counts[:, :experts], axis=1)
    slot_second = jnp.sum(picked[1] * (counts[:, experts:] + totals), axis=1)
    code_first = routing[:, 0] * padded + slot_first.astype(jnp.int32)
    code_second = routing[:, 1] * padded + slot_second.astype(jnp.int32)
    chunk_codes = []
    offset = 0
    for size in chunk_sizes:
        chunk_codes.append(
            (np.arange(experts)[:, None] * padded + offset + np.arange(size)[None, :])
            .reshape(-1)
            .astype(np.int32)
        )
        offset += size

    def spread(first_values, second_values):
        buffers = []
        for codes in chunk_codes:
            hit_first = (codes[:, None] == code_first[None, :]).astype(BF16)
            hit_second = (codes[:, None] == code_second[None, :]).astype(BF16)
            if first_values is second_values:
                buffers.append(dot(hit_first + hit_second, first_values).astype(BF16))
            else:
                buffers.append(
                    (dot(hit_first, first_values) + dot(hit_second, second_values)).astype(BF16)
                )
        return buffers

    def collect(buffers, code, first=0):
        total = None
        for codes, buffer in zip(chunk_codes[first:], buffers):
            part = dot((code[:, None] == codes[None, :]).astype(BF16), buffer)
            total = part if total is None else total + part
        return total

    normed_in = rms_norm(start_rows, gain_rows[0]).astype(BF16)
    project = dot(normed_in, qkv_weight).astype(BF16)
    query, keys, values = (project, 0), (project, PAIRS), (project, 2 * PAIRS)
    context, lse = attend(query, keys, values, places, lines)
    first_half = start_rows + dot(context, out_weight)
    normed_half = rms_norm(first_half, gain_rows[1])
    rounded_half = normed_half.astype(BF16)

    first_rows = jnp.where(decoder, cot, rounded_half)
    sent = spread(first_rows, first_rows)
    arrived_one = [exchange(part, experts) for part in sent]
    returned_one = []
    for k in range(2):
        part, piece = together(arrived_one[k], pieces[k])
        part = expert_forward(part, expert_first, expert_second)
        part, pieces[k] = together(part, lax.ppermute(piece, "half", forward))
        if k == 1:
            part, pieces[2] = together(part, pieces[2])
        returned_one.append(exchange(part, experts))
    returned_one[1], pieces[2] = together(
        returned_one[1], lax.ppermute(pieces[2], "half", forward)
    )
    both_weights = jnp.concatenate(pieces)
    memory_proj, memory_value = both_weights[:, :D], both_weights[:, D:]
    enc_gates = gate_pair(normed_half, router_weight, *picked)
    enc_first = collect(returned_one, code_first)
    enc_second = collect(returned_one, code_second)
    encoded = first_half + enc_gates[0] * enc_first + enc_gates[1] * enc_second
    memory = rms_norm(encoded, gain_rows[2]).astype(BF16)
    memory_in = lax.ppermute(memory, "half", forward)

    cross_query = dot(rounded_half, proj_weight).astype(BF16)
    memory_both = dot(memory_in, both_weights).astype(BF16)
    memory_keys, memory_values = (memory_both, 0), (memory_both, PAIRS)
    cross_context, cross_lse = attend(
        (cross_query, 0), memory_keys, memory_values, places, None
    )
    second_half = first_half + dot(cross_context, value_weight)
    normed_second = rms_norm(second_half, gain_rows[2])
    dec_gates = gate_pair(normed_second, router_weight, *picked)

    rounded_second = normed_second.astype(BF16)
    arrived_two = [exchange(part, experts) for part in spread(rounded_second, rounded_second)]
    all_codes = np.concatenate(chunk_codes)
    gate_rows = jnp.sum(
        jnp.where(all_codes[:, None] == code_first[None, :], dec_gates[0][:, 0][None, :], 0.0)
        + jnp.where(all_codes[:, None] == code_second[None, :], dec_gates[1][:, 0][None, :], 0.0),
        axis=1,
    )
    edge = experts * chunk_sizes[0]

    def exchange_lines(lines):
        parts = []
        for line in lines:
            parts += [line[:edge].reshape(experts, -1), line[edge:].reshape(experts, -1)]
        moved = lax.all_gather(jnp.concatenate(parts, axis=1), "expert", axis=0)
        moved = lax.dynamic_index_in_dim(moved, lax.axis_index("expert"), 1, keepdims=False)
        results = []
        first = 0
        for _ in lines:
            halves = []
            for size in chunk_sizes:
                halves.append(moved[:, first : first + size].reshape(-1))
                first += size
            results.append(jnp.concatenate(halves))
        return results

    actives_two = []
    returned_two = []
    gate_grads = []
    for part, grad_part in zip(arrived_two, arrived_one):
        grad_arrived, active, line = expert_both(part, grad_part, expert_first, expert_second)
        gate_grads.append(line[:, 0])
        actives_two.append(active)
        returned_two.append(exchange(grad_arrived, experts))
    first_parts, line_grads = together(
        [collect(returned_two[:1], code) for code in (code_first, code_second)],
        jnp.concatenate(gate_grads),
    )
    line_grads, arrived_gates = exchange_lines([line_grads, gate_rows])

    def collect_line(line, code):
        return jnp.sum(
            jnp.where(code[:, None] == all_codes[None, :], line[None, :], 0.0), axis=1, keepdims=True
        )

    def router_back(gates, grad_first, grad_second):
        pulled = gates[0] * gates[1] * (grad_first - grad_second)
        grad_logits = pulled * (picked[0] - picked[1])
        return grad_logits, jnp.dot(grad_logits, router_weight.T, precision=HIGHEST)

    dec_logits, dec_normed = router_back(
        dec_gates, collect_line(line_grads, code_first), collect_line(line_grads, code_second)
    )
    dec_normed = (
        dec_normed
        + dec_gates[0] * (first_parts[0] + collect(returned_two[1:], code_first, 1))
        + dec_gates[1] * (first_parts[1] + collect(returned_two[1:], code_second, 1))
    )
    pulled_rows, gain_dec_moe = rms_back(dec_normed, second_half, gain_rows[2])
    grad_second_half = cot_f + pulled_rows

    rounded_grad = grad_second_half.astype(BF16)
    grad_cross_context = dot_nt(rounded_grad, value_weight).astype(BF16)
    grad_cross_query, grad_memory_keys, grad_memory_values = attend_back(
        (cross_query, 0),
        memory_keys,
        memory_values,
        grad_cross_context,
        cross_lse,
        places,
        None,
    )
    key_part = dot_nt(grad_memory_keys, memory_proj)
    value_part, key_part = together(dot_nt(grad_memory_values, memory_value), key_part)
    grad_memory, actives_two = together((key_part + value_part).astype(BF16), actives_two)
    produced_two = [dot(active, expert_second).astype(BF16) for active in actives_two]
    grad_memory, grad_memory_keys, grad_memory_values, produced_two = together(
        lax.ppermute(grad_memory, "half", backward),
        grad_memory_keys,
        grad_memory_values,
        produced_two,
    )
    back_keys = lax.ppermute(grad_memory_keys, "half", backward)
    grad_memory = grad_memory.astype(F32)
    pulled_rows, gain_cross = rms_back(
        dot_nt(grad_cross_query, proj_weight), first_half, gain_rows[1]
    )
    grad_first_dec = grad_second_half + pulled_rows

    pulled_rows, gain_memory = rms_back(grad_memory, encoded, gain_rows[2])
    grad_encoded = cot_f + pulled_rows
    grad_gate_first = jnp.sum(grad_encoded * enc_first, axis=1, keepdims=True)
    grad_gate_second = jnp.sum(grad_encoded * enc_second, axis=1, keepdims=True)
    sent = spread(
        (enc_gates[0] * grad_encoded).astype(BF16), (enc_gates[1] * grad_encoded).astype(BF16)
    )
    normed_sharded = jnp.swapaxes(
        normed_in.reshape(row_count, 2, lax.axis_size("expert"), -1), 1, 2
    ).reshape(row_count, D)
    back_keys, grad_memory_values = together(back_keys, grad_memory_values)
    back_values = lax.ppermute(grad_memory_values, "half", backward)
    grad_proj = dot_tn(
        jnp.where(decoder, rounded_half, memory), jnp.where(decoder, grad_cross_query, back_keys)
    ).astype(BF16)
    sent = [jnp.where(decoder, produced, part) for produced, part in zip(produced_two, sent)]
    sent[1], normed_sharded, grad_proj = together(sent[1], normed_sharded, grad_proj)
    early = [group_parts(grad_proj, group)]
    arrived_three = [exchange(part, experts) for part in sent]
    flags = jnp.stack([decoder.astype(jnp.int32), group])
    scales = jnp.where(decoder, arrived_gates, 1.0)[:, None]
    most = max(part.shape[0] for part in arrived_one)
    kept = None
    returned_three = []
    for k, scale in enumerate((scales[:edge], scales[edge:])):
        grad_arrived, kept = expert_back(
            flags,
            arrived_one[k],
            arrived_two[k],
            arrived_three[k],
            scale,
            expert_first,
            expert_second,
            kept,
            k,
            most,
        )
        if k == 0:
            grad_arrived, back_values, early = together(grad_arrived, back_values, early)
            arrived_three[1], back_values = together(arrived_three[1], back_values)
            grad_value = dot_tn(
                jnp.where(decoder, cross_context, memory),
                jnp.where(decoder, rounded_grad, back_values),
            )
            early.append(group_parts(grad_value.astype(BF16), group))
        else:
            grad_arrived, early, kept, returned_three[0], arrived_three = together(
                grad_arrived, early, kept, returned_three[0], arrived_three
            )
        returned_three.append(exchange(grad_arrived, experts))

    expert_rows, expert_grad_rows, actives, keep_halves, send_halves = [
        part.reshape(2 * most, -1) for part in kept
    ]
    first_group = group == 0
    half_ff = FF // 2
    in_cuts = (0, 256, 512, 640, 768, 896, D)
    out_cuts = (0, 256, 512, half_ff)

    def cut(values, cuts):
        return [[values[first:last]] for first, last in zip(cuts[:-1], cuts[1:])]

    first_in = dot_tn(expert_rows[:, : in_cuts[1]], send_halves).astype(BF16)
    rest_in = dot_tn(expert_rows[:, in_cuts[1] :], send_halves).astype(BF16)
    sends = [[first_in]] + cut(rest_in, [place - in_cuts[1] for place in in_cuts[1:]])

    def swapped(parts):
        return [lax.ppermute(part, "group", SWAP) for part in parts]

    gots = [swapped(sends[0])]
    early = jnp.concatenate([mine + other for mine, other in early], axis=1)
    early = with_layout_constraint(early, Layout((0, 1)))
    returned_three[1], sends, gots, early = together(returned_three[1], sends, gots, early)
    early = expert_scatter(early)

    enc_logits, enc_normed = router_back(enc_gates, grad_gate_first, grad_gate_second)
    enc_normed = enc_normed + collect(returned_three, code_first) + collect(returned_three, code_second)
    pulled_rows, gain_enc_moe = rms_back(enc_normed, first_half, gain_rows[1])
    grad_first = jnp.where(decoder, grad_first_dec, grad_encoded + pulled_rows)

    rounded_grad = grad_first.astype(BF16)
    grad_context = dot_nt(rounded_grad, out_weight).astype(BF16)
    gots.append(swapped(sends[1]))
    halves = [
        attend_back(query, keys, values, grad_context, lse, places, lines, 0, PAIRS // 2)
    ]
    halves[0], gots, sends[2], early, grad_context = together(
        halves[0], gots, sends[2], early, grad_context
    )
    early = expert_gather(early)
    gots.append(swapped(sends[2]))
    halves.append(
        attend_back(query, keys, values, grad_context, lse, places, lines, PAIRS // 2, PAIRS // 2)
    )
    halves, gots, kept, arrived_three = together(
        halves, gots, (actives, expert_grad_rows), arrived_three
    )
    late_first = dot_tn(normed_sharded, jnp.concatenate(halves[0][:3], axis=1))
    late_first, halves, sends[3], kept, rounded_grad, early = together(
        late_first.astype(BF16), halves, sends[3], kept, rounded_grad, early
    )
    late_first = expert_scatter(late_first)
    gots.append(swapped(sends[3]))
    grad_project = jnp.concatenate(
        [half[part] for part in range(3) for half in halves], axis=1
    )
    grad_lines = jnp.concatenate([half[3] for half in halves])

    grad_table = jnp.dot(grad_lines.reshape(H, LINE), hits, precision=HIGHEST)
    grad_router = lax.dot_general(
        jnp.where(decoder, normed_second, normed_half),
        jnp.where(decoder, dec_logits, enc_logits),
        (((0,), (0,)), ((), ())),
        precision=HIGHEST,
    )
    grad_normed = dot_nt(grad_project, qkv_weight)
    grad_normed, gots, sends[4] = together(grad_normed, gots, sends[4])
    gots.append(swapped(sends[4]))
    pulled_rows, gain_self = rms_back(grad_normed, start_rows, gain_rows[0])
    grad_starts = grad_first + pulled_rows
    gain_grads = jnp.stack(
        [
            gain_self,
            jnp.where(decoder, gain_cross, gain_enc_moe),
            jnp.where(decoder, gain_dec_moe, gain_memory),
        ]
    )
    table_rows = jnp.pad(grad_table.reshape(2, -1), ((0, 0), (0, (D - H * NBKT) // 2)))
    small = jnp.concatenate([grad_router, gain_grads.T, table_rows.reshape(D, 1)], axis=1)
    small = jnp.pad(small, ((0, 0), (0, 128 - small.shape[1])))
    late_second = jnp.concatenate(
        [
            dot_tn(normed_sharded, jnp.concatenate(halves[1][:3], axis=1)).astype(BF16),
            shard_rows(small),
            shard_rows(dot_tn(context, rounded_grad)),
        ],
        axis=1,
    )
    late_second = expert_scatter(late_second)
    keep_in = dot_tn(expert_rows, keep_halves)
    keep_in, gots, late_first, sends[5], kept = together(keep_in, gots, late_first, sends[5], kept)
    gots.append(swapped(sends[5]))
    actives, expert_grad_rows = kept
    send_out = dot_tn(
        jnp.where(first_group, actives[:, half_ff:], actives[:, :half_ff]), expert_grad_rows
    ).astype(BF16)
    out_sends = cut(send_out, out_cuts)
    out_sends, gots, late_first, kept = together(out_sends, gots, late_first, kept)
    late_first = group_swap(late_first, group)
    grad_expert_in = add_pieces(keep_in, [part[0] for part in gots])
    grad_expert_in, late_first, out_sends, kept = together(
        grad_expert_in, late_first, out_sends, kept
    )
    late_first = expert_gather(late_first)
    out_gots = [swapped(out_sends[0])]
    actives, expert_grad_rows = kept
    keep_out = dot_tn(
        jnp.where(first_group, actives[:, :half_ff], actives[:, half_ff:]), expert_grad_rows
    )
    keep_out, out_gots, out_sends = together(keep_out, out_gots, out_sends)
    out_gots.append(swapped(out_sends[1]))
    late_second, out_gots, out_sends, arrived_three = together(
        late_second, out_gots, out_sends, arrived_three
    )
    late_second = group_swap(late_second, group)
    late_second, out_sends, arrived_three = together(late_second, out_sends, arrived_three)
    late_second = expert_gather(late_second)
    out_gots.append(swapped(out_sends[2]))
    decoded = (
        second_half
        + dec_gates[0] * collect(arrived_three, code_first)
        + dec_gates[1] * collect(arrived_three, code_second)
    )
    result = jnp.where(decoder, decoded, encoded)

    result = result.astype(BF16)
    grad_expert_out = add_pieces(keep_out, [part[0] for part in out_gots])
    small = late_second[:, 3 * D // 2 : 3 * D // 2 + 128].astype(F32)
    small_table = small[: H * NBKT // 2, experts + 3].reshape(H // 2, NBKT)
    return (
        result[None],
        grad_starts.astype(BF16)[None],
        small[:, experts : experts + 3].T[None],
        small_table[None],
        interleave(late_second, 1, interleave(late_first, 0))[None],
        late_second[:, 3 * D // 2 + 128 :].astype(F32)[None],
        early[:, :D].astype(F32)[None],
        early[:, D:].astype(F32)[None],
        small[:, :experts][None],
        grad_expert_in[None, None],
        grad_expert_out[None, None],
    )


def solution(mesh):
    in_specs = (
        P("half", ("expert", "group"), None),
        P("half", ("expert", "group"), None),
        P(("expert", "group")),
        P("half", ("expert", "group"), None),
        P("half", None, None),
        P("half", None, None),
        P("half", None, None),
        P("half", None, None),
        P("half", None, None),
        P("half", None, None),
        P("half", None, None),
        P("half", "expert", None, None),
        P("half", "expert", None, None),
    )
    out_specs = (
        P("half", ("expert", "group"), None),
        P("half", ("expert", "group"), None),
        P("half", None, "group"),
        P("half", "group", None),
        P("half", "group", None),
        P("half", "group", None),
        P("half", "group", None),
        P("half", "group", None),
        P("half", "group", None),
        P("half", "expert", None, "group"),
        P("half", "expert", "group", None),
    )
    return jax.shard_map(
        per_device, mesh=mesh, in_specs=in_specs, out_specs=out_specs, check_vma=False
    )
```

```python
from functools import partial

import jax
import jax.numpy as jnp
import numpy as np
from jax import lax
from jax.experimental import pallas as pl
from jax.experimental.layout import Layout, with_layout_constraint
from jax.experimental.pallas import tpu as pltpu
from jax.sharding import PartitionSpec as P

D = 1024
H = 16
HD = 64
FF = 2816
NBKT = 32
DEC_SLOT = 128
DEC_LEN = 114
ENC_MOST = 512
ENC_MIN = 32
ITEMS = 5

EPSILON = 1e-06
MASKED = -1e30
HIGHEST = lax.Precision.HIGHEST
BLOCK = 128
PAIRS = H // 2
DIAGONAL = ENC_MOST // BLOCK - 1
LINE = 2 * ENC_MOST
FF_TILE = 256
CROSS_WIDE = 2
SELF_WIDE = 2
F32 = jnp.float32
BF16 = jnp.bfloat16
GELU_SCALE = float(np.sqrt(2.0 / np.pi))
GELU_CUBE = 0.044715
SWAP = ((0, 1), (1, 0))
VMEM_LIMIT = 60 * 1024 * 1024


def bucket_limits(exact_range, growth, divisions):
    limits = []
    for number in range(1, divisions):
        candidate = exact_range
        while candidate**divisions < exact_range**divisions * growth**number:
            candidate = candidate + 1
        limits.append(candidate)
    return limits


def rel_buckets(offset, causal):
    if causal:
        behind = np.maximum(-offset, 0)
        return np.minimum(behind, 16) + sum(
            (behind >= threshold).astype(np.int32) for threshold in bucket_limits(16, 8, 16)
        )
    distance = np.abs(offset)
    return (
        (offset > 0).astype(np.int32) * 16
        + np.minimum(distance, 8)
        + sum((distance >= threshold).astype(np.int32) for threshold in bucket_limits(8, 16, 8))
    )


def bucket_hits(offset, causal):
    return (rel_buckets(offset, causal)[:, None] == np.arange(NBKT)[None, :]).astype(np.float32)


def inverse_rms(values):
    return lax.rsqrt(jnp.mean(values * values, axis=-1, keepdims=True) + EPSILON)


def rms_norm(values, gain_vec):
    return values * inverse_rms(values) * gain_vec


def rms_back(grad_normed, values, gain_vec):
    scale = inverse_rms(values)
    unit = values * scale
    pulled = grad_normed * gain_vec
    grad_values = scale * (pulled - unit * jnp.mean(pulled * unit, axis=-1, keepdims=True))
    return grad_values, jnp.sum(grad_normed * unit, axis=0)


def dot(a, b):
    return jnp.dot(a, b, preferred_element_type=F32)


def dot_nt(a, b):
    return lax.dot_general(a, b, (((1,), (1,)), ((), ())), preferred_element_type=F32)


def dot_tn(a, b):
    return lax.dot_general(a, b, (((0,), (0,)), ((), ())), preferred_element_type=F32)


def skew(line, rows):
    width = line.shape[1]
    tile = jnp.broadcast_to(line, (8, width))
    row = lax.broadcasted_iota(jnp.int32, (8, width), 0)
    for step in (1, 2, 4):
        tile = jnp.where((row & step) != 0, pltpu.roll(tile, step, 1), tile)
    return jnp.concatenate(
        [pltpu.roll(tile, width - rows + first, 1) for first in range(0, rows, 8)], axis=0
    )


def unskew(total):
    rows, width = total.shape
    summed = None
    for first in range(0, rows, 8):
        moved = pltpu.roll(total[first : first + 8], rows - first, 1)
        summed = moved if summed is None else summed + moved
    row = lax.broadcasted_iota(jnp.int32, (8, width), 0)
    for step in (1, 2, 4):
        summed = jnp.where((row & step) != 0, pltpu.roll(summed, width - step, 1), summed)
    return jnp.sum(summed, axis=0, keepdims=True)


def own_lanes(head):
    return (lax.broadcasted_iota(jnp.int32, (1, 2 * HD), 1) // HD) == head


def head_lanes(head, value):
    return jnp.where(own_lanes(head), value, 0.0).astype(BF16)


def tile_places(keys, queries):
    key = lax.broadcasted_iota(jnp.int32, (keys, queries), 0)
    query = lax.broadcasted_iota(jnp.int32, (keys, queries), 1)
    return key, query


def causal_tile():
    key, query = tile_places(BLOCK, BLOCK)
    return (key <= query) & (key < DEC_LEN)


def short_tile():
    key, query = tile_places(BLOCK, BLOCK)
    return (key // ENC_MIN) == (query // ENC_MIN)


def bias_tiles(rows, queries, shares):
    return [
        (
            slice(block * BLOCK, (block + 1) * BLOCK),
            slice((DIAGONAL - block % (rows // BLOCK // shares)) * BLOCK, None),
            queries,
        )
        for block in range(rows // BLOCK)
    ]


def add_bias(scores, bias_ref, head, shares):
    rows, queries = scores.shape
    return joined(
        [
            scores[here] + bias_ref[head, :, lanes.start : lanes.start + queries]
            for here, lanes, queries in bias_tiles(rows, queries, shares)
        ]
    )


def add_bias_grad(dbias_ref, head, grad_scores, shares):
    rows, queries = grad_scores.shape
    sums = {}
    for here, lanes, queries in bias_tiles(rows, queries, shares):
        part = grad_scores[here]
        sums[lanes.start] = sums[lanes.start] + part if lanes.start in sums else part
    for first, part in sums.items():
        dbias_ref[head, :, first : first + queries] += part


def masked(scores, mask):
    return scores if mask is None else jnp.where(mask, scores, MASKED)


def key_parts(rows, shares):
    step = rows.shape[0] // shares
    return [rows[first : first + step] for first in range(0, rows.shape[0], step)]


def spread_max(values, shares):
    return [jnp.max(part, axis=0, keepdims=True) for part in key_parts(values, shares)]


def joined(parts):
    return parts[0] if len(parts) == 1 else jnp.concatenate(parts, axis=0)


def per_share(lines, rows):
    step = rows // len(lines)
    if len(lines) == 1:
        return lines[0]
    return jnp.concatenate(
        [jnp.broadcast_to(line, (step, line.shape[1])) for line in lines], axis=0
    )


def attend_groups(groups, bias_ref):
    units = [(group, head) for group in groups for head in range(2)]
    scores = []
    for (queries, keys, values, mask), head in units:
        scale = head_lanes(head, HD**-0.5)
        part = joined([dot_nt(key, query * scale) for query, key in zip(queries, keys)])
        scores.append(part)
    contexts = []
    log_sums = []
    for ((queries, keys, values, mask), head), part in zip(units, scores):
        shares = len(queries)
        if bias_ref is not None:
            part = add_bias(part, bias_ref, head, shares)
        part = masked(part, mask)
        highest = spread_max(part, shares)
        exponent = jnp.exp(part - per_share(highest, part.shape[0]))
        totals = [jnp.sum(rows, axis=0, keepdims=True) for rows in key_parts(exponent, shares)]
        log_sums.append([top + jnp.log(total) for top, total in zip(highest, totals)])
        rounded = key_parts(exponent.astype(BF16), shares)
        contexts.append(
            [
                dot_tn(rows, jnp.where(own_lanes(head), value, jnp.ones_like(value)))
                for rows, value in zip(rounded, values)
            ]
        )
    results = []
    for number in range(len(groups)):
        rows = []
        lines = []
        for share in range(len(groups[number][0])):
            first, second = contexts[2 * number][share], contexts[2 * number + 1][share]
            sums = jnp.where(own_lanes(0), second, first)
            context = jnp.where(own_lanes(0), first, second) / pltpu.roll(sums, HD, 1)
            rows.append(context.astype(BF16))
            lines.append(
                jnp.concatenate(
                    [log_sums[2 * number][share], log_sums[2 * number + 1][share]], axis=0
                )
            )
        results.append((rows, lines))
    return results


def attend_groups_back(groups, bias_ref, dbias_ref):
    units = [(group, head) for group in groups for head in range(2)]
    scores = []
    pulls = []
    for (queries, keys, values, mask, grads, lines), head in units:
        scale = head_lanes(head, HD**-0.5)
        own = head_lanes(head, 1.0)
        scores.append(joined([dot_nt(key, query * scale) for query, key in zip(queries, keys)]))
        pulls.append(joined([dot_nt(value, grad * own) for value, grad in zip(values, grads)]))
    totals = []
    for ((queries, keys, values, mask, grads, lines), head), part, pull in zip(units, scores, pulls):
        shares = len(queries)
        scale = head_lanes(head, HD**-0.5)
        own = head_lanes(head, 1.0)
        if bias_ref is not None:
            part = add_bias(part, bias_ref, head, shares)
        part = masked(part, mask)
        weights = jnp.exp(part - per_share([line[head : head + 1] for line in lines], part.shape[0]))
        product = weights * pull
        inner = [jnp.sum(rows, axis=0, keepdims=True) for rows in key_parts(product, shares)]
        grad_scores = product - weights * per_share(inner, part.shape[0])
        if dbias_ref is not None:
            add_bias_grad(dbias_ref, head, grad_scores, shares)
        rounded = key_parts(grad_scores.astype(BF16), shares)
        weights = key_parts(weights.astype(BF16), shares)
        totals.append(
            [
                [dot_tn(rows, key * scale) for rows, key in zip(rounded, keys)],
                [dot(rows, query * scale) for rows, query in zip(rounded, queries)],
                [dot(rows, grad * own) for rows, grad in zip(weights, grads)],
            ]
        )
    results = []
    for number in range(len(groups)):
        results.append(
            [
                [(one + two).astype(BF16) for one, two in zip(first, second)]
                for first, second in zip(totals[2 * number], totals[2 * number + 1])
            ]
        )
    return results


def short_places(place, item):
    later = (item >= place).astype(jnp.int32)
    return pl.multiple_of(item * ENC_MIN + later * ENC_MOST, ENC_MIN), item + later


def gather_short(ref, place, lanes):
    return jnp.concatenate(
        [ref[pl.ds(short_places(place, item)[0], ENC_MIN), lanes] for item in range(ITEMS - 1)],
        axis=0,
    )


def scatter_short(ref, place, rows, lanes):
    for item in range(ITEMS - 1):
        ref[pl.ds(short_places(place, item)[0], ENC_MIN), lanes] = rows[
            item * ENC_MIN : (item + 1) * ENC_MIN
        ]


def block_rows(block):
    return slice(block * BLOCK, (block + 1) * BLOCK)


def self_attend_kernel(place_ref, q_ref, k_ref, v_ref, line_ref, out_ref, lse_ref, bias_ref):
    pairs = range(q_ref.shape[1] // (2 * HD))
    for pair in pairs:
        for head in range(2):
            bias_ref[pair, head] = skew(line_ref[pair, head : head + 1, :], BLOCK)
    place = place_ref[0]
    decoder = place_ref[1] == 1

    @pl.when(decoder)
    def _():
        blocks = [block_rows(block) for block in range(ITEMS)]
        for pair in pairs:
            lanes = pair_lanes(pair)
            shares = tuple([ref[here, lanes] for here in blocks] for ref in (q_ref, k_ref, v_ref))
            mask = joined([causal_tile()] * ITEMS)
            ((rows, lines),) = attend_groups([shares + (mask,)], bias_ref.at[pair])
            for here, part, line in zip(blocks, rows, lines):
                out_ref[here, lanes] = part
                lse_ref[pair, :, here] = line

    @pl.when(jnp.logical_not(decoder))
    def _():
        here = pl.ds(pl.multiple_of(place * ENC_MIN, ENC_MIN), ENC_MOST)
        for pair in pairs:
            lanes = pair_lanes(pair)
            group = tuple([ref[here, lanes]] for ref in (q_ref, k_ref, v_ref)) + (None,)
            ((rows, lines),) = attend_groups([group], bias_ref.at[pair])
            out_ref[here, lanes] = rows[0]
            lse_ref[pair, :, :ENC_MOST] = lines[0]
        for pair in pairs:
            lanes = pair_lanes(pair)
            group = tuple([gather_short(ref, place, lanes)] for ref in (q_ref, k_ref, v_ref))
            ((rows, lines),) = attend_groups([group + (short_tile(),)], bias_ref.at[pair])
            scatter_short(out_ref, place, rows[0], lanes)
            lse_ref[pair, :, ENC_MOST:] = lines[0]


def self_attend_back_kernel(
    place_ref, q_ref, k_ref, v_ref, dc_ref, lse_ref, line_ref,
    dq_ref, dk_ref, dv_ref, dline_ref, bias_ref, dbias_ref,
):
    pairs = range(q_ref.shape[1] // (2 * HD))
    for pair in pairs:
        for head in range(2):
            bias_ref[pair, head] = skew(line_ref[pair, head : head + 1, :], BLOCK)
    dbias_ref[...] = jnp.zeros(dbias_ref.shape, F32)
    place = place_ref[0]
    decoder = place_ref[1] == 1
    ins = (q_ref, k_ref, v_ref)
    outs = (dq_ref, dk_ref, dv_ref)

    @pl.when(decoder)
    def _():
        blocks = [block_rows(block) for block in range(ITEMS)]
        for pair in pairs:
            lanes = pair_lanes(pair)
            shares = tuple([ref[here, lanes] for here in blocks] for ref in ins)
            shares += (
                joined([causal_tile()] * ITEMS),
                [dc_ref[here, lanes] for here in blocks],
                [lse_ref[pair, :, here] for here in blocks],
            )
            (grads,) = attend_groups_back([shares], bias_ref.at[pair], dbias_ref.at[pair])
            for ref, rows in zip(outs, grads):
                for here, part in zip(blocks, rows):
                    ref[here, lanes] = part

    @pl.when(jnp.logical_not(decoder))
    def _():
        here = pl.ds(pl.multiple_of(place * ENC_MIN, ENC_MIN), ENC_MOST)
        for pair in pairs:
            lanes = pair_lanes(pair)
            groups = [
                tuple([ref[here, lanes]] for ref in ins)
                + (None, [dc_ref[here, lanes]], [lse_ref[pair, :, :ENC_MOST]]),
                tuple([gather_short(ref, place, lanes)] for ref in ins)
                + (
                    short_tile(),
                    [gather_short(dc_ref, place, lanes)],
                    [lse_ref[pair, :, ENC_MOST:]],
                ),
            ]
            grads, short_grads = attend_groups_back(
                groups, bias_ref.at[pair], dbias_ref.at[pair]
            )
            for ref, rows, short_rows in zip(outs, grads, short_grads):
                ref[here, lanes] = rows[0]
                scatter_short(ref, place, short_rows[0], lanes)

    for pair in pairs:
        for head in range(2):
            dline_ref[pair, head : head + 1, :] = unskew(dbias_ref[pair, head])


def cross_places(place):
    long_pair = (
        pl.ds(pl.multiple_of(place * BLOCK, BLOCK), BLOCK),
        pl.ds(pl.multiple_of(place * ENC_MIN, ENC_MIN), ENC_MOST),
    )
    pairs = []
    for item in range(ITEMS - 1):
        start, number = short_places(place, item)
        pairs.append(
            (pl.ds(pl.multiple_of(number * BLOCK, BLOCK), BLOCK), pl.ds(start, ENC_MIN))
        )
    return [[long_pair], pairs]


def pair_lanes(pair):
    return slice(pair * 2 * HD, (pair + 1) * 2 * HD)


def cross_attend_kernel(place_ref, q_ref, k_ref, v_ref, out_ref, lse_ref):
    places = cross_places(place_ref[0])
    pairs = [(pair, spots) for pair in range(q_ref.shape[1] // (2 * HD)) for spots in places]
    groups = [
        (
            [q_ref[here, pair_lanes(pair)] for here, there in spots],
            [k_ref[there, pair_lanes(pair)] for here, there in spots],
            [v_ref[there, pair_lanes(pair)] for here, there in spots],
            None,
        )
        for pair, spots in pairs
    ]
    number = 0
    for (pair, spots), (rows, lines) in zip(pairs, attend_groups(groups, None)):
        for (here, there), part, line in zip(spots, rows, lines):
            out_ref[here, pair_lanes(pair)] = part
            lse_ref[pair, :, block_rows(number % ITEMS)] = line
            number += 1


def cross_attend_back_kernel(
    place_ref, q_ref, k_ref, v_ref, dc_ref, lse_ref, dq_ref, dk_ref, dv_ref
):
    places = cross_places(place_ref[0])
    pairs = [(pair, spots) for pair in range(q_ref.shape[1] // (2 * HD)) for spots in places]
    groups = []
    number = 0
    for pair, spots in pairs:
        lanes = pair_lanes(pair)
        lines = []
        for _ in spots:
            lines.append(lse_ref[pair, :, block_rows(number % ITEMS)])
            number += 1
        groups.append(
            (
                [q_ref[here, lanes] for here, there in spots],
                [k_ref[there, lanes] for here, there in spots],
                [v_ref[there, lanes] for here, there in spots],
                None,
                [dc_ref[here, lanes] for here, there in spots],
                lines,
            )
        )
    for (pair, spots), grads in zip(pairs, attend_groups_back(groups, None, None)):
        for number, (here, there) in enumerate(spots):
            dq_ref[here, pair_lanes(pair)] = grads[0][number]
            dk_ref[there, pair_lanes(pair)] = grads[1][number]
            dv_ref[there, pair_lanes(pair)] = grads[2][number]


def pair_spec(rows, first, wide):
    return pl.BlockSpec((rows, wide * 2 * HD), lambda step, places: (0, first // wide + step))


def flat_spec(first, wide, *shape):
    return pl.BlockSpec((wide,) + shape, lambda step, places: (first // wide + step, 0, 0))


def pair_call(kernel, places, operands, specs, out_specs, out_shape, scratch, work, pairs, wide):
    rows = ITEMS * BLOCK
    share = rows * rows * D * pairs // PAIRS
    return pl.pallas_call(
        kernel,
        grid_spec=pltpu.PrefetchScalarGridSpec(
            num_scalar_prefetch=1,
            grid=(pairs // wide,),
            in_specs=specs,
            out_specs=out_specs,
            scratch_shapes=scratch,
        ),
        out_shape=out_shape,
        compiler_params=pltpu.CompilerParams(vmem_limit_bytes=VMEM_LIMIT),
        cost_estimate=pl.CostEstimate(
            flops=work * share, bytes_accessed=16 * rows * D, transcendentals=share // HD
        ),
        name=kernel.__name__,
    )(places, *operands)


def attend(query, keys, values, places, lines):
    rows = query[0].shape[0]
    wide = SELF_WIDE if lines is not None else CROSS_WIDE
    operands = [part[0] for part in (query, keys, values)]
    specs = [pair_spec(rows, part[1], wide) for part in (query, keys, values)]
    scratch = []
    if lines is not None:
        operands.append(lines)
        specs.append(flat_spec(0, wide, 2, LINE))
        scratch.append(pltpu.VMEM((wide, 2, BLOCK, LINE), F32))
    return pair_call(
        cross_attend_kernel if lines is None else self_attend_kernel,
        places,
        operands,
        specs,
        [pair_spec(rows, 0, wide), flat_spec(0, wide, 2, rows)],
        [
            jax.ShapeDtypeStruct((rows, D), BF16),
            jax.ShapeDtypeStruct((PAIRS, 2, rows), F32),
        ],
        scratch,
        4,
        PAIRS,
        wide,
    )


def attend_back(query, keys, values, grad_context, lse, places, lines, first=0, pairs=PAIRS):
    rows = query[0].shape[0]
    wide = SELF_WIDE if lines is not None else CROSS_WIDE
    operands = [part[0] for part in (query, keys, values)] + [grad_context, lse]
    specs = [pair_spec(rows, part[1] + first, wide) for part in (query, keys, values)]
    specs += [pair_spec(rows, first, wide), flat_spec(first, wide, 2, rows)]
    out_specs = [pair_spec(rows, 0, wide)] * 3
    out_shape = [jax.ShapeDtypeStruct((rows, pairs * 2 * HD), BF16)] * 3
    scratch = []
    if lines is not None:
        operands.append(lines)
        specs.append(flat_spec(first, wide, 2, LINE))
        out_specs.append(flat_spec(0, wide, 2, LINE))
        out_shape.append(jax.ShapeDtypeStruct((pairs, 2, LINE), F32))
        scratch += [pltpu.VMEM((wide, 2, BLOCK, LINE), F32)] * 2
    return pair_call(
        cross_attend_back_kernel if lines is None else self_attend_back_kernel,
        places,
        operands,
        specs,
        out_specs,
        out_shape,
        scratch,
        10,
        pairs,
        wide,
    )


def exchange(rows, experts):
    parts = rows.reshape(experts, -1, rows.shape[-1])
    return lax.all_to_all(parts, "expert", split_axis=0, concat_axis=0, tiled=True).reshape(
        rows.shape
    )


def gelu_parts(value):
    square = value * value
    bend = jnp.tanh(value * (GELU_SCALE + GELU_SCALE * GELU_CUBE * square))
    half = 0.5 + 0.5 * bend
    slope = half + value * (half * (1.0 - bend)) * (
        GELU_SCALE + 3.0 * GELU_SCALE * GELU_CUBE * square
    )
    return value * half, slope


def row_blocks(rows):
    step = rows // 2
    return [slice(first, first + step) for first in range(0, rows, step)]


def expert_forward_kernel(x_ref, gate_ref, up_ref, down_ref, out_ref, total_ref):
    @pl.when(pl.program_id(0) == 0)
    def _():
        total_ref[...] = jnp.zeros(total_ref.shape, F32)

    for here in row_blocks(x_ref.shape[0]):
        rows = x_ref[here, :]
        value, _ = gelu_parts(dot(rows, gate_ref[...]))
        active = (value * dot(rows, up_ref[...])).astype(BF16)
        total_ref[here, :] += dot(active, down_ref[...])

    @pl.when(pl.program_id(0) == pl.num_programs(0) - 1)
    def _():
        out_ref[...] = total_ref[...].astype(BF16)


def hidden_grads(rows, grad_rows, gate_ref, up_ref, down_ref):
    gate = dot(rows, gate_ref[...])
    up = dot(rows, up_ref[...])
    grad_active = dot_nt(grad_rows, down_ref[...])
    value, slope = gelu_parts(gate)
    grad_gate = (grad_active * (up * slope)).astype(BF16)
    grad_up = (grad_active * value).astype(BF16)
    return value * up, grad_active, grad_gate, grad_up


def expert_both_kernel(
    x_ref, g_ref, gate_ref, up_ref, down_ref, dx_ref, active_ref, line_ref, dx_total, line_total
):
    @pl.when(pl.program_id(0) == 0)
    def _():
        dx_total[...] = jnp.zeros(dx_total.shape, F32)
        line_total[...] = jnp.zeros(line_total.shape, F32)

    for here in row_blocks(x_ref.shape[0]):
        active, grad_active, grad_gate, grad_up = hidden_grads(
            x_ref[here, :], g_ref[here, :], gate_ref, up_ref, down_ref
        )
        dx_total[here, :] += dot_nt(grad_gate, gate_ref[...]) + dot_nt(grad_up, up_ref[...])
        active_ref[here, :] = active.astype(BF16)
        product = active * grad_active
        line_total[here, :] += sum(
            product[:, first : first + 128] for first in range(0, product.shape[1], 128)
        )

    @pl.when(pl.program_id(0) == pl.num_programs(0) - 1)
    def _():
        dx_ref[...] = dx_total[...].astype(BF16)
        line_ref[...] = jnp.sum(line_total[...], axis=1, keepdims=True)


def expert_back_kernel(flags_ref, *refs, count):
    one_ref, two_ref, three_ref, scale_ref, gate_ref, up_ref, down_ref = refs[:7]
    dx_ref, x_ref, g_ref, active_ref, keep_ref, send_ref, dx_total, sems = refs[-8:]
    decoder = flags_ref[0] == 1
    first_group = flags_ref[1] == 0
    most = x_ref.shape[1]
    spare = slice(count, most)

    def load(rows, grads):
        copies = [
            pltpu.make_async_copy(rows, x_ref.at[0, pl.ds(0, count)], sems.at[0]),
            pltpu.make_async_copy(grads, g_ref.at[0, pl.ds(0, count)], sems.at[1]),
        ]
        for copy in copies:
            copy.start()
        for copy in copies:
            copy.wait()

    @pl.when(pl.program_id(0) == 0)
    def _():
        dx_total[...] = jnp.zeros(dx_total.shape, F32)

        @pl.when(decoder)
        def _():
            load(two_ref, one_ref)

        @pl.when(jnp.logical_not(decoder))
        def _():
            load(one_ref, three_ref)

        grads = g_ref[0, :count, :].astype(F32) * scale_ref[...]
        g_ref[0, :count, :] = grads.astype(BF16)
        if count < most:
            x_ref[0, spare, :] = jnp.zeros((most - count, D), BF16)
            g_ref[0, spare, :] = jnp.zeros((most - count, D), BF16)

    for here in row_blocks(count):
        active, _, grad_gate, grad_up = hidden_grads(
            x_ref[0, here, :], g_ref[0, here, :], gate_ref, up_ref, down_ref
        )
        dx_total[here, :] += dot_nt(grad_gate, gate_ref[...]) + dot_nt(grad_up, up_ref[...])
        active_ref[0, here, :] = active.astype(BF16)
        keep_ref[0, here, :] = jnp.where(first_group, grad_gate, grad_up)
        send_ref[0, here, :] = jnp.where(first_group, grad_up, grad_gate)
    if count < most:
        for ref in (active_ref, keep_ref, send_ref):
            ref[0, spare, :] = jnp.zeros((most - count, FF_TILE), BF16)

    @pl.when(pl.program_id(0) == pl.num_programs(0) - 1)
    def _():
        dx_ref[...] = dx_total[...].astype(BF16)


def expert_specs(rows):
    tiles = FF // FF_TILE
    whole = pl.BlockSpec((rows, D), lambda tile, *_: (0, 0))
    weight_specs = [
        pl.BlockSpec((D, FF_TILE), lambda tile, *_: (0, tile)),
        pl.BlockSpec((D, FF_TILE), lambda tile, *_: (0, tiles + tile)),
        pl.BlockSpec((FF_TILE, D), lambda tile, *_: (tile, 0)),
    ]
    return whole, weight_specs, tiles


def expert_cost(rows, products):
    return pl.CostEstimate(
        flops=2 * products * rows * D * FF, bytes_accessed=6 * D * FF, transcendentals=rows * FF
    )


def expert_forward(arrived, expert_first, expert_second):
    rows = arrived.shape[0]
    whole, weight_specs, tiles = expert_specs(rows)
    return pl.pallas_call(
        expert_forward_kernel,
        grid=(tiles,),
        in_specs=[whole] + weight_specs,
        out_specs=whole,
        out_shape=jax.ShapeDtypeStruct((rows, D), BF16),
        scratch_shapes=[pltpu.VMEM((rows, D), F32)],
        compiler_params=pltpu.CompilerParams(vmem_limit_bytes=VMEM_LIMIT),
        cost_estimate=expert_cost(rows, 3),
        name="expert_forward",
    )(arrived, expert_first, expert_first, expert_second)


def expert_both(arrived, grad_rows, expert_first, expert_second):
    rows = arrived.shape[0]
    whole, weight_specs, tiles = expert_specs(rows)
    row_shape = jax.ShapeDtypeStruct((rows, D), BF16)
    total = pltpu.VMEM((rows, D), F32)
    return pl.pallas_call(
        expert_both_kernel,
        grid=(tiles,),
        in_specs=[whole, whole] + weight_specs,
        out_specs=[
            whole,
            pl.BlockSpec((rows, FF_TILE), lambda tile: (0, tile)),
            pl.BlockSpec((rows, 1), lambda tile: (0, 0)),
        ],
        out_shape=[
            row_shape,
            jax.ShapeDtypeStruct((rows, FF), BF16),
            jax.ShapeDtypeStruct((rows, 1), F32),
        ],
        scratch_shapes=[total, pltpu.VMEM((rows, 128), F32)],
        compiler_params=pltpu.CompilerParams(vmem_limit_bytes=VMEM_LIMIT),
        cost_estimate=expert_cost(rows, 5),
        name="expert_both",
    )(arrived, grad_rows, expert_first, expert_first, expert_second)


def expert_back(flags, one, two, three, scale, expert_first, expert_second, kept, number, most):
    rows = one.shape[0]
    whole, weight_specs, tiles = expert_specs(rows)
    part = pl.BlockSpec((1, most, D), lambda tile, *_: (number, 0, 0))
    strip = pl.BlockSpec((1, most, FF_TILE), lambda tile, *_: (number, 0, tile))
    kept_shapes = [jax.ShapeDtypeStruct((2, most, D), BF16)] * 2
    kept_shapes += [jax.ShapeDtypeStruct((2, most, FF), BF16)] * 3
    anywhere = pl.BlockSpec(memory_space=pl.ANY)
    in_specs = [anywhere] * 3 + [pl.BlockSpec((rows, 1), lambda tile, *_: (0, 0))] + weight_specs
    operands = [one, two, three, scale, expert_first, expert_first, expert_second]
    aliases = {}
    if kept is not None:
        aliases = {1 + len(operands) + place: 1 + place for place in range(len(kept))}
        in_specs += [anywhere] * len(kept)
        operands += kept
    dx, *kept = pl.pallas_call(
        partial(expert_back_kernel, count=rows),
        grid_spec=pltpu.PrefetchScalarGridSpec(
            num_scalar_prefetch=1,
            grid=(tiles,),
            in_specs=in_specs,
            out_specs=[whole, part, part, strip, strip, strip],
            scratch_shapes=[pltpu.VMEM((rows, D), F32), pltpu.SemaphoreType.DMA((2,))],
        ),
        out_shape=[jax.ShapeDtypeStruct((rows, D), BF16)] + kept_shapes,
        input_output_aliases=aliases,
        compiler_params=pltpu.CompilerParams(vmem_limit_bytes=VMEM_LIMIT),
        cost_estimate=expert_cost(rows, 5),
        name="expert_back",
    )(flags, *operands)
    return dx, list(kept)


def gate_pair(normed, router_weight, picked_first, picked_second):
    logits = jnp.dot(normed, router_weight, precision=HIGHEST)
    first = jnp.sum(logits * picked_first, axis=1, keepdims=True)
    second = jnp.sum(logits * picked_second, axis=1, keepdims=True)
    return jax.nn.sigmoid(first - second), jax.nn.sigmoid(second - first)


def group_halves(rows, group):
    half = rows.shape[0] // 2
    sent = lax.dynamic_slice_in_dim(rows, (1 - group) * half, half, 0)
    kept = lax.dynamic_slice_in_dim(rows, group * half, half, 0)
    return kept, sent


def group_parts(rows, group):
    kept, sent = group_halves(rows, group)
    return kept, lax.ppermute(sent, "group", SWAP)


def group_swap(rows, group):
    kept, got = group_parts(rows, group)
    return kept + got


def shard_rows(grad):
    rows, columns = grad.shape
    parts = grad.astype(BF16).reshape(2, lax.axis_size("expert"), -1, columns)
    return jnp.swapaxes(parts, 0, 1).reshape(rows, columns)


def expert_scatter(rows):
    return lax.psum_scatter(rows, "expert", scatter_dimension=0, tiled=True)


def expert_gather(rows):
    return lax.all_gather(rows, "expert", axis=0, tiled=True)


def widen_kernel(part_ref, *refs):
    refs[-1][...] = part_ref[...].astype(F32)


def interleave(part, place, whole=None):
    rows = part.shape[0]
    half = D // 2
    operands = [part] if whole is None else [part, whole]
    specs = [pl.BlockSpec((rows, half), lambda step: (0, step))]
    if whole is not None:
        specs.append(pl.BlockSpec(memory_space=pl.ANY))
    return pl.pallas_call(
        widen_kernel,
        grid=(3,),
        in_specs=specs,
        out_specs=pl.BlockSpec((rows, half), lambda step: (0, 2 * step + place)),
        out_shape=jax.ShapeDtypeStruct((rows, 3 * D), F32),
        input_output_aliases={} if whole is None else {1: 0},
        compiler_params=pltpu.CompilerParams(vmem_limit_bytes=VMEM_LIMIT),
        cost_estimate=pl.CostEstimate(flops=0, bytes_accessed=9 * rows * D, transcendentals=0),
        name="interleave",
    )(*operands)


def add_pieces_kernel(kept_ref, *refs, spans):
    step = pl.program_id(0)
    for piece_ref, (first, last) in zip(refs[:-1], spans):

        @pl.when((step >= first) & (step < last))
        def _():
            refs[-1][...] = kept_ref[...] + piece_ref[...].astype(F32)


def add_pieces(kept, pieces, block):
    rows, columns = kept.shape
    spans = []
    specs = [pl.BlockSpec((block, columns), lambda step: (step, 0))]
    for piece in pieces:
        first = spans[-1][1] if spans else 0
        last = first + piece.shape[0] // block
        spans.append((first, last))

        def place(step, first=first, last=last):
            return jnp.clip(step - first, 0, last - first - 1), 0

        specs.append(pl.BlockSpec((block, columns), place))
    return pl.pallas_call(
        partial(add_pieces_kernel, spans=spans),
        grid=(rows // block,),
        in_specs=specs,
        out_specs=specs[0],
        out_shape=jax.ShapeDtypeStruct((rows, columns), F32),
        compiler_params=pltpu.CompilerParams(vmem_limit_bytes=VMEM_LIMIT),
        cost_estimate=pl.CostEstimate(
            flops=rows * columns, bytes_accessed=10 * rows * columns, transcendentals=0
        ),
        name="add_pieces",
    )(kept, *pieces)


def together(*values):
    return lax.optimization_barrier(values)


def per_device(
    inputs,
    cotangent,
    enc_lengths,
    routes,
    norm_gains,
    rel_bias,
    self_qkv,
    self_out,
    cross_proj,
    cross_value,
    router,
    expert_in,
    expert_out,
):
    decoder = lax.axis_index("half") == 1
    group = lax.axis_index("group")
    start_rows = inputs[0].astype(F32)
    row_count = start_rows.shape[0]
    gain_rows = norm_gains[0]
    bias_table = rel_bias[0]
    qkv_weight = self_qkv[0]
    out_weight = self_out[0]
    proj_weight = cross_proj[0]
    value_weight = cross_value[0]
    router_weight = router[0]
    expert_first = expert_in[0, 0]
    expert_second = expert_out[0, 0]
    routing = routes[0]
    experts = router_weight.shape[1]
    cot = cotangent[0]
    cot_f = cot.astype(F32)

    forward = [(0, 1)]
    backward = [(1, 0)]
    half_rows = D // 2
    both_weights = jnp.concatenate([proj_weight, value_weight], axis=1)
    pieces = [both_weights[first:last] for first, last in ((0, 352), (352, 704), (704, D))]

    long_place = jnp.sum(jnp.arange(ITEMS) * (enc_lengths == ENC_MOST)).astype(jnp.int32)
    places = jnp.stack([long_place, decoder.astype(jnp.int32)])
    offsets = ENC_MOST - np.arange(LINE)
    hits = jnp.where(decoder, bucket_hits(offsets, True), bucket_hits(offsets, False))
    lines = jnp.dot(bias_table, hits.T, precision=HIGHEST).reshape(PAIRS, 2, LINE)

    capacity = 5 * row_count // (2 * experts)
    padded = -(-capacity // 8) * 8
    first_chunk = padded // 16 * 8
    chunk_sizes = (first_chunk, padded - first_chunk)
    picked = [
        (routing[:, k : k + 1] == jnp.arange(experts, dtype=jnp.int32)[None, :]).astype(F32)
        for k in range(2)
    ]
    before = jnp.asarray(np.tril(np.ones((row_count, row_count)), -1), BF16)
    counts = dot(before, jnp.concatenate(picked, axis=1).astype(BF16))
    totals = jnp.sum(picked[0], axis=0, keepdims=True)
    slot_first = jnp.sum(picked[0] * counts[:, :experts], axis=1)
    slot_second = jnp.sum(picked[1] * (counts[:, experts:] + totals), axis=1)
    code_first = routing[:, 0] * padded + slot_first.astype(jnp.int32)
    code_second = routing[:, 1] * padded + slot_second.astype(jnp.int32)
    chunk_codes = []
    offset = 0
    for size in chunk_sizes:
        chunk_codes.append(
            (np.arange(experts)[:, None] * padded + offset + np.arange(size)[None, :])
            .reshape(-1)
            .astype(np.int32)
        )
        offset += size

    def spread(first_values, second_values):
        buffers = []
        for codes in chunk_codes:
            hit_first = (codes[:, None] == code_first[None, :]).astype(BF16)
            hit_second = (codes[:, None] == code_second[None, :]).astype(BF16)
            if first_values is second_values:
                buffers.append(dot(hit_first + hit_second, first_values).astype(BF16))
            else:
                buffers.append(
                    (dot(hit_first, first_values) + dot(hit_second, second_values)).astype(BF16)
                )
        return buffers

    def collect(buffers, code, first=0):
        total = None
        for codes, buffer in zip(chunk_codes[first:], buffers):
            part = dot((code[:, None] == codes[None, :]).astype(BF16), buffer)
            total = part if total is None else total + part
        return total

    normed_in = rms_norm(start_rows, gain_rows[0]).astype(BF16)
    project = dot(normed_in, qkv_weight).astype(BF16)
    query, keys, values = (project, 0), (project, PAIRS), (project, 2 * PAIRS)
    context, lse = attend(query, keys, values, places, lines)
    first_half = start_rows + dot(context, out_weight)
    normed_half = rms_norm(first_half, gain_rows[1])
    rounded_half = normed_half.astype(BF16)

    first_rows = jnp.where(decoder, cot, rounded_half)
    sent = spread(first_rows, first_rows)
    arrived_one = [exchange(part, experts) for part in sent]
    returned_one = []
    for k in range(2):
        part, piece = together(arrived_one[k], pieces[k])
        part = expert_forward(part, expert_first, expert_second)
        part, pieces[k] = together(part, lax.ppermute(piece, "half", forward))
        if k == 1:
            part, pieces[2] = together(part, pieces[2])
        returned_one.append(exchange(part, experts))
    returned_one[1], pieces[2] = together(
        returned_one[1], lax.ppermute(pieces[2], "half", forward)
    )
    both_weights = jnp.concatenate(pieces)
    memory_proj, memory_value = both_weights[:, :D], both_weights[:, D:]
    enc_gates = gate_pair(normed_half, router_weight, *picked)
    enc_first = collect(returned_one, code_first)
    enc_second = collect(returned_one, code_second)
    encoded = first_half + enc_gates[0] * enc_first + enc_gates[1] * enc_second
    memory = rms_norm(encoded, gain_rows[2]).astype(BF16)
    memory_in = lax.ppermute(memory, "half", forward)

    cross_query = dot(rounded_half, proj_weight).astype(BF16)
    memory_both = dot(memory_in, both_weights).astype(BF16)
    memory_keys, memory_values = (memory_both, 0), (memory_both, PAIRS)
    cross_context, cross_lse = attend(
        (cross_query, 0), memory_keys, memory_values, places, None
    )
    second_half = first_half + dot(cross_context, value_weight)
    normed_second = rms_norm(second_half, gain_rows[2])
    dec_gates = gate_pair(normed_second, router_weight, *picked)

    rounded_second = normed_second.astype(BF16)
    arrived_two = [exchange(part, experts) for part in spread(rounded_second, rounded_second)]
    all_codes = np.concatenate(chunk_codes)
    gate_rows = jnp.sum(
        jnp.where(all_codes[:, None] == code_first[None, :], dec_gates[0][:, 0][None, :], 0.0)
        + jnp.where(all_codes[:, None] == code_second[None, :], dec_gates[1][:, 0][None, :], 0.0),
        axis=1,
    )
    edge = experts * chunk_sizes[0]

    def exchange_lines(lines):
        parts = []
        for line in lines:
            parts += [line[:edge].reshape(experts, -1), line[edge:].reshape(experts, -1)]
        moved = lax.all_gather(jnp.concatenate(parts, axis=1), "expert", axis=0)
        moved = lax.dynamic_index_in_dim(moved, lax.axis_index("expert"), 1, keepdims=False)
        results = []
        first = 0
        for _ in lines:
            halves = []
            for size in chunk_sizes:
                halves.append(moved[:, first : first + size].reshape(-1))
                first += size
            results.append(jnp.concatenate(halves))
        return results

    actives_two = []
    returned_two = []
    gate_grads = []
    for part, grad_part in zip(arrived_two, arrived_one):
        grad_arrived, active, line = expert_both(part, grad_part, expert_first, expert_second)
        gate_grads.append(line[:, 0])
        actives_two.append(active)
        returned_two.append(exchange(grad_arrived, experts))
    first_parts, line_grads = together(
        [collect(returned_two[:1], code) for code in (code_first, code_second)],
        jnp.concatenate(gate_grads),
    )
    line_grads, arrived_gates = exchange_lines([line_grads, gate_rows])

    def collect_line(line, code):
        return jnp.sum(
            jnp.where(code[:, None] == all_codes[None, :], line[None, :], 0.0), axis=1, keepdims=True
        )

    def router_back(gates, grad_first, grad_second):
        pulled = gates[0] * gates[1] * (grad_first - grad_second)
        grad_logits = pulled * (picked[0] - picked[1])
        return grad_logits, jnp.dot(grad_logits, router_weight.T, precision=HIGHEST)

    dec_logits, dec_normed = router_back(
        dec_gates, collect_line(line_grads, code_first), collect_line(line_grads, code_second)
    )
    dec_normed = (
        dec_normed
        + dec_gates[0] * (first_parts[0] + collect(returned_two[1:], code_first, 1))
        + dec_gates[1] * (first_parts[1] + collect(returned_two[1:], code_second, 1))
    )
    pulled_rows, gain_dec_moe = rms_back(dec_normed, second_half, gain_rows[2])
    grad_second_half = cot_f + pulled_rows

    rounded_grad = grad_second_half.astype(BF16)
    grad_cross_context = dot_nt(rounded_grad, value_weight).astype(BF16)
    grad_cross_query, grad_memory_keys, grad_memory_values = attend_back(
        (cross_query, 0),
        memory_keys,
        memory_values,
        grad_cross_context,
        cross_lse,
        places,
        None,
    )
    key_part = dot_nt(grad_memory_keys, memory_proj)
    value_part, key_part = together(dot_nt(grad_memory_values, memory_value), key_part)
    grad_memory, actives_two = together((key_part + value_part).astype(BF16), actives_two)
    produced_two = [dot(active, expert_second).astype(BF16) for active in actives_two]
    grad_memory, grad_memory_keys, grad_memory_values, produced_two = together(
        lax.ppermute(grad_memory, "half", backward),
        grad_memory_keys,
        grad_memory_values,
        produced_two,
    )
    back_keys = lax.ppermute(grad_memory_keys, "half", backward)
    grad_memory = grad_memory.astype(F32)
    pulled_rows, gain_cross = rms_back(
        dot_nt(grad_cross_query, proj_weight), first_half, gain_rows[1]
    )
    grad_first_dec = grad_second_half + pulled_rows

    pulled_rows, gain_memory = rms_back(grad_memory, encoded, gain_rows[2])
    grad_encoded = cot_f + pulled_rows
    grad_gate_first = jnp.sum(grad_encoded * enc_first, axis=1, keepdims=True)
    grad_gate_second = jnp.sum(grad_encoded * enc_second, axis=1, keepdims=True)
    sent = spread(
        (enc_gates[0] * grad_encoded).astype(BF16), (enc_gates[1] * grad_encoded).astype(BF16)
    )
    normed_sharded = jnp.swapaxes(
        normed_in.reshape(row_count, 2, lax.axis_size("expert"), -1), 1, 2
    ).reshape(row_count, D)
    back_keys, grad_memory_values = together(back_keys, grad_memory_values)
    back_values = lax.ppermute(grad_memory_values, "half", backward)
    grad_proj = dot_tn(
        jnp.where(decoder, rounded_half, memory), jnp.where(decoder, grad_cross_query, back_keys)
    ).astype(BF16)
    sent = [jnp.where(decoder, produced, part) for produced, part in zip(produced_two, sent)]
    flags = jnp.stack([decoder.astype(jnp.int32), group])
    scales = jnp.where(decoder, arrived_gates, 1.0)[:, None]
    scales = [scales[:edge], scales[edge:]]
    proj_kept, proj_sent = group_halves(grad_proj, group)
    sent[1], normed_sharded, proj_kept, proj_sent, flags, scales = together(
        sent[1], normed_sharded, proj_kept, proj_sent, flags, scales
    )
    early = [(proj_kept, lax.ppermute(proj_sent, "group", SWAP))]
    arrived_three = [exchange(part, experts) for part in sent]
    most = max(part.shape[0] for part in arrived_one)
    kept = None
    returned_three = []
    for k, scale in enumerate(scales):
        grad_arrived, kept = expert_back(
            flags,
            arrived_one[k],
            arrived_two[k],
            arrived_three[k],
            scale,
            expert_first,
            expert_second,
            kept,
            k,
            most,
        )
        if k == 0:
            grad_arrived, back_values, early = together(grad_arrived, back_values, early)
            arrived_three[1], back_values = together(arrived_three[1], back_values)
            grad_value = dot_tn(
                jnp.where(decoder, cross_context, memory),
                jnp.where(decoder, rounded_grad, back_values),
            )
            early.append(group_parts(grad_value.astype(BF16), group))
        else:
            grad_arrived, early, kept, returned_three[0], arrived_three = together(
                grad_arrived, early, kept, returned_three[0], arrived_three
            )
        returned_three.append(exchange(grad_arrived, experts))

    expert_rows, expert_grad_rows, actives, keep_halves, send_halves = [
        part.reshape(2 * most, -1) for part in kept
    ]
    first_group = group == 0
    half_ff = FF // 2
    in_cuts = (0, 256, 512, 640, 768, 896, D)
    out_cuts = (0, half_ff // 4, half_ff // 2, half_ff)

    def cut(values, cuts):
        return [[values[first:last]] for first, last in zip(cuts[:-1], cuts[1:])]

    first_in = dot_tn(expert_rows[:, : in_cuts[1]], send_halves).astype(BF16)
    rest_in = dot_tn(expert_rows[:, in_cuts[1] :], send_halves).astype(BF16)
    sends = [[first_in]] + cut(rest_in, [place - in_cuts[1] for place in in_cuts[1:]])

    def swapped(parts):
        return [lax.ppermute(part, "group", SWAP) for part in parts]

    gots = [swapped(sends[0])]
    early = jnp.concatenate([mine + other for mine, other in early], axis=1)
    early = with_layout_constraint(early, Layout((0, 1)))
    returned_three[1], sends, gots, early = together(returned_three[1], sends, gots, early)
    early = expert_scatter(early)

    enc_logits, enc_normed = router_back(enc_gates, grad_gate_first, grad_gate_second)
    enc_normed = enc_normed + collect(returned_three, code_first) + collect(returned_three, code_second)
    pulled_rows, gain_enc_moe = rms_back(enc_normed, first_half, gain_rows[1])
    grad_first = jnp.where(decoder, grad_first_dec, grad_encoded + pulled_rows)

    rounded_grad = grad_first.astype(BF16)
    grad_context = dot_nt(rounded_grad, out_weight).astype(BF16)
    gots.append(swapped(sends[1]))
    halves = [
        attend_back(query, keys, values, grad_context, lse, places, lines, 0, PAIRS // 2)
    ]
    halves[0], gots, sends[2], early, grad_context = together(
        halves[0], gots, sends[2], early, grad_context
    )
    early = expert_gather(early)
    gots.append(swapped(sends[2]))
    halves.append(
        attend_back(query, keys, values, grad_context, lse, places, lines, PAIRS // 2, PAIRS // 2)
    )
    halves, gots, kept, arrived_three = together(
        halves, gots, (actives, expert_grad_rows), arrived_three
    )
    late_first = dot_tn(normed_sharded, jnp.concatenate(halves[0][:3], axis=1))
    late_first, halves, sends[3], kept, rounded_grad, early = together(
        late_first.astype(BF16), halves, sends[3], kept, rounded_grad, early
    )
    late_first = expert_scatter(late_first)
    gots.append(swapped(sends[3]))
    grad_project = jnp.concatenate(
        [half[part] for part in range(3) for half in halves], axis=1
    )
    grad_lines = jnp.concatenate([half[3] for half in halves])

    grad_table = jnp.dot(grad_lines.reshape(H, LINE), hits, precision=HIGHEST)
    grad_router = lax.dot_general(
        jnp.where(decoder, normed_second, normed_half),
        jnp.where(decoder, dec_logits, enc_logits),
        (((0,), (0,)), ((), ())),
        precision=HIGHEST,
    )
    grad_normed = dot_nt(grad_project, qkv_weight)
    grad_normed, gots, sends[4] = together(grad_normed, gots, sends[4])
    gots.append(swapped(sends[4]))
    pulled_rows, gain_self = rms_back(grad_normed, start_rows, gain_rows[0])
    grad_starts = grad_first + pulled_rows
    gain_grads = jnp.stack(
        [
            gain_self,
            jnp.where(decoder, gain_cross, gain_enc_moe),
            jnp.where(decoder, gain_dec_moe, gain_memory),
        ]
    )
    table_rows = jnp.pad(grad_table.reshape(2, -1), ((0, 0), (0, (D - H * NBKT) // 2)))
    small = jnp.concatenate([grad_router, gain_grads.T, table_rows.reshape(D, 1)], axis=1)
    small = jnp.pad(small, ((0, 0), (0, 128 - small.shape[1])))
    late_second = jnp.concatenate(
        [
            dot_tn(normed_sharded, jnp.concatenate(halves[1][:3], axis=1)).astype(BF16),
            shard_rows(small),
            shard_rows(dot_tn(context, rounded_grad)),
        ],
        axis=1,
    )
    late_second = expert_scatter(late_second)
    keep_in = dot_tn(expert_rows, keep_halves)
    keep_in, gots, late_first, sends[5], kept = together(keep_in, gots, late_first, sends[5], kept)
    gots.append(swapped(sends[5]))
    actives, expert_grad_rows = kept
    send_out = dot_tn(
        jnp.where(first_group, actives[:, half_ff:], actives[:, :half_ff]), expert_grad_rows
    ).astype(BF16)
    out_sends = cut(send_out, out_cuts)
    out_sends, gots, late_first, kept = together(out_sends, gots, late_first, kept)
    late_first = group_swap(late_first, group)
    grad_expert_in = add_pieces(keep_in, [part[0] for part in gots], BLOCK)
    grad_expert_in, late_first, out_sends, kept = together(
        grad_expert_in, late_first, out_sends, kept
    )
    late_first = expert_gather(late_first)
    out_gots = [swapped(out_sends[0])]
    actives, expert_grad_rows = kept
    keep_out = dot_tn(
        jnp.where(first_group, actives[:, :half_ff], actives[:, half_ff:]), expert_grad_rows
    )
    keep_out, out_gots, out_sends = together(keep_out, out_gots, out_sends)
    out_gots.append(swapped(out_sends[1]))
    late_second, out_gots, out_sends, arrived_three = together(
        late_second, out_gots, out_sends, arrived_three
    )
    late_second = group_swap(late_second, group)
    late_second, out_sends, arrived_three = together(late_second, out_sends, arrived_three)
    late_second = expert_gather(late_second)
    out_gots.append(swapped(out_sends[2]))
    decoded = (
        second_half
        + dec_gates[0] * collect(arrived_three, code_first)
        + dec_gates[1] * collect(arrived_three, code_second)
    )
    result = jnp.where(decoder, decoded, encoded)

    result = result.astype(BF16)
    grad_expert_out = add_pieces(keep_out, [part[0] for part in out_gots], half_ff // 4)
    small = late_second[:, 3 * D // 2 : 3 * D // 2 + 128].astype(F32)
    small_table = small[: H * NBKT // 2, experts + 3].reshape(H // 2, NBKT)
    return (
        result[None],
        grad_starts.astype(BF16)[None],
        small[:, experts : experts + 3].T[None],
        small_table[None],
        interleave(late_second, 1, interleave(late_first, 0))[None],
        late_second[:, 3 * D // 2 + 128 :].astype(F32)[None],
        early[:, :D].astype(F32)[None],
        early[:, D:].astype(F32)[None],
        small[:, :experts][None],
        grad_expert_in[None, None],
        grad_expert_out[None, None],
    )


def solution(mesh):
    in_specs = (
        P("half", ("expert", "group"), None),
        P("half", ("expert", "group"), None),
        P(("expert", "group")),
        P("half", ("expert", "group"), None),
        P("half", None, None),
        P("half", None, None),
        P("half", None, None),
        P("half", None, None),
        P("half", None, None),
        P("half", None, None),
        P("half", None, None),
        P("half", "expert", None, None),
        P("half", "expert", None, None),
    )
    out_specs = (
        P("half", ("expert", "group"), None),
        P("half", ("expert", "group"), None),
        P("half", None, "group"),
        P("half", "group", None),
        P("half", "group", None),
        P("half", "group", None),
        P("half", "group", None),
        P("half", "group", None),
        P("half", "group", None),
        P("half", "expert", None, "group"),
        P("half", "expert", "group", None),
    )
    return jax.shard_map(
        per_device, mesh=mesh, in_specs=in_specs, out_specs=out_specs, check_vma=False
    )
```

```python
from functools import partial

import jax
import jax.numpy as jnp
import numpy as np
from jax import lax
from jax.experimental import pallas as pl
from jax.experimental.layout import Layout, with_layout_constraint
from jax.experimental.pallas import tpu as pltpu
from jax.sharding import PartitionSpec as P

D = 1024
H = 16
HD = 64
FF = 2816
NBKT = 32
DEC_SLOT = 128
DEC_LEN = 114
ENC_MOST = 512
ENC_MIN = 32
ITEMS = 5

EPSILON = 1e-06
MASKED = -1e30
HIGHEST = lax.Precision.HIGHEST
BLOCK = 128
PAIRS = H // 2
DIAGONAL = ENC_MOST // BLOCK - 1
LINE = 2 * ENC_MOST
FF_TILE = 256
CROSS_WIDE = 2
SELF_WIDE = 2
F32 = jnp.float32
BF16 = jnp.bfloat16
GELU_SCALE = float(np.sqrt(2.0 / np.pi))
GELU_CUBE = 0.044715
SWAP = ((0, 1), (1, 0))
VMEM_LIMIT = 60 * 1024 * 1024


def bucket_limits(exact_range, growth, divisions):
    limits = []
    for number in range(1, divisions):
        candidate = exact_range
        while candidate**divisions < exact_range**divisions * growth**number:
            candidate = candidate + 1
        limits.append(candidate)
    return limits


def rel_buckets(offset, causal):
    if causal:
        behind = np.maximum(-offset, 0)
        return np.minimum(behind, 16) + sum(
            (behind >= threshold).astype(np.int32) for threshold in bucket_limits(16, 8, 16)
        )
    distance = np.abs(offset)
    return (
        (offset > 0).astype(np.int32) * 16
        + np.minimum(distance, 8)
        + sum((distance >= threshold).astype(np.int32) for threshold in bucket_limits(8, 16, 8))
    )


def bucket_hits(offset, causal):
    return (rel_buckets(offset, causal)[:, None] == np.arange(NBKT)[None, :]).astype(np.float32)


def inverse_rms(values):
    return lax.rsqrt(jnp.mean(values * values, axis=-1, keepdims=True) + EPSILON)


def rms_norm(values, gain_vec):
    return values * inverse_rms(values) * gain_vec


def rms_back(grad_normed, values, gain_vec):
    scale = inverse_rms(values)
    unit = values * scale
    pulled = grad_normed * gain_vec
    grad_values = scale * (pulled - unit * jnp.mean(pulled * unit, axis=-1, keepdims=True))
    return grad_values, jnp.sum(grad_normed * unit, axis=0)


def dot(a, b):
    return jnp.dot(a, b, preferred_element_type=F32)


def dot_nt(a, b):
    return lax.dot_general(a, b, (((1,), (1,)), ((), ())), preferred_element_type=F32)


def dot_tn(a, b):
    return lax.dot_general(a, b, (((0,), (0,)), ((), ())), preferred_element_type=F32)


def skew(line, rows):
    width = line.shape[1]
    tile = jnp.broadcast_to(line, (8, width))
    row = lax.broadcasted_iota(jnp.int32, (8, width), 0)
    for step in (1, 2, 4):
        tile = jnp.where((row & step) != 0, pltpu.roll(tile, step, 1), tile)
    return jnp.concatenate(
        [pltpu.roll(tile, width - rows + first, 1) for first in range(0, rows, 8)], axis=0
    )


def unskew(total):
    rows, width = total.shape
    summed = None
    for first in range(0, rows, 8):
        moved = pltpu.roll(total[first : first + 8], rows - first, 1)
        summed = moved if summed is None else summed + moved
    row = lax.broadcasted_iota(jnp.int32, (8, width), 0)
    for step in (1, 2, 4):
        summed = jnp.where((row & step) != 0, pltpu.roll(summed, width - step, 1), summed)
    return jnp.sum(summed, axis=0, keepdims=True)


def own_lanes(head):
    return (lax.broadcasted_iota(jnp.int32, (1, 2 * HD), 1) // HD) == head


def head_lanes(head, value):
    return jnp.where(own_lanes(head), value, 0.0).astype(BF16)


def tile_places(keys, queries):
    key = lax.broadcasted_iota(jnp.int32, (keys, queries), 0)
    query = lax.broadcasted_iota(jnp.int32, (keys, queries), 1)
    return key, query


def causal_tile():
    key, query = tile_places(BLOCK, BLOCK)
    return (key <= query) & (key < DEC_LEN)


def short_tile():
    key, query = tile_places(BLOCK, BLOCK)
    return (key // ENC_MIN) == (query // ENC_MIN)


def bias_tiles(rows, queries, shares):
    return [
        (
            slice(block * BLOCK, (block + 1) * BLOCK),
            slice((DIAGONAL - block % (rows // BLOCK // shares)) * BLOCK, None),
            queries,
        )
        for block in range(rows // BLOCK)
    ]


def add_bias(scores, bias_ref, head, shares):
    rows, queries = scores.shape
    return joined(
        [
            scores[here] + bias_ref[head, :, lanes.start : lanes.start + queries]
            for here, lanes, queries in bias_tiles(rows, queries, shares)
        ]
    )


def add_bias_grad(dbias_ref, head, grad_scores, shares):
    rows, queries = grad_scores.shape
    sums = {}
    for here, lanes, queries in bias_tiles(rows, queries, shares):
        part = grad_scores[here]
        sums[lanes.start] = sums[lanes.start] + part if lanes.start in sums else part
    for first, part in sums.items():
        dbias_ref[head, :, first : first + queries] += part


def masked(scores, mask):
    return scores if mask is None else jnp.where(mask, scores, MASKED)


def key_parts(rows, shares):
    step = rows.shape[0] // shares
    return [rows[first : first + step] for first in range(0, rows.shape[0], step)]


def spread_max(values, shares):
    return [jnp.max(part, axis=0, keepdims=True) for part in key_parts(values, shares)]


def joined(parts):
    return parts[0] if len(parts) == 1 else jnp.concatenate(parts, axis=0)


def per_share(lines, rows):
    step = rows // len(lines)
    if len(lines) == 1:
        return lines[0]
    return jnp.concatenate(
        [jnp.broadcast_to(line, (step, line.shape[1])) for line in lines], axis=0
    )


def attend_groups(groups, bias_ref):
    units = [(group, head) for group in groups for head in range(2)]
    scores = []
    for (queries, keys, values, mask), head in units:
        scale = head_lanes(head, HD**-0.5)
        part = joined([dot_nt(key, query * scale) for query, key in zip(queries, keys)])
        scores.append(part)
    contexts = []
    log_sums = []
    for ((queries, keys, values, mask), head), part in zip(units, scores):
        shares = len(queries)
        if bias_ref is not None:
            part = add_bias(part, bias_ref, head, shares)
        part = masked(part, mask)
        highest = spread_max(part, shares)
        exponent = jnp.exp(part - per_share(highest, part.shape[0]))
        totals = [jnp.sum(rows, axis=0, keepdims=True) for rows in key_parts(exponent, shares)]
        log_sums.append([top + jnp.log(total) for top, total in zip(highest, totals)])
        rounded = key_parts(exponent.astype(BF16), shares)
        contexts.append(
            [
                dot_tn(rows, jnp.where(own_lanes(head), value, jnp.ones_like(value)))
                for rows, value in zip(rounded, values)
            ]
        )
    results = []
    for number in range(len(groups)):
        rows = []
        lines = []
        for share in range(len(groups[number][0])):
            first, second = contexts[2 * number][share], contexts[2 * number + 1][share]
            sums = jnp.where(own_lanes(0), second, first)
            context = jnp.where(own_lanes(0), first, second) / pltpu.roll(sums, HD, 1)
            rows.append(context.astype(BF16))
            lines.append(
                jnp.concatenate(
                    [log_sums[2 * number][share], log_sums[2 * number + 1][share]], axis=0
                )
            )
        results.append((rows, lines))
    return results


def attend_groups_back(groups, bias_ref, dbias_ref):
    units = [(group, head) for group in groups for head in range(2)]
    scores = []
    pulls = []
    for (queries, keys, values, mask, grads, lines), head in units:
        scale = head_lanes(head, HD**-0.5)
        own = head_lanes(head, 1.0)
        scores.append(joined([dot_nt(key, query * scale) for query, key in zip(queries, keys)]))
        pulls.append(joined([dot_nt(value, grad * own) for value, grad in zip(values, grads)]))
    totals = []
    for ((queries, keys, values, mask, grads, lines), head), part, pull in zip(units, scores, pulls):
        shares = len(queries)
        scale = head_lanes(head, HD**-0.5)
        own = head_lanes(head, 1.0)
        if bias_ref is not None:
            part = add_bias(part, bias_ref, head, shares)
        part = masked(part, mask)
        weights = jnp.exp(part - per_share([line[head : head + 1] for line in lines], part.shape[0]))
        product = weights * pull
        inner = [jnp.sum(rows, axis=0, keepdims=True) for rows in key_parts(product, shares)]
        grad_scores = product - weights * per_share(inner, part.shape[0])
        if dbias_ref is not None:
            add_bias_grad(dbias_ref, head, grad_scores, shares)
        rounded = key_parts(grad_scores.astype(BF16), shares)
        weights = key_parts(weights.astype(BF16), shares)
        totals.append(
            [
                [dot_tn(rows, key * scale) for rows, key in zip(rounded, keys)],
                [dot(rows, query * scale) for rows, query in zip(rounded, queries)],
                [dot(rows, grad * own) for rows, grad in zip(weights, grads)],
            ]
        )
    results = []
    for number in range(len(groups)):
        results.append(
            [
                [(one + two).astype(BF16) for one, two in zip(first, second)]
                for first, second in zip(totals[2 * number], totals[2 * number + 1])
            ]
        )
    return results


def short_places(place, item):
    later = (item >= place).astype(jnp.int32)
    return pl.multiple_of(item * ENC_MIN + later * ENC_MOST, ENC_MIN), item + later


def gather_short(ref, place, lanes):
    return jnp.concatenate(
        [ref[pl.ds(short_places(place, item)[0], ENC_MIN), lanes] for item in range(ITEMS - 1)],
        axis=0,
    )


def scatter_short(ref, place, rows, lanes):
    for item in range(ITEMS - 1):
        ref[pl.ds(short_places(place, item)[0], ENC_MIN), lanes] = rows[
            item * ENC_MIN : (item + 1) * ENC_MIN
        ]


def block_rows(block):
    return slice(block * BLOCK, (block + 1) * BLOCK)


def self_attend_kernel(place_ref, q_ref, k_ref, v_ref, line_ref, out_ref, lse_ref, bias_ref):
    pairs = range(q_ref.shape[1] // (2 * HD))
    for pair in pairs:
        for head in range(2):
            bias_ref[pair, head] = skew(line_ref[pair, head : head + 1, :], BLOCK)
    place = place_ref[0]
    decoder = place_ref[1] == 1

    @pl.when(decoder)
    def _():
        blocks = [block_rows(block) for block in range(ITEMS)]
        for pair in pairs:
            lanes = pair_lanes(pair)
            shares = tuple([ref[here, lanes] for here in blocks] for ref in (q_ref, k_ref, v_ref))
            mask = joined([causal_tile()] * ITEMS)
            ((rows, lines),) = attend_groups([shares + (mask,)], bias_ref.at[pair])
            for here, part, line in zip(blocks, rows, lines):
                out_ref[here, lanes] = part
                lse_ref[pair, :, here] = line

    @pl.when(jnp.logical_not(decoder))
    def _():
        here = pl.ds(pl.multiple_of(place * ENC_MIN, ENC_MIN), ENC_MOST)
        for pair in pairs:
            lanes = pair_lanes(pair)
            group = tuple([ref[here, lanes]] for ref in (q_ref, k_ref, v_ref)) + (None,)
            ((rows, lines),) = attend_groups([group], bias_ref.at[pair])
            out_ref[here, lanes] = rows[0]
            lse_ref[pair, :, :ENC_MOST] = lines[0]
        for pair in pairs:
            lanes = pair_lanes(pair)
            group = tuple([gather_short(ref, place, lanes)] for ref in (q_ref, k_ref, v_ref))
            ((rows, lines),) = attend_groups([group + (short_tile(),)], bias_ref.at[pair])
            scatter_short(out_ref, place, rows[0], lanes)
            lse_ref[pair, :, ENC_MOST:] = lines[0]


def self_attend_back_kernel(
    place_ref, q_ref, k_ref, v_ref, dc_ref, lse_ref, line_ref,
    dq_ref, dk_ref, dv_ref, dline_ref, bias_ref, dbias_ref,
):
    pairs = range(q_ref.shape[1] // (2 * HD))
    for pair in pairs:
        for head in range(2):
            bias_ref[pair, head] = skew(line_ref[pair, head : head + 1, :], BLOCK)
    dbias_ref[...] = jnp.zeros(dbias_ref.shape, F32)
    place = place_ref[0]
    decoder = place_ref[1] == 1
    ins = (q_ref, k_ref, v_ref)
    outs = (dq_ref, dk_ref, dv_ref)

    @pl.when(decoder)
    def _():
        blocks = [block_rows(block) for block in range(ITEMS)]
        for pair in pairs:
            lanes = pair_lanes(pair)
            shares = tuple([ref[here, lanes] for here in blocks] for ref in ins)
            shares += (
                joined([causal_tile()] * ITEMS),
                [dc_ref[here, lanes] for here in blocks],
                [lse_ref[pair, :, here] for here in blocks],
            )
            (grads,) = attend_groups_back([shares], bias_ref.at[pair], dbias_ref.at[pair])
            for ref, rows in zip(outs, grads):
                for here, part in zip(blocks, rows):
                    ref[here, lanes] = part

    @pl.when(jnp.logical_not(decoder))
    def _():
        here = pl.ds(pl.multiple_of(place * ENC_MIN, ENC_MIN), ENC_MOST)
        for pair in pairs:
            lanes = pair_lanes(pair)
            groups = [
                tuple([ref[here, lanes]] for ref in ins)
                + (None, [dc_ref[here, lanes]], [lse_ref[pair, :, :ENC_MOST]]),
                tuple([gather_short(ref, place, lanes)] for ref in ins)
                + (
                    short_tile(),
                    [gather_short(dc_ref, place, lanes)],
                    [lse_ref[pair, :, ENC_MOST:]],
                ),
            ]
            grads, short_grads = attend_groups_back(
                groups, bias_ref.at[pair], dbias_ref.at[pair]
            )
            for ref, rows, short_rows in zip(outs, grads, short_grads):
                ref[here, lanes] = rows[0]
                scatter_short(ref, place, short_rows[0], lanes)

    for pair in pairs:
        for head in range(2):
            dline_ref[pair, head : head + 1, :] = unskew(dbias_ref[pair, head])


def cross_places(place):
    long_pair = (
        pl.ds(pl.multiple_of(place * BLOCK, BLOCK), BLOCK),
        pl.ds(pl.multiple_of(place * ENC_MIN, ENC_MIN), ENC_MOST),
    )
    pairs = []
    for item in range(ITEMS - 1):
        start, number = short_places(place, item)
        pairs.append(
            (pl.ds(pl.multiple_of(number * BLOCK, BLOCK), BLOCK), pl.ds(start, ENC_MIN))
        )
    return [[long_pair], pairs]


def pair_lanes(pair):
    return slice(pair * 2 * HD, (pair + 1) * 2 * HD)


def cross_attend_kernel(place_ref, q_ref, k_ref, v_ref, out_ref, lse_ref):
    places = cross_places(place_ref[0])
    pairs = [(pair, spots) for pair in range(q_ref.shape[1] // (2 * HD)) for spots in places]
    groups = [
        (
            [q_ref[here, pair_lanes(pair)] for here, there in spots],
            [k_ref[there, pair_lanes(pair)] for here, there in spots],
            [v_ref[there, pair_lanes(pair)] for here, there in spots],
            None,
        )
        for pair, spots in pairs
    ]
    number = 0
    for (pair, spots), (rows, lines) in zip(pairs, attend_groups(groups, None)):
        for (here, there), part, line in zip(spots, rows, lines):
            out_ref[here, pair_lanes(pair)] = part
            lse_ref[pair, :, block_rows(number % ITEMS)] = line
            number += 1


def cross_attend_back_kernel(
    place_ref, q_ref, k_ref, v_ref, dc_ref, lse_ref, dq_ref, dk_ref, dv_ref
):
    places = cross_places(place_ref[0])
    pairs = [(pair, spots) for pair in range(q_ref.shape[1] // (2 * HD)) for spots in places]
    groups = []
    number = 0
    for pair, spots in pairs:
        lanes = pair_lanes(pair)
        lines = []
        for _ in spots:
            lines.append(lse_ref[pair, :, block_rows(number % ITEMS)])
            number += 1
        groups.append(
            (
                [q_ref[here, lanes] for here, there in spots],
                [k_ref[there, lanes] for here, there in spots],
                [v_ref[there, lanes] for here, there in spots],
                None,
                [dc_ref[here, lanes] for here, there in spots],
                lines,
            )
        )
    for (pair, spots), grads in zip(pairs, attend_groups_back(groups, None, None)):
        for number, (here, there) in enumerate(spots):
            dq_ref[here, pair_lanes(pair)] = grads[0][number]
            dk_ref[there, pair_lanes(pair)] = grads[1][number]
            dv_ref[there, pair_lanes(pair)] = grads[2][number]


def pair_spec(rows, first, wide):
    return pl.BlockSpec((rows, wide * 2 * HD), lambda step, places: (0, first // wide + step))


def flat_spec(first, wide, *shape):
    return pl.BlockSpec((wide,) + shape, lambda step, places: (first // wide + step, 0, 0))


def pair_call(kernel, places, operands, specs, out_specs, out_shape, scratch, work, pairs, wide):
    rows = ITEMS * BLOCK
    share = rows * rows * D * pairs // PAIRS
    return pl.pallas_call(
        kernel,
        grid_spec=pltpu.PrefetchScalarGridSpec(
            num_scalar_prefetch=1,
            grid=(pairs // wide,),
            in_specs=specs,
            out_specs=out_specs,
            scratch_shapes=scratch,
        ),
        out_shape=out_shape,
        compiler_params=pltpu.CompilerParams(vmem_limit_bytes=VMEM_LIMIT),
        cost_estimate=pl.CostEstimate(
            flops=work * share, bytes_accessed=16 * rows * D, transcendentals=share // HD
        ),
        name=kernel.__name__,
    )(places, *operands)


def attend(query, keys, values, places, lines):
    rows = query[0].shape[0]
    wide = SELF_WIDE if lines is not None else CROSS_WIDE
    operands = [part[0] for part in (query, keys, values)]
    specs = [pair_spec(rows, part[1], wide) for part in (query, keys, values)]
    scratch = []
    if lines is not None:
        operands.append(lines)
        specs.append(flat_spec(0, wide, 2, LINE))
        scratch.append(pltpu.VMEM((wide, 2, BLOCK, LINE), F32))
    return pair_call(
        cross_attend_kernel if lines is None else self_attend_kernel,
        places,
        operands,
        specs,
        [pair_spec(rows, 0, wide), flat_spec(0, wide, 2, rows)],
        [
            jax.ShapeDtypeStruct((rows, D), BF16),
            jax.ShapeDtypeStruct((PAIRS, 2, rows), F32),
        ],
        scratch,
        4,
        PAIRS,
        wide,
    )


def attend_back(query, keys, values, grad_context, lse, places, lines, first=0, pairs=PAIRS):
    rows = query[0].shape[0]
    wide = SELF_WIDE if lines is not None else CROSS_WIDE
    operands = [part[0] for part in (query, keys, values)] + [grad_context, lse]
    specs = [pair_spec(rows, part[1] + first, wide) for part in (query, keys, values)]
    specs += [pair_spec(rows, first, wide), flat_spec(first, wide, 2, rows)]
    out_specs = [pair_spec(rows, 0, wide)] * 3
    out_shape = [jax.ShapeDtypeStruct((rows, pairs * 2 * HD), BF16)] * 3
    scratch = []
    if lines is not None:
        operands.append(lines)
        specs.append(flat_spec(first, wide, 2, LINE))
        out_specs.append(flat_spec(0, wide, 2, LINE))
        out_shape.append(jax.ShapeDtypeStruct((pairs, 2, LINE), F32))
        scratch += [pltpu.VMEM((wide, 2, BLOCK, LINE), F32)] * 2
    return pair_call(
        cross_attend_back_kernel if lines is None else self_attend_back_kernel,
        places,
        operands,
        specs,
        out_specs,
        out_shape,
        scratch,
        10,
        pairs,
        wide,
    )


def exchange(rows, experts):
    parts = rows.reshape(experts, -1, rows.shape[-1])
    return lax.all_to_all(parts, "expert", split_axis=0, concat_axis=0, tiled=True).reshape(
        rows.shape
    )


def gelu_parts(value):
    square = value * value
    bend = jnp.tanh(value * (GELU_SCALE + GELU_SCALE * GELU_CUBE * square))
    half = 0.5 + 0.5 * bend
    slope = half + value * (half * (1.0 - bend)) * (
        GELU_SCALE + 3.0 * GELU_SCALE * GELU_CUBE * square
    )
    return value * half, slope


def row_blocks(rows):
    step = rows // 2
    return [slice(first, first + step) for first in range(0, rows, step)]


def expert_forward_kernel(x_ref, gate_ref, up_ref, down_ref, out_ref, total_ref):
    @pl.when(pl.program_id(0) == 0)
    def _():
        total_ref[...] = jnp.zeros(total_ref.shape, F32)

    for here in row_blocks(x_ref.shape[0]):
        rows = x_ref[here, :]
        value, _ = gelu_parts(dot(rows, gate_ref[...]))
        active = (value * dot(rows, up_ref[...])).astype(BF16)
        total_ref[here, :] += dot(active, down_ref[...])

    @pl.when(pl.program_id(0) == pl.num_programs(0) - 1)
    def _():
        out_ref[...] = total_ref[...].astype(BF16)


def hidden_grads(rows, grad_rows, gate_ref, up_ref, down_ref):
    gate = dot(rows, gate_ref[...])
    up = dot(rows, up_ref[...])
    grad_active = dot_nt(grad_rows, down_ref[...])
    value, slope = gelu_parts(gate)
    grad_gate = (grad_active * (up * slope)).astype(BF16)
    grad_up = (grad_active * value).astype(BF16)
    return value * up, grad_active, grad_gate, grad_up


def expert_both_kernel(
    x_ref, g_ref, gate_ref, up_ref, down_ref, dx_ref, active_ref, line_ref, dx_total, line_total
):
    @pl.when(pl.program_id(0) == 0)
    def _():
        dx_total[...] = jnp.zeros(dx_total.shape, F32)
        line_total[...] = jnp.zeros(line_total.shape, F32)

    for here in row_blocks(x_ref.shape[0]):
        active, grad_active, grad_gate, grad_up = hidden_grads(
            x_ref[here, :], g_ref[here, :], gate_ref, up_ref, down_ref
        )
        dx_total[here, :] += dot_nt(grad_gate, gate_ref[...]) + dot_nt(grad_up, up_ref[...])
        active_ref[here, :] = active.astype(BF16)
        product = active * grad_active
        line_total[here, :] += sum(
            product[:, first : first + 128] for first in range(0, product.shape[1], 128)
        )

    @pl.when(pl.program_id(0) == pl.num_programs(0) - 1)
    def _():
        dx_ref[...] = dx_total[...].astype(BF16)
        line_ref[...] = jnp.sum(line_total[...], axis=1, keepdims=True)


def expert_back_kernel(flags_ref, *refs, count):
    one_ref, two_ref, three_ref, scale_ref, gate_ref, up_ref, down_ref = refs[:7]
    dx_ref, x_ref, g_ref, active_ref, keep_ref, send_ref, dx_total, sems = refs[-8:]
    decoder = flags_ref[0] == 1
    first_group = flags_ref[1] == 0
    most = x_ref.shape[1]
    spare = slice(count, most)

    def load(rows, grads):
        copies = [
            pltpu.make_async_copy(rows, x_ref.at[0, pl.ds(0, count)], sems.at[0]),
            pltpu.make_async_copy(grads, g_ref.at[0, pl.ds(0, count)], sems.at[1]),
        ]
        for copy in copies:
            copy.start()
        for copy in copies:
            copy.wait()

    @pl.when(pl.program_id(0) == 0)
    def _():
        dx_total[...] = jnp.zeros(dx_total.shape, F32)

        @pl.when(decoder)
        def _():
            load(two_ref, one_ref)

        @pl.when(jnp.logical_not(decoder))
        def _():
            load(one_ref, three_ref)

        grads = g_ref[0, :count, :].astype(F32) * scale_ref[...]
        g_ref[0, :count, :] = grads.astype(BF16)
        if count < most:
            x_ref[0, spare, :] = jnp.zeros((most - count, D), BF16)
            g_ref[0, spare, :] = jnp.zeros((most - count, D), BF16)

    for here in row_blocks(count):
        active, _, grad_gate, grad_up = hidden_grads(
            x_ref[0, here, :], g_ref[0, here, :], gate_ref, up_ref, down_ref
        )
        dx_total[here, :] += dot_nt(grad_gate, gate_ref[...]) + dot_nt(grad_up, up_ref[...])
        active_ref[0, here, :] = active.astype(BF16)
        keep_ref[0, here, :] = jnp.where(first_group, grad_gate, grad_up)
        send_ref[0, here, :] = jnp.where(first_group, grad_up, grad_gate)
    if count < most:
        for ref in (active_ref, keep_ref, send_ref):
            ref[0, spare, :] = jnp.zeros((most - count, FF_TILE), BF16)

    @pl.when(pl.program_id(0) == pl.num_programs(0) - 1)
    def _():
        dx_ref[...] = dx_total[...].astype(BF16)


def expert_specs(rows):
    tiles = FF // FF_TILE
    whole = pl.BlockSpec((rows, D), lambda tile, *_: (0, 0))
    weight_specs = [
        pl.BlockSpec((D, FF_TILE), lambda tile, *_: (0, tile)),
        pl.BlockSpec((D, FF_TILE), lambda tile, *_: (0, tiles + tile)),
        pl.BlockSpec((FF_TILE, D), lambda tile, *_: (tile, 0)),
    ]
    return whole, weight_specs, tiles


def expert_cost(rows, products):
    return pl.CostEstimate(
        flops=2 * products * rows * D * FF, bytes_accessed=6 * D * FF, transcendentals=rows * FF
    )


def expert_forward(arrived, expert_first, expert_second):
    rows = arrived.shape[0]
    whole, weight_specs, tiles = expert_specs(rows)
    return pl.pallas_call(
        expert_forward_kernel,
        grid=(tiles,),
        in_specs=[whole] + weight_specs,
        out_specs=whole,
        out_shape=jax.ShapeDtypeStruct((rows, D), BF16),
        scratch_shapes=[pltpu.VMEM((rows, D), F32)],
        compiler_params=pltpu.CompilerParams(vmem_limit_bytes=VMEM_LIMIT),
        cost_estimate=expert_cost(rows, 3),
        name="expert_forward",
    )(arrived, expert_first, expert_first, expert_second)


def expert_both(arrived, grad_rows, expert_first, expert_second):
    rows = arrived.shape[0]
    whole, weight_specs, tiles = expert_specs(rows)
    row_shape = jax.ShapeDtypeStruct((rows, D), BF16)
    total = pltpu.VMEM((rows, D), F32)
    return pl.pallas_call(
        expert_both_kernel,
        grid=(tiles,),
        in_specs=[whole, whole] + weight_specs,
        out_specs=[
            whole,
            pl.BlockSpec((rows, FF_TILE), lambda tile: (0, tile)),
            pl.BlockSpec((rows, 1), lambda tile: (0, 0)),
        ],
        out_shape=[
            row_shape,
            jax.ShapeDtypeStruct((rows, FF), BF16),
            jax.ShapeDtypeStruct((rows, 1), F32),
        ],
        scratch_shapes=[total, pltpu.VMEM((rows, 128), F32)],
        compiler_params=pltpu.CompilerParams(vmem_limit_bytes=VMEM_LIMIT),
        cost_estimate=expert_cost(rows, 5),
        name="expert_both",
    )(arrived, grad_rows, expert_first, expert_first, expert_second)


def expert_back(flags, one, two, three, scale, expert_first, expert_second, kept, number, most):
    rows = one.shape[0]
    whole, weight_specs, tiles = expert_specs(rows)
    part = pl.BlockSpec((1, most, D), lambda tile, *_: (number, 0, 0))
    strip = pl.BlockSpec((1, most, FF_TILE), lambda tile, *_: (number, 0, tile))
    kept_shapes = [jax.ShapeDtypeStruct((2, most, D), BF16)] * 2
    kept_shapes += [jax.ShapeDtypeStruct((2, most, FF), BF16)] * 3
    anywhere = pl.BlockSpec(memory_space=pl.ANY)
    in_specs = [anywhere] * 3 + [pl.BlockSpec((rows, 1), lambda tile, *_: (0, 0))] + weight_specs
    operands = [one, two, three, scale, expert_first, expert_first, expert_second]
    aliases = {}
    if kept is not None:
        aliases = {1 + len(operands) + place: 1 + place for place in range(len(kept))}
        in_specs += [anywhere] * len(kept)
        operands += kept
    dx, *kept = pl.pallas_call(
        partial(expert_back_kernel, count=rows),
        grid_spec=pltpu.PrefetchScalarGridSpec(
            num_scalar_prefetch=1,
            grid=(tiles,),
            in_specs=in_specs,
            out_specs=[whole, part, part, strip, strip, strip],
            scratch_shapes=[pltpu.VMEM((rows, D), F32), pltpu.SemaphoreType.DMA((2,))],
        ),
        out_shape=[jax.ShapeDtypeStruct((rows, D), BF16)] + kept_shapes,
        input_output_aliases=aliases,
        compiler_params=pltpu.CompilerParams(vmem_limit_bytes=VMEM_LIMIT),
        cost_estimate=expert_cost(rows, 5),
        name="expert_back",
    )(flags, *operands)
    return dx, list(kept)


def gate_pair(normed, router_weight, picked_first, picked_second):
    logits = jnp.dot(normed, router_weight, precision=HIGHEST)
    first = jnp.sum(logits * picked_first, axis=1, keepdims=True)
    second = jnp.sum(logits * picked_second, axis=1, keepdims=True)
    return jax.nn.sigmoid(first - second), jax.nn.sigmoid(second - first)


def group_halves(rows, group):
    half = rows.shape[0] // 2
    sent = lax.dynamic_slice_in_dim(rows, (1 - group) * half, half, 0)
    kept = lax.dynamic_slice_in_dim(rows, group * half, half, 0)
    return kept, sent


def group_parts(rows, group):
    kept, sent = group_halves(rows, group)
    return kept, lax.ppermute(sent, "group", SWAP)


def group_swap(rows, group):
    kept, got = group_parts(rows, group)
    return kept + got


def shard_rows(grad):
    rows, columns = grad.shape
    parts = grad.astype(BF16).reshape(2, lax.axis_size("expert"), -1, columns)
    return jnp.swapaxes(parts, 0, 1).reshape(rows, columns)


def expert_scatter(rows):
    return lax.psum_scatter(rows, "expert", scatter_dimension=0, tiled=True)


def expert_gather(rows):
    return lax.all_gather(rows, "expert", axis=0, tiled=True)


def widen_kernel(part_ref, *refs):
    refs[-1][...] = part_ref[...].astype(F32)


def interleave(part, place, whole=None):
    rows = part.shape[0]
    half = D // 2
    operands = [part] if whole is None else [part, whole]
    specs = [pl.BlockSpec((rows, half), lambda step: (0, step))]
    if whole is not None:
        specs.append(pl.BlockSpec(memory_space=pl.ANY))
    return pl.pallas_call(
        widen_kernel,
        grid=(3,),
        in_specs=specs,
        out_specs=pl.BlockSpec((rows, half), lambda step: (0, 2 * step + place)),
        out_shape=jax.ShapeDtypeStruct((rows, 3 * D), F32),
        input_output_aliases={} if whole is None else {1: 0},
        compiler_params=pltpu.CompilerParams(vmem_limit_bytes=VMEM_LIMIT),
        cost_estimate=pl.CostEstimate(flops=0, bytes_accessed=9 * rows * D, transcendentals=0),
        name="interleave",
    )(*operands)


def add_pieces_kernel(kept_ref, *refs, spans):
    step = pl.program_id(0)
    for piece_ref, (first, last) in zip(refs[:-1], spans):

        @pl.when((step >= first) & (step < last))
        def _():
            refs[-1][...] = kept_ref[...] + piece_ref[...].astype(F32)


def add_pieces(kept, pieces, block):
    rows, columns = kept.shape
    spans = []
    specs = [pl.BlockSpec((block, columns), lambda step: (step, 0))]
    for piece in pieces:
        first = spans[-1][1] if spans else 0
        last = first + piece.shape[0] // block
        spans.append((first, last))

        def place(step, first=first, last=last):
            return jnp.clip(step - first, 0, last - first - 1), 0

        specs.append(pl.BlockSpec((block, columns), place))
    return pl.pallas_call(
        partial(add_pieces_kernel, spans=spans),
        grid=(rows // block,),
        in_specs=specs,
        out_specs=specs[0],
        out_shape=jax.ShapeDtypeStruct((rows, columns), F32),
        compiler_params=pltpu.CompilerParams(vmem_limit_bytes=VMEM_LIMIT),
        cost_estimate=pl.CostEstimate(
            flops=rows * columns, bytes_accessed=10 * rows * columns, transcendentals=0
        ),
        name="add_pieces",
    )(kept, *pieces)


def together(*values):
    return lax.optimization_barrier(values)


def per_device(
    inputs,
    cotangent,
    enc_lengths,
    routes,
    norm_gains,
    rel_bias,
    self_qkv,
    self_out,
    cross_proj,
    cross_value,
    router,
    expert_in,
    expert_out,
):
    decoder = lax.axis_index("half") == 1
    group = lax.axis_index("group")
    start_rows = inputs[0].astype(F32)
    row_count = start_rows.shape[0]
    gain_rows = norm_gains[0]
    bias_table = rel_bias[0]
    qkv_weight = self_qkv[0]
    out_weight = self_out[0]
    proj_weight = cross_proj[0]
    value_weight = cross_value[0]
    router_weight = router[0]
    expert_first = expert_in[0, 0]
    expert_second = expert_out[0, 0]
    routing = routes[0]
    experts = router_weight.shape[1]
    cot = cotangent[0]
    cot_f = cot.astype(F32)

    forward = [(0, 1)]
    backward = [(1, 0)]
    half_rows = D // 2
    both_weights = jnp.concatenate([proj_weight, value_weight], axis=1)
    pieces = [both_weights[first:last] for first, last in ((0, 352), (352, 704), (704, D))]

    long_place = jnp.sum(jnp.arange(ITEMS) * (enc_lengths == ENC_MOST)).astype(jnp.int32)
    places = jnp.stack([long_place, decoder.astype(jnp.int32)])
    offsets = ENC_MOST - np.arange(LINE)
    hits = jnp.where(decoder, bucket_hits(offsets, True), bucket_hits(offsets, False))
    lines = jnp.dot(bias_table, hits.T, precision=HIGHEST).reshape(PAIRS, 2, LINE)

    capacity = 5 * row_count // (2 * experts)
    padded = -(-capacity // 8) * 8
    first_chunk = padded // 16 * 8
    chunk_sizes = (first_chunk, padded - first_chunk)
    picked = [
        (routing[:, k : k + 1] == jnp.arange(experts, dtype=jnp.int32)[None, :]).astype(F32)
        for k in range(2)
    ]
    before = jnp.asarray(np.tril(np.ones((row_count, row_count)), -1), BF16)
    counts = dot(before, jnp.concatenate(picked, axis=1).astype(BF16))
    totals = jnp.sum(picked[0], axis=0, keepdims=True)
    slot_first = jnp.sum(picked[0] * counts[:, :experts], axis=1)
    slot_second = jnp.sum(picked[1] * (counts[:, experts:] + totals), axis=1)
    code_first = routing[:, 0] * padded + slot_first.astype(jnp.int32)
    code_second = routing[:, 1] * padded + slot_second.astype(jnp.int32)
    chunk_codes = []
    offset = 0
    for size in chunk_sizes:
        chunk_codes.append(
            (np.arange(experts)[:, None] * padded + offset + np.arange(size)[None, :])
            .reshape(-1)
            .astype(np.int32)
        )
        offset += size

    def spread(first_values, second_values):
        buffers = []
        for codes in chunk_codes:
            hit_first = (codes[:, None] == code_first[None, :]).astype(BF16)
            hit_second = (codes[:, None] == code_second[None, :]).astype(BF16)
            if first_values is second_values:
                buffers.append(dot(hit_first + hit_second, first_values).astype(BF16))
            else:
                buffers.append(
                    (dot(hit_first, first_values) + dot(hit_second, second_values)).astype(BF16)
                )
        return buffers

    def collect(buffers, code, first=0):
        total = None
        for codes, buffer in zip(chunk_codes[first:], buffers):
            part = dot((code[:, None] == codes[None, :]).astype(BF16), buffer)
            total = part if total is None else total + part
        return total

    normed_in = rms_norm(start_rows, gain_rows[0]).astype(BF16)
    project = dot(normed_in, qkv_weight).astype(BF16)
    query, keys, values = (project, 0), (project, PAIRS), (project, 2 * PAIRS)
    context, lse = attend(query, keys, values, places, lines)
    first_half = start_rows + dot(context, out_weight)
    normed_half = rms_norm(first_half, gain_rows[1])
    rounded_half = normed_half.astype(BF16)

    first_rows = jnp.where(decoder, cot, rounded_half)
    sent = spread(first_rows, first_rows)
    arrived_one = [exchange(part, experts) for part in sent]
    returned_one = []
    for k in range(2):
        part, piece = together(arrived_one[k], pieces[k])
        part = expert_forward(part, expert_first, expert_second)
        part, pieces[k] = together(part, lax.ppermute(piece, "half", forward))
        if k == 1:
            part, pieces[2] = together(part, pieces[2])
        returned_one.append(exchange(part, experts))
    returned_one[1], pieces[2] = together(
        returned_one[1], lax.ppermute(pieces[2], "half", forward)
    )
    both_weights = jnp.concatenate(pieces)
    memory_proj, memory_value = both_weights[:, :D], both_weights[:, D:]
    enc_gates = gate_pair(normed_half, router_weight, *picked)
    enc_first = collect(returned_one, code_first)
    enc_second = collect(returned_one, code_second)
    encoded = first_half + enc_gates[0] * enc_first + enc_gates[1] * enc_second
    memory = rms_norm(encoded, gain_rows[2]).astype(BF16)
    memory_in = lax.ppermute(memory, "half", forward)

    cross_query = dot(rounded_half, proj_weight).astype(BF16)
    memory_both = dot(memory_in, both_weights).astype(BF16)
    memory_keys, memory_values = (memory_both, 0), (memory_both, PAIRS)
    cross_context, cross_lse = attend(
        (cross_query, 0), memory_keys, memory_values, places, None
    )
    second_half = first_half + dot(cross_context, value_weight)
    normed_second = rms_norm(second_half, gain_rows[2])
    dec_gates = gate_pair(normed_second, router_weight, *picked)

    rounded_second = normed_second.astype(BF16)
    arrived_two = [exchange(part, experts) for part in spread(rounded_second, rounded_second)]
    all_codes = np.concatenate(chunk_codes)
    gate_rows = jnp.sum(
        jnp.where(all_codes[:, None] == code_first[None, :], dec_gates[0][:, 0][None, :], 0.0)
        + jnp.where(all_codes[:, None] == code_second[None, :], dec_gates[1][:, 0][None, :], 0.0),
        axis=1,
    )
    edge = experts * chunk_sizes[0]

    def exchange_lines(lines):
        parts = []
        for line in lines:
            parts += [line[:edge].reshape(experts, -1), line[edge:].reshape(experts, -1)]
        moved = lax.all_gather(jnp.concatenate(parts, axis=1), "expert", axis=0)
        moved = lax.dynamic_index_in_dim(moved, lax.axis_index("expert"), 1, keepdims=False)
        results = []
        first = 0
        for _ in lines:
            halves = []
            for size in chunk_sizes:
                halves.append(moved[:, first : first + size].reshape(-1))
                first += size
            results.append(jnp.concatenate(halves))
        return results

    actives_two = []
    returned_two = []
    gate_grads = []
    for part, grad_part in zip(arrived_two, arrived_one):
        grad_arrived, active, line = expert_both(part, grad_part, expert_first, expert_second)
        gate_grads.append(line[:, 0])
        actives_two.append(active)
        returned_two.append(exchange(grad_arrived, experts))
    first_parts, line_grads = together(
        [collect(returned_two[:1], code) for code in (code_first, code_second)],
        jnp.concatenate(gate_grads),
    )
    line_grads, arrived_gates = exchange_lines([line_grads, gate_rows])

    def collect_line(line, code):
        return jnp.sum(
            jnp.where(code[:, None] == all_codes[None, :], line[None, :], 0.0), axis=1, keepdims=True
        )

    def router_back(gates, grad_first, grad_second):
        pulled = gates[0] * gates[1] * (grad_first - grad_second)
        grad_logits = pulled * (picked[0] - picked[1])
        return grad_logits, jnp.dot(grad_logits, router_weight.T, precision=HIGHEST)

    dec_logits, dec_normed = router_back(
        dec_gates, collect_line(line_grads, code_first), collect_line(line_grads, code_second)
    )
    dec_normed = (
        dec_normed
        + dec_gates[0] * (first_parts[0] + collect(returned_two[1:], code_first, 1))
        + dec_gates[1] * (first_parts[1] + collect(returned_two[1:], code_second, 1))
    )
    pulled_rows, gain_dec_moe = rms_back(dec_normed, second_half, gain_rows[2])
    grad_second_half = cot_f + pulled_rows

    rounded_grad = grad_second_half.astype(BF16)
    grad_cross_context = dot_nt(rounded_grad, value_weight).astype(BF16)
    grad_cross_query, grad_memory_keys, grad_memory_values = attend_back(
        (cross_query, 0),
        memory_keys,
        memory_values,
        grad_cross_context,
        cross_lse,
        places,
        None,
    )
    key_part = dot_nt(grad_memory_keys, memory_proj)
    value_part, key_part = together(dot_nt(grad_memory_values, memory_value), key_part)
    grad_memory, actives_two = together((key_part + value_part).astype(BF16), actives_two)
    produced_two = [dot(active, expert_second).astype(BF16) for active in actives_two]
    grad_memory, grad_memory_keys, grad_memory_values, produced_two = together(
        lax.ppermute(grad_memory, "half", backward),
        grad_memory_keys,
        grad_memory_values,
        produced_two,
    )
    back_keys = lax.ppermute(grad_memory_keys, "half", backward)
    grad_memory = grad_memory.astype(F32)
    pulled_rows, gain_cross = rms_back(
        dot_nt(grad_cross_query, proj_weight), first_half, gain_rows[1]
    )
    grad_first_dec = grad_second_half + pulled_rows

    pulled_rows, gain_memory = rms_back(grad_memory, encoded, gain_rows[2])
    grad_encoded = cot_f + pulled_rows
    grad_gate_first = jnp.sum(grad_encoded * enc_first, axis=1, keepdims=True)
    grad_gate_second = jnp.sum(grad_encoded * enc_second, axis=1, keepdims=True)
    sent = spread(
        (enc_gates[0] * grad_encoded).astype(BF16), (enc_gates[1] * grad_encoded).astype(BF16)
    )
    normed_sharded = jnp.swapaxes(
        normed_in.reshape(row_count, 2, lax.axis_size("expert"), -1), 1, 2
    ).reshape(row_count, D)
    back_keys, grad_memory_values = together(back_keys, grad_memory_values)
    back_values = lax.ppermute(grad_memory_values, "half", backward)
    grad_proj = dot_tn(
        jnp.where(decoder, rounded_half, memory), jnp.where(decoder, grad_cross_query, back_keys)
    ).astype(BF16)
    sent = [jnp.where(decoder, produced, part) for produced, part in zip(produced_two, sent)]
    flags = jnp.stack([decoder.astype(jnp.int32), group])
    scales = jnp.where(decoder, arrived_gates, 1.0)[:, None]
    scales = [scales[:edge], scales[edge:]]
    proj_kept, proj_sent = group_halves(grad_proj, group)
    sent[1], normed_sharded, proj_kept, proj_sent, flags, scales = together(
        sent[1], normed_sharded, proj_kept, proj_sent, flags, scales
    )
    early = [(proj_kept, lax.ppermute(proj_sent, "group", SWAP))]
    arrived_three = [exchange(part, experts) for part in sent]
    most = max(part.shape[0] for part in arrived_one)
    kept = None
    returned_three = []
    for k, scale in enumerate(scales):
        grad_arrived, kept = expert_back(
            flags,
            arrived_one[k],
            arrived_two[k],
            arrived_three[k],
            scale,
            expert_first,
            expert_second,
            kept,
            k,
            most,
        )
        if k == 0:
            grad_arrived, back_values, early = together(grad_arrived, back_values, early)
            arrived_three[1], back_values = together(arrived_three[1], back_values)
            grad_value = dot_tn(
                jnp.where(decoder, cross_context, memory),
                jnp.where(decoder, rounded_grad, back_values),
            )
            early.append(group_parts(grad_value.astype(BF16), group))
        else:
            grad_arrived, early, kept, returned_three[0], arrived_three = together(
                grad_arrived, early, kept, returned_three[0], arrived_three
            )
        returned_three.append(exchange(grad_arrived, experts))

    expert_rows, expert_grad_rows, actives, keep_halves, send_halves = [
        part.reshape(2 * most, -1) for part in kept
    ]
    first_group = group == 0
    half_ff = FF // 2
    in_cuts = (0, 256, 512, 640, 768, 896, D)
    out_cuts = (0, half_ff // 4, half_ff // 2, half_ff)

    def cut(values, cuts):
        return [[values[first:last]] for first, last in zip(cuts[:-1], cuts[1:])]

    first_in = dot_tn(expert_rows[:, : in_cuts[1]], send_halves).astype(BF16)
    rest_in = dot_tn(expert_rows[:, in_cuts[1] :], send_halves).astype(BF16)
    sends = [[first_in]] + cut(rest_in, [place - in_cuts[1] for place in in_cuts[1:]])

    def swapped(parts):
        return [lax.ppermute(part, "group", SWAP) for part in parts]

    gots = [swapped(sends[0])]
    early = jnp.concatenate([mine + other for mine, other in early], axis=1)
    early = with_layout_constraint(early, Layout((0, 1)))
    returned_three[1], sends, gots, early = together(returned_three[1], sends, gots, early)
    early = expert_scatter(early)

    enc_logits, enc_normed = router_back(enc_gates, grad_gate_first, grad_gate_second)
    enc_normed = enc_normed + collect(returned_three, code_first) + collect(returned_three, code_second)
    pulled_rows, gain_enc_moe = rms_back(enc_normed, first_half, gain_rows[1])
    grad_first = jnp.where(decoder, grad_first_dec, grad_encoded + pulled_rows)

    rounded_grad = grad_first.astype(BF16)
    grad_context = dot_nt(rounded_grad, out_weight).astype(BF16)
    gots.append(swapped(sends[1]))
    halves = [
        attend_back(query, keys, values, grad_context, lse, places, lines, 0, PAIRS // 2)
    ]
    halves[0], gots, sends[2], early, grad_context = together(
        halves[0], gots, sends[2], early, grad_context
    )
    early = expert_gather(early)
    gots.append(swapped(sends[2]))
    halves.append(
        attend_back(query, keys, values, grad_context, lse, places, lines, PAIRS // 2, PAIRS // 2)
    )
    halves, gots, kept, arrived_three = together(
        halves, gots, (actives, expert_grad_rows), arrived_three
    )
    late_first = dot_tn(normed_sharded, jnp.concatenate(halves[0][:3], axis=1))
    late_first, halves, sends[3], kept, rounded_grad, early = together(
        late_first.astype(BF16), halves, sends[3], kept, rounded_grad, early
    )
    late_first = expert_scatter(late_first)
    gots.append(swapped(sends[3]))
    grad_project = jnp.concatenate(
        [half[part] for part in range(3) for half in halves], axis=1
    )
    grad_lines = jnp.concatenate([half[3] for half in halves])

    grad_table = jnp.dot(grad_lines.reshape(H, LINE), hits, precision=HIGHEST)
    grad_router = lax.dot_general(
        jnp.where(decoder, normed_second, normed_half),
        jnp.where(decoder, dec_logits, enc_logits),
        (((0,), (0,)), ((), ())),
        precision=HIGHEST,
    )
    grad_normed = dot_nt(grad_project, qkv_weight)
    grad_normed, gots, sends[4] = together(grad_normed, gots, sends[4])
    gots.append(swapped(sends[4]))
    pulled_rows, gain_self = rms_back(grad_normed, start_rows, gain_rows[0])
    grad_starts = grad_first + pulled_rows
    gain_grads = jnp.stack(
        [
            gain_self,
            jnp.where(decoder, gain_cross, gain_enc_moe),
            jnp.where(decoder, gain_dec_moe, gain_memory),
        ]
    )
    table_rows = jnp.pad(grad_table.reshape(2, -1), ((0, 0), (0, (D - H * NBKT) // 2)))
    small = jnp.concatenate([grad_router, gain_grads.T, table_rows.reshape(D, 1)], axis=1)
    small = jnp.pad(small, ((0, 0), (0, 128 - small.shape[1])))
    late_second = jnp.concatenate(
        [
            dot_tn(normed_sharded, jnp.concatenate(halves[1][:3], axis=1)).astype(BF16),
            shard_rows(small),
            shard_rows(dot_tn(context, rounded_grad)),
        ],
        axis=1,
    )
    late_second, gots, sends[5] = together(late_second, gots, sends[5])
    gots.append(swapped(sends[5]))
    late_second = expert_scatter(late_second)
    keep_in = dot_tn(expert_rows, keep_halves)
    keep_in, gots, late_first, kept = together(keep_in, gots, late_first, kept)
    actives, expert_grad_rows = kept
    send_out = dot_tn(
        jnp.where(first_group, actives[:, half_ff:], actives[:, :half_ff]), expert_grad_rows
    ).astype(BF16)
    out_sends = cut(send_out, out_cuts)
    out_sends, gots, late_first, kept = together(out_sends, gots, late_first, kept)
    late_first = group_swap(late_first, group)
    grad_expert_in = add_pieces(keep_in, [part[0] for part in gots], BLOCK)
    grad_expert_in, late_first, out_sends, kept = together(
        grad_expert_in, late_first, out_sends, kept
    )
    late_first = expert_gather(late_first)
    out_gots = [swapped(out_sends[0])]
    actives, expert_grad_rows = kept
    keep_out = dot_tn(
        jnp.where(first_group, actives[:, :half_ff], actives[:, half_ff:]), expert_grad_rows
    )
    keep_out, out_gots, out_sends = together(keep_out, out_gots, out_sends)
    out_gots.append(swapped(out_sends[1]))
    late_second, out_gots, out_sends, arrived_three = together(
        late_second, out_gots, out_sends, arrived_three
    )
    late_second = group_swap(late_second, group)
    late_second, out_sends, arrived_three = together(late_second, out_sends, arrived_three)
    late_second = expert_gather(late_second)
    last_got, late_first = together(swapped(out_sends[2]), late_first)
    out_gots.append(last_got)
    decoded = (
        second_half
        + dec_gates[0] * collect(arrived_three, code_first)
        + dec_gates[1] * collect(arrived_three, code_second)
    )
    result = jnp.where(decoder, decoded, encoded)

    result = result.astype(BF16)
    grad_expert_out = add_pieces(keep_out, [part[0] for part in out_gots], half_ff // 4)
    small = late_second[:, 3 * D // 2 : 3 * D // 2 + 128].astype(F32)
    small_table = small[: H * NBKT // 2, experts + 3].reshape(H // 2, NBKT)
    return (
        result[None],
        grad_starts.astype(BF16)[None],
        small[:, experts : experts + 3].T[None],
        small_table[None],
        interleave(late_second, 1, interleave(late_first, 0))[None],
        late_second[:, 3 * D // 2 + 128 :].astype(F32)[None],
        early[:, :D].astype(F32)[None],
        early[:, D:].astype(F32)[None],
        small[:, :experts][None],
        grad_expert_in[None, None],
        grad_expert_out[None, None],
    )


def solution(mesh):
    in_specs = (
        P("half", ("expert", "group"), None),
        P("half", ("expert", "group"), None),
        P(("expert", "group")),
        P("half", ("expert", "group"), None),
        P("half", None, None),
        P("half", None, None),
        P("half", None, None),
        P("half", None, None),
        P("half", None, None),
        P("half", None, None),
        P("half", None, None),
        P("half", "expert", None, None),
        P("half", "expert", None, None),
    )
    out_specs = (
        P("half", ("expert", "group"), None),
        P("half", ("expert", "group"), None),
        P("half", None, "group"),
        P("half", "group", None),
        P("half", "group", None),
        P("half", "group", None),
        P("half", "group", None),
        P("half", "group", None),
        P("half", "group", None),
        P("half", "expert", None, "group"),
        P("half", "expert", "group", None),
    )
    return jax.shard_map(
        per_device, mesh=mesh, in_specs=in_specs, out_specs=out_specs, check_vma=False
    )
```

```python
from functools import partial

import jax
import jax.numpy as jnp
import numpy as np
from jax import lax
from jax.experimental import pallas as pl
from jax.experimental.layout import Layout, with_layout_constraint
from jax.experimental.pallas import tpu as pltpu
from jax.sharding import PartitionSpec as P

D = 1024
H = 16
HD = 64
FF = 2816
NBKT = 32
DEC_SLOT = 128
DEC_LEN = 114
ENC_MOST = 512
ENC_MIN = 32
ITEMS = 5

EPSILON = 1e-06
MASKED = -1e30
HIGHEST = lax.Precision.HIGHEST
BLOCK = 128
PAIRS = H // 2
DIAGONAL = ENC_MOST // BLOCK - 1
LINE = 2 * ENC_MOST
FF_TILE = 256
CROSS_WIDE = 2
SELF_WIDE = 2
F32 = jnp.float32
BF16 = jnp.bfloat16
GELU_SCALE = float(np.sqrt(2.0 / np.pi))
GELU_CUBE = 0.044715
SWAP = ((0, 1), (1, 0))
VMEM_LIMIT = 60 * 1024 * 1024


def bucket_limits(exact_range, growth, divisions):
    limits = []
    for number in range(1, divisions):
        candidate = exact_range
        while candidate**divisions < exact_range**divisions * growth**number:
            candidate = candidate + 1
        limits.append(candidate)
    return limits


def rel_buckets(offset, causal):
    if causal:
        behind = np.maximum(-offset, 0)
        return np.minimum(behind, 16) + sum(
            (behind >= threshold).astype(np.int32) for threshold in bucket_limits(16, 8, 16)
        )
    distance = np.abs(offset)
    return (
        (offset > 0).astype(np.int32) * 16
        + np.minimum(distance, 8)
        + sum((distance >= threshold).astype(np.int32) for threshold in bucket_limits(8, 16, 8))
    )


def bucket_hits(offset, causal):
    return (rel_buckets(offset, causal)[:, None] == np.arange(NBKT)[None, :]).astype(np.float32)


def inverse_rms(values):
    return lax.rsqrt(jnp.mean(values * values, axis=-1, keepdims=True) + EPSILON)


def rms_norm(values, gain_vec):
    return values * inverse_rms(values) * gain_vec


def rms_back(grad_normed, values, gain_vec):
    scale = inverse_rms(values)
    unit = values * scale
    pulled = grad_normed * gain_vec
    grad_values = scale * (pulled - unit * jnp.mean(pulled * unit, axis=-1, keepdims=True))
    return grad_values, jnp.sum(grad_normed * unit, axis=0)


def dot(a, b):
    return jnp.dot(a, b, preferred_element_type=F32)


def dot_nt(a, b):
    return lax.dot_general(a, b, (((1,), (1,)), ((), ())), preferred_element_type=F32)


def dot_tn(a, b):
    return lax.dot_general(a, b, (((0,), (0,)), ((), ())), preferred_element_type=F32)


def skew(line, rows):
    width = line.shape[1]
    tile = jnp.broadcast_to(line, (8, width))
    row = lax.broadcasted_iota(jnp.int32, (8, width), 0)
    for step in (1, 2, 4):
        tile = jnp.where((row & step) != 0, pltpu.roll(tile, step, 1), tile)
    return jnp.concatenate(
        [pltpu.roll(tile, width - rows + first, 1) for first in range(0, rows, 8)], axis=0
    )


def unskew(total):
    rows, width = total.shape
    summed = None
    for first in range(0, rows, 8):
        moved = pltpu.roll(total[first : first + 8], rows - first, 1)
        summed = moved if summed is None else summed + moved
    row = lax.broadcasted_iota(jnp.int32, (8, width), 0)
    for step in (1, 2, 4):
        summed = jnp.where((row & step) != 0, pltpu.roll(summed, width - step, 1), summed)
    return jnp.sum(summed, axis=0, keepdims=True)


def own_lanes(head):
    return (lax.broadcasted_iota(jnp.int32, (1, 2 * HD), 1) // HD) == head


def head_lanes(head, value):
    return jnp.where(own_lanes(head), value, 0.0).astype(BF16)


def tile_places(keys, queries):
    key = lax.broadcasted_iota(jnp.int32, (keys, queries), 0)
    query = lax.broadcasted_iota(jnp.int32, (keys, queries), 1)
    return key, query


def causal_tile():
    key, query = tile_places(BLOCK, BLOCK)
    return (key <= query) & (key < DEC_LEN)


def short_tile():
    key, query = tile_places(BLOCK, BLOCK)
    return (key // ENC_MIN) == (query // ENC_MIN)


def bias_tiles(rows, queries, shares):
    return [
        (
            slice(block * BLOCK, (block + 1) * BLOCK),
            slice((DIAGONAL - block % (rows // BLOCK // shares)) * BLOCK, None),
            queries,
        )
        for block in range(rows // BLOCK)
    ]


def add_bias(scores, bias_ref, head, shares):
    rows, queries = scores.shape
    return joined(
        [
            scores[here] + bias_ref[head, :, lanes.start : lanes.start + queries]
            for here, lanes, queries in bias_tiles(rows, queries, shares)
        ]
    )


def add_bias_grad(dbias_ref, head, grad_scores, shares):
    rows, queries = grad_scores.shape
    sums = {}
    for here, lanes, queries in bias_tiles(rows, queries, shares):
        part = grad_scores[here]
        sums[lanes.start] = sums[lanes.start] + part if lanes.start in sums else part
    for first, part in sums.items():
        dbias_ref[head, :, first : first + queries] += part


def masked(scores, mask):
    return scores if mask is None else jnp.where(mask, scores, MASKED)


def key_parts(rows, shares):
    step = rows.shape[0] // shares
    return [rows[first : first + step] for first in range(0, rows.shape[0], step)]


def spread_max(values, shares):
    return [jnp.max(part, axis=0, keepdims=True) for part in key_parts(values, shares)]


def joined(parts):
    return parts[0] if len(parts) == 1 else jnp.concatenate(parts, axis=0)


def per_share(lines, rows):
    step = rows // len(lines)
    if len(lines) == 1:
        return lines[0]
    return jnp.concatenate(
        [jnp.broadcast_to(line, (step, line.shape[1])) for line in lines], axis=0
    )


def attend_groups(groups, bias_ref):
    units = [(group, head) for group in groups for head in range(2)]
    scores = []
    for (queries, keys, values, mask), head in units:
        scale = head_lanes(head, HD**-0.5)
        part = joined([dot_nt(key, query * scale) for query, key in zip(queries, keys)])
        scores.append(part)
    contexts = []
    log_sums = []
    for ((queries, keys, values, mask), head), part in zip(units, scores):
        shares = len(queries)
        if bias_ref is not None:
            part = add_bias(part, bias_ref, head, shares)
        part = masked(part, mask)
        highest = spread_max(part, shares)
        exponent = jnp.exp(part - per_share(highest, part.shape[0]))
        totals = [jnp.sum(rows, axis=0, keepdims=True) for rows in key_parts(exponent, shares)]
        log_sums.append([top + jnp.log(total) for top, total in zip(highest, totals)])
        rounded = key_parts(exponent.astype(BF16), shares)
        contexts.append(
            [
                dot_tn(rows, jnp.where(own_lanes(head), value, jnp.ones_like(value)))
                for rows, value in zip(rounded, values)
            ]
        )
    results = []
    for number in range(len(groups)):
        rows = []
        lines = []
        for share in range(len(groups[number][0])):
            first, second = contexts[2 * number][share], contexts[2 * number + 1][share]
            sums = jnp.where(own_lanes(0), second, first)
            context = jnp.where(own_lanes(0), first, second) / pltpu.roll(sums, HD, 1)
            rows.append(context.astype(BF16))
            lines.append(
                jnp.concatenate(
                    [log_sums[2 * number][share], log_sums[2 * number + 1][share]], axis=0
                )
            )
        results.append((rows, lines))
    return results


def attend_groups_back(groups, bias_ref, dbias_ref):
    units = [(group, head) for group in groups for head in range(2)]
    scores = []
    pulls = []
    for (queries, keys, values, mask, grads, lines), head in units:
        scale = head_lanes(head, HD**-0.5)
        own = head_lanes(head, 1.0)
        scores.append(joined([dot_nt(key, query * scale) for query, key in zip(queries, keys)]))
        pulls.append(joined([dot_nt(value, grad * own) for value, grad in zip(values, grads)]))
    totals = []
    for ((queries, keys, values, mask, grads, lines), head), part, pull in zip(units, scores, pulls):
        shares = len(queries)
        scale = head_lanes(head, HD**-0.5)
        own = head_lanes(head, 1.0)
        if bias_ref is not None:
            part = add_bias(part, bias_ref, head, shares)
        part = masked(part, mask)
        weights = jnp.exp(part - per_share([line[head : head + 1] for line in lines], part.shape[0]))
        product = weights * pull
        inner = [jnp.sum(rows, axis=0, keepdims=True) for rows in key_parts(product, shares)]
        grad_scores = product - weights * per_share(inner, part.shape[0])
        if dbias_ref is not None:
            add_bias_grad(dbias_ref, head, grad_scores, shares)
        rounded = key_parts(grad_scores.astype(BF16), shares)
        weights = key_parts(weights.astype(BF16), shares)
        totals.append(
            [
                [dot_tn(rows, key * scale) for rows, key in zip(rounded, keys)],
                [dot(rows, query * scale) for rows, query in zip(rounded, queries)],
                [dot(rows, grad * own) for rows, grad in zip(weights, grads)],
            ]
        )
    results = []
    for number in range(len(groups)):
        results.append(
            [
                [(one + two).astype(BF16) for one, two in zip(first, second)]
                for first, second in zip(totals[2 * number], totals[2 * number + 1])
            ]
        )
    return results


def short_places(place, item):
    later = (item >= place).astype(jnp.int32)
    return pl.multiple_of(item * ENC_MIN + later * ENC_MOST, ENC_MIN), item + later


def gather_short(ref, place, lanes):
    return jnp.concatenate(
        [ref[pl.ds(short_places(place, item)[0], ENC_MIN), lanes] for item in range(ITEMS - 1)],
        axis=0,
    )


def scatter_short(ref, place, rows, lanes):
    for item in range(ITEMS - 1):
        ref[pl.ds(short_places(place, item)[0], ENC_MIN), lanes] = rows[
            item * ENC_MIN : (item + 1) * ENC_MIN
        ]


def block_rows(block):
    return slice(block * BLOCK, (block + 1) * BLOCK)


def self_attend_kernel(place_ref, q_ref, k_ref, v_ref, line_ref, out_ref, lse_ref, bias_ref):
    pairs = range(q_ref.shape[1] // (2 * HD))
    for pair in pairs:
        for head in range(2):
            bias_ref[pair, head] = skew(line_ref[pair, head : head + 1, :], BLOCK)
    place = place_ref[0]
    decoder = place_ref[1] == 1

    @pl.when(decoder)
    def _():
        blocks = [block_rows(block) for block in range(ITEMS)]
        for pair in pairs:
            lanes = pair_lanes(pair)
            shares = tuple([ref[here, lanes] for here in blocks] for ref in (q_ref, k_ref, v_ref))
            mask = joined([causal_tile()] * ITEMS)
            ((rows, lines),) = attend_groups([shares + (mask,)], bias_ref.at[pair])
            for here, part, line in zip(blocks, rows, lines):
                out_ref[here, lanes] = part
                lse_ref[pair, :, here] = line

    @pl.when(jnp.logical_not(decoder))
    def _():
        here = pl.ds(pl.multiple_of(place * ENC_MIN, ENC_MIN), ENC_MOST)
        for pair in pairs:
            lanes = pair_lanes(pair)
            group = tuple([ref[here, lanes]] for ref in (q_ref, k_ref, v_ref)) + (None,)
            ((rows, lines),) = attend_groups([group], bias_ref.at[pair])
            out_ref[here, lanes] = rows[0]
            lse_ref[pair, :, :ENC_MOST] = lines[0]
        for pair in pairs:
            lanes = pair_lanes(pair)
            group = tuple([gather_short(ref, place, lanes)] for ref in (q_ref, k_ref, v_ref))
            ((rows, lines),) = attend_groups([group + (short_tile(),)], bias_ref.at[pair])
            scatter_short(out_ref, place, rows[0], lanes)
            lse_ref[pair, :, ENC_MOST:] = lines[0]


def self_attend_back_kernel(
    place_ref, q_ref, k_ref, v_ref, dc_ref, lse_ref, line_ref,
    dq_ref, dk_ref, dv_ref, dline_ref, bias_ref, dbias_ref,
):
    pairs = range(q_ref.shape[1] // (2 * HD))
    for pair in pairs:
        for head in range(2):
            bias_ref[pair, head] = skew(line_ref[pair, head : head + 1, :], BLOCK)
    dbias_ref[...] = jnp.zeros(dbias_ref.shape, F32)
    place = place_ref[0]
    decoder = place_ref[1] == 1
    ins = (q_ref, k_ref, v_ref)
    outs = (dq_ref, dk_ref, dv_ref)

    @pl.when(decoder)
    def _():
        blocks = [block_rows(block) for block in range(ITEMS)]
        for pair in pairs:
            lanes = pair_lanes(pair)
            shares = tuple([ref[here, lanes] for here in blocks] for ref in ins)
            shares += (
                joined([causal_tile()] * ITEMS),
                [dc_ref[here, lanes] for here in blocks],
                [lse_ref[pair, :, here] for here in blocks],
            )
            (grads,) = attend_groups_back([shares], bias_ref.at[pair], dbias_ref.at[pair])
            for ref, rows in zip(outs, grads):
                for here, part in zip(blocks, rows):
                    ref[here, lanes] = part

    @pl.when(jnp.logical_not(decoder))
    def _():
        here = pl.ds(pl.multiple_of(place * ENC_MIN, ENC_MIN), ENC_MOST)
        for pair in pairs:
            lanes = pair_lanes(pair)
            groups = [
                tuple([ref[here, lanes]] for ref in ins)
                + (None, [dc_ref[here, lanes]], [lse_ref[pair, :, :ENC_MOST]]),
                tuple([gather_short(ref, place, lanes)] for ref in ins)
                + (
                    short_tile(),
                    [gather_short(dc_ref, place, lanes)],
                    [lse_ref[pair, :, ENC_MOST:]],
                ),
            ]
            grads, short_grads = attend_groups_back(
                groups, bias_ref.at[pair], dbias_ref.at[pair]
            )
            for ref, rows, short_rows in zip(outs, grads, short_grads):
                ref[here, lanes] = rows[0]
                scatter_short(ref, place, short_rows[0], lanes)

    for pair in pairs:
        for head in range(2):
            dline_ref[pair, head : head + 1, :] = unskew(dbias_ref[pair, head])


def cross_places(place):
    long_pair = (
        pl.ds(pl.multiple_of(place * BLOCK, BLOCK), BLOCK),
        pl.ds(pl.multiple_of(place * ENC_MIN, ENC_MIN), ENC_MOST),
    )
    pairs = []
    for item in range(ITEMS - 1):
        start, number = short_places(place, item)
        pairs.append(
            (pl.ds(pl.multiple_of(number * BLOCK, BLOCK), BLOCK), pl.ds(start, ENC_MIN))
        )
    return [[long_pair], pairs]


def pair_lanes(pair):
    return slice(pair * 2 * HD, (pair + 1) * 2 * HD)


def cross_attend_kernel(place_ref, q_ref, k_ref, v_ref, out_ref, lse_ref):
    places = cross_places(place_ref[0])
    pairs = [(pair, spots) for pair in range(q_ref.shape[1] // (2 * HD)) for spots in places]
    groups = [
        (
            [q_ref[here, pair_lanes(pair)] for here, there in spots],
            [k_ref[there, pair_lanes(pair)] for here, there in spots],
            [v_ref[there, pair_lanes(pair)] for here, there in spots],
            None,
        )
        for pair, spots in pairs
    ]
    number = 0
    for (pair, spots), (rows, lines) in zip(pairs, attend_groups(groups, None)):
        for (here, there), part, line in zip(spots, rows, lines):
            out_ref[here, pair_lanes(pair)] = part
            lse_ref[pair, :, block_rows(number % ITEMS)] = line
            number += 1


def cross_attend_back_kernel(
    place_ref, q_ref, k_ref, v_ref, dc_ref, lse_ref, dq_ref, dk_ref, dv_ref
):
    places = cross_places(place_ref[0])
    pairs = [(pair, spots) for pair in range(q_ref.shape[1] // (2 * HD)) for spots in places]
    groups = []
    number = 0
    for pair, spots in pairs:
        lanes = pair_lanes(pair)
        lines = []
        for _ in spots:
            lines.append(lse_ref[pair, :, block_rows(number % ITEMS)])
            number += 1
        groups.append(
            (
                [q_ref[here, lanes] for here, there in spots],
                [k_ref[there, lanes] for here, there in spots],
                [v_ref[there, lanes] for here, there in spots],
                None,
                [dc_ref[here, lanes] for here, there in spots],
                lines,
            )
        )
    for (pair, spots), grads in zip(pairs, attend_groups_back(groups, None, None)):
        for number, (here, there) in enumerate(spots):
            dq_ref[here, pair_lanes(pair)] = grads[0][number]
            dk_ref[there, pair_lanes(pair)] = grads[1][number]
            dv_ref[there, pair_lanes(pair)] = grads[2][number]


def pair_spec(rows, first, wide):
    return pl.BlockSpec((rows, wide * 2 * HD), lambda step, places: (0, first // wide + step))


def flat_spec(first, wide, *shape):
    return pl.BlockSpec((wide,) + shape, lambda step, places: (first // wide + step, 0, 0))


def pair_call(kernel, places, operands, specs, out_specs, out_shape, scratch, work, pairs, wide):
    rows = ITEMS * BLOCK
    share = rows * rows * D * pairs // PAIRS
    return pl.pallas_call(
        kernel,
        grid_spec=pltpu.PrefetchScalarGridSpec(
            num_scalar_prefetch=1,
            grid=(pairs // wide,),
            in_specs=specs,
            out_specs=out_specs,
            scratch_shapes=scratch,
        ),
        out_shape=out_shape,
        compiler_params=pltpu.CompilerParams(vmem_limit_bytes=VMEM_LIMIT),
        cost_estimate=pl.CostEstimate(
            flops=work * share, bytes_accessed=16 * rows * D, transcendentals=share // HD
        ),
        name=kernel.__name__,
    )(places, *operands)


def attend(query, keys, values, places, lines):
    rows = query[0].shape[0]
    wide = SELF_WIDE if lines is not None else CROSS_WIDE
    operands = [part[0] for part in (query, keys, values)]
    specs = [pair_spec(rows, part[1], wide) for part in (query, keys, values)]
    scratch = []
    if lines is not None:
        operands.append(lines)
        specs.append(flat_spec(0, wide, 2, LINE))
        scratch.append(pltpu.VMEM((wide, 2, BLOCK, LINE), F32))
    return pair_call(
        cross_attend_kernel if lines is None else self_attend_kernel,
        places,
        operands,
        specs,
        [pair_spec(rows, 0, wide), flat_spec(0, wide, 2, rows)],
        [
            jax.ShapeDtypeStruct((rows, D), BF16),
            jax.ShapeDtypeStruct((PAIRS, 2, rows), F32),
        ],
        scratch,
        4,
        PAIRS,
        wide,
    )


def attend_back(query, keys, values, grad_context, lse, places, lines, first=0, pairs=PAIRS):
    rows = query[0].shape[0]
    wide = SELF_WIDE if lines is not None else CROSS_WIDE
    operands = [part[0] for part in (query, keys, values)] + [grad_context, lse]
    specs = [pair_spec(rows, part[1] + first, wide) for part in (query, keys, values)]
    specs += [pair_spec(rows, first, wide), flat_spec(first, wide, 2, rows)]
    out_specs = [pair_spec(rows, 0, wide)] * 3
    out_shape = [jax.ShapeDtypeStruct((rows, pairs * 2 * HD), BF16)] * 3
    scratch = []
    if lines is not None:
        operands.append(lines)
        specs.append(flat_spec(first, wide, 2, LINE))
        out_specs.append(flat_spec(0, wide, 2, LINE))
        out_shape.append(jax.ShapeDtypeStruct((pairs, 2, LINE), F32))
        scratch += [pltpu.VMEM((wide, 2, BLOCK, LINE), F32)] * 2
    return pair_call(
        cross_attend_back_kernel if lines is None else self_attend_back_kernel,
        places,
        operands,
        specs,
        out_specs,
        out_shape,
        scratch,
        10,
        pairs,
        wide,
    )


def exchange(rows, experts):
    parts = rows.reshape(experts, -1, rows.shape[-1])
    return lax.all_to_all(parts, "expert", split_axis=0, concat_axis=0, tiled=True).reshape(
        rows.shape
    )


def gelu_parts(value):
    square = value * value
    bend = jnp.tanh(value * (GELU_SCALE + GELU_SCALE * GELU_CUBE * square))
    half = 0.5 + 0.5 * bend
    slope = half + value * (half * (1.0 - bend)) * (
        GELU_SCALE + 3.0 * GELU_SCALE * GELU_CUBE * square
    )
    return value * half, slope


def row_blocks(rows):
    step = rows // 2
    return [slice(first, first + step) for first in range(0, rows, step)]


def expert_forward_kernel(x_ref, gate_ref, up_ref, down_ref, out_ref, total_ref):
    @pl.when(pl.program_id(0) == 0)
    def _():
        total_ref[...] = jnp.zeros(total_ref.shape, F32)

    for here in row_blocks(x_ref.shape[0]):
        rows = x_ref[here, :]
        value, _ = gelu_parts(dot(rows, gate_ref[...]))
        active = (value * dot(rows, up_ref[...])).astype(BF16)
        total_ref[here, :] += dot(active, down_ref[...])

    @pl.when(pl.program_id(0) == pl.num_programs(0) - 1)
    def _():
        out_ref[...] = total_ref[...].astype(BF16)


def hidden_grads(rows, grad_rows, gate_ref, up_ref, down_ref):
    gate = dot(rows, gate_ref[...])
    up = dot(rows, up_ref[...])
    grad_active = dot_nt(grad_rows, down_ref[...])
    value, slope = gelu_parts(gate)
    grad_gate = (grad_active * (up * slope)).astype(BF16)
    grad_up = (grad_active * value).astype(BF16)
    return value * up, grad_active, grad_gate, grad_up


def expert_both_kernel(
    x_ref, g_ref, gate_ref, up_ref, down_ref, dx_ref, active_ref, line_ref, dx_total, line_total
):
    @pl.when(pl.program_id(0) == 0)
    def _():
        dx_total[...] = jnp.zeros(dx_total.shape, F32)
        line_total[...] = jnp.zeros(line_total.shape, F32)

    for here in row_blocks(x_ref.shape[0]):
        active, grad_active, grad_gate, grad_up = hidden_grads(
            x_ref[here, :], g_ref[here, :], gate_ref, up_ref, down_ref
        )
        dx_total[here, :] += dot_nt(grad_gate, gate_ref[...]) + dot_nt(grad_up, up_ref[...])
        active_ref[here, :] = active.astype(BF16)
        product = active * grad_active
        line_total[here, :] += sum(
            product[:, first : first + 128] for first in range(0, product.shape[1], 128)
        )

    @pl.when(pl.program_id(0) == pl.num_programs(0) - 1)
    def _():
        dx_ref[...] = dx_total[...].astype(BF16)
        line_ref[...] = jnp.sum(line_total[...], axis=1, keepdims=True)


def expert_back_kernel(flags_ref, *refs, count):
    one_ref, two_ref, three_ref, scale_ref, gate_ref, up_ref, down_ref = refs[:7]
    dx_ref, x_ref, g_ref, active_ref, keep_ref, send_ref, dx_total, sems = refs[-8:]
    decoder = flags_ref[0] == 1
    first_group = flags_ref[1] == 0
    most = x_ref.shape[1]
    spare = slice(count, most)

    def load(rows, grads):
        copies = [
            pltpu.make_async_copy(rows, x_ref.at[0, pl.ds(0, count)], sems.at[0]),
            pltpu.make_async_copy(grads, g_ref.at[0, pl.ds(0, count)], sems.at[1]),
        ]
        for copy in copies:
            copy.start()
        for copy in copies:
            copy.wait()

    @pl.when(pl.program_id(0) == 0)
    def _():
        dx_total[...] = jnp.zeros(dx_total.shape, F32)

        @pl.when(decoder)
        def _():
            load(two_ref, one_ref)

        @pl.when(jnp.logical_not(decoder))
        def _():
            load(one_ref, three_ref)

        grads = g_ref[0, :count, :].astype(F32) * scale_ref[...]
        g_ref[0, :count, :] = grads.astype(BF16)
        if count < most:
            x_ref[0, spare, :] = jnp.zeros((most - count, D), BF16)
            g_ref[0, spare, :] = jnp.zeros((most - count, D), BF16)

    for here in row_blocks(count):
        active, _, grad_gate, grad_up = hidden_grads(
            x_ref[0, here, :], g_ref[0, here, :], gate_ref, up_ref, down_ref
        )
        dx_total[here, :] += dot_nt(grad_gate, gate_ref[...]) + dot_nt(grad_up, up_ref[...])
        active_ref[0, here, :] = active.astype(BF16)
        keep_ref[0, here, :] = jnp.where(first_group, grad_gate, grad_up)
        send_ref[0, here, :] = jnp.where(first_group, grad_up, grad_gate)
    if count < most:
        for ref in (active_ref, keep_ref, send_ref):
            ref[0, spare, :] = jnp.zeros((most - count, FF_TILE), BF16)

    @pl.when(pl.program_id(0) == pl.num_programs(0) - 1)
    def _():
        dx_ref[...] = dx_total[...].astype(BF16)


def expert_specs(rows):
    tiles = FF // FF_TILE
    whole = pl.BlockSpec((rows, D), lambda tile, *_: (0, 0))
    weight_specs = [
        pl.BlockSpec((D, FF_TILE), lambda tile, *_: (0, tile)),
        pl.BlockSpec((D, FF_TILE), lambda tile, *_: (0, tiles + tile)),
        pl.BlockSpec((FF_TILE, D), lambda tile, *_: (tile, 0)),
    ]
    return whole, weight_specs, tiles


def expert_cost(rows, products):
    return pl.CostEstimate(
        flops=2 * products * rows * D * FF, bytes_accessed=6 * D * FF, transcendentals=rows * FF
    )


def expert_forward(arrived, expert_first, expert_second):
    rows = arrived.shape[0]
    whole, weight_specs, tiles = expert_specs(rows)
    return pl.pallas_call(
        expert_forward_kernel,
        grid=(tiles,),
        in_specs=[whole] + weight_specs,
        out_specs=whole,
        out_shape=jax.ShapeDtypeStruct((rows, D), BF16),
        scratch_shapes=[pltpu.VMEM((rows, D), F32)],
        compiler_params=pltpu.CompilerParams(vmem_limit_bytes=VMEM_LIMIT),
        cost_estimate=expert_cost(rows, 3),
        name="expert_forward",
    )(arrived, expert_first, expert_first, expert_second)


def expert_both(arrived, grad_rows, expert_first, expert_second):
    rows = arrived.shape[0]
    whole, weight_specs, tiles = expert_specs(rows)
    row_shape = jax.ShapeDtypeStruct((rows, D), BF16)
    total = pltpu.VMEM((rows, D), F32)
    return pl.pallas_call(
        expert_both_kernel,
        grid=(tiles,),
        in_specs=[whole, whole] + weight_specs,
        out_specs=[
            whole,
            pl.BlockSpec((rows, FF_TILE), lambda tile: (0, tile)),
            pl.BlockSpec((rows, 1), lambda tile: (0, 0)),
        ],
        out_shape=[
            row_shape,
            jax.ShapeDtypeStruct((rows, FF), BF16),
            jax.ShapeDtypeStruct((rows, 1), F32),
        ],
        scratch_shapes=[total, pltpu.VMEM((rows, 128), F32)],
        compiler_params=pltpu.CompilerParams(vmem_limit_bytes=VMEM_LIMIT),
        cost_estimate=expert_cost(rows, 5),
        name="expert_both",
    )(arrived, grad_rows, expert_first, expert_first, expert_second)


def expert_back(flags, one, two, three, scale, expert_first, expert_second, kept, number, most):
    rows = one.shape[0]
    whole, weight_specs, tiles = expert_specs(rows)
    part = pl.BlockSpec((1, most, D), lambda tile, *_: (number, 0, 0))
    strip = pl.BlockSpec((1, most, FF_TILE), lambda tile, *_: (number, 0, tile))
    kept_shapes = [jax.ShapeDtypeStruct((2, most, D), BF16)] * 2
    kept_shapes += [jax.ShapeDtypeStruct((2, most, FF), BF16)] * 3
    anywhere = pl.BlockSpec(memory_space=pl.ANY)
    in_specs = [anywhere] * 3 + [pl.BlockSpec((rows, 1), lambda tile, *_: (0, 0))] + weight_specs
    operands = [one, two, three, scale, expert_first, expert_first, expert_second]
    aliases = {}
    if kept is not None:
        aliases = {1 + len(operands) + place: 1 + place for place in range(len(kept))}
        in_specs += [anywhere] * len(kept)
        operands += kept
    dx, *kept = pl.pallas_call(
        partial(expert_back_kernel, count=rows),
        grid_spec=pltpu.PrefetchScalarGridSpec(
            num_scalar_prefetch=1,
            grid=(tiles,),
            in_specs=in_specs,
            out_specs=[whole, part, part, strip, strip, strip],
            scratch_shapes=[pltpu.VMEM((rows, D), F32), pltpu.SemaphoreType.DMA((2,))],
        ),
        out_shape=[jax.ShapeDtypeStruct((rows, D), BF16)] + kept_shapes,
        input_output_aliases=aliases,
        compiler_params=pltpu.CompilerParams(vmem_limit_bytes=VMEM_LIMIT),
        cost_estimate=expert_cost(rows, 5),
        name="expert_back",
    )(flags, *operands)
    return dx, list(kept)


def gate_pair(normed, router_weight, picked_first, picked_second):
    logits = jnp.dot(normed, router_weight, precision=HIGHEST)
    first = jnp.sum(logits * picked_first, axis=1, keepdims=True)
    second = jnp.sum(logits * picked_second, axis=1, keepdims=True)
    return jax.nn.sigmoid(first - second), jax.nn.sigmoid(second - first)


def group_halves(rows, group):
    half = rows.shape[0] // 2
    sent = lax.dynamic_slice_in_dim(rows, (1 - group) * half, half, 0)
    kept = lax.dynamic_slice_in_dim(rows, group * half, half, 0)
    return kept, sent


def group_parts(rows, group):
    kept, sent = group_halves(rows, group)
    return kept, lax.ppermute(sent, "group", SWAP)


def group_swap(rows, group):
    kept, got = group_parts(rows, group)
    return kept + got


def shard_rows(grad):
    rows, columns = grad.shape
    parts = grad.astype(BF16).reshape(2, lax.axis_size("expert"), -1, columns)
    return jnp.swapaxes(parts, 0, 1).reshape(rows, columns)


def expert_scatter(rows):
    return lax.psum_scatter(rows, "expert", scatter_dimension=0, tiled=True)


def expert_gather(rows):
    return lax.all_gather(rows, "expert", axis=0, tiled=True)


def widen_kernel(part_ref, *refs):
    refs[-1][...] = part_ref[...].astype(F32)


def interleave(part, place, whole=None):
    rows = part.shape[0]
    half = D // 2
    operands = [part] if whole is None else [part, whole]
    specs = [pl.BlockSpec((rows, half), lambda step: (0, step))]
    if whole is not None:
        specs.append(pl.BlockSpec(memory_space=pl.ANY))
    return pl.pallas_call(
        widen_kernel,
        grid=(3,),
        in_specs=specs,
        out_specs=pl.BlockSpec((rows, half), lambda step: (0, 2 * step + place)),
        out_shape=jax.ShapeDtypeStruct((rows, 3 * D), F32),
        input_output_aliases={} if whole is None else {1: 0},
        compiler_params=pltpu.CompilerParams(vmem_limit_bytes=VMEM_LIMIT),
        cost_estimate=pl.CostEstimate(flops=0, bytes_accessed=9 * rows * D, transcendentals=0),
        name="interleave",
    )(*operands)


def add_pieces_kernel(kept_ref, *refs, spans):
    step = pl.program_id(0)
    for piece_ref, (first, last) in zip(refs[:-1], spans):

        @pl.when((step >= first) & (step < last))
        def _():
            refs[-1][...] = kept_ref[...] + piece_ref[...].astype(F32)


def add_pieces(kept, pieces, block):
    rows, columns = kept.shape
    spans = []
    specs = [pl.BlockSpec((block, columns), lambda step: (step, 0))]
    for piece in pieces:
        first = spans[-1][1] if spans else 0
        last = first + piece.shape[0] // block
        spans.append((first, last))

        def place(step, first=first, last=last):
            return jnp.clip(step - first, 0, last - first - 1), 0

        specs.append(pl.BlockSpec((block, columns), place))
    return pl.pallas_call(
        partial(add_pieces_kernel, spans=spans),
        grid=(rows // block,),
        in_specs=specs,
        out_specs=specs[0],
        out_shape=jax.ShapeDtypeStruct((rows, columns), F32),
        compiler_params=pltpu.CompilerParams(vmem_limit_bytes=VMEM_LIMIT),
        cost_estimate=pl.CostEstimate(
            flops=rows * columns, bytes_accessed=10 * rows * columns, transcendentals=0
        ),
        name="add_pieces",
    )(kept, *pieces)


def together(*values):
    return lax.optimization_barrier(values)


def per_device(
    inputs,
    cotangent,
    enc_lengths,
    routes,
    norm_gains,
    rel_bias,
    self_qkv,
    self_out,
    cross_proj,
    cross_value,
    router,
    expert_in,
    expert_out,
):
    decoder = lax.axis_index("half") == 1
    group = lax.axis_index("group")
    start_rows = inputs[0].astype(F32)
    row_count = start_rows.shape[0]
    gain_rows = norm_gains[0]
    bias_table = rel_bias[0]
    qkv_weight = self_qkv[0]
    out_weight = self_out[0]
    proj_weight = cross_proj[0]
    value_weight = cross_value[0]
    router_weight = router[0]
    expert_first = expert_in[0, 0]
    expert_second = expert_out[0, 0]
    routing = routes[0]
    experts = router_weight.shape[1]
    cot = cotangent[0]
    cot_f = cot.astype(F32)

    forward = [(0, 1)]
    backward = [(1, 0)]
    half_rows = D // 2
    both_weights = jnp.concatenate([proj_weight, value_weight], axis=1)
    pieces = [both_weights[first:last] for first, last in ((0, 352), (352, 704), (704, D))]

    long_place = jnp.sum(jnp.arange(ITEMS) * (enc_lengths == ENC_MOST)).astype(jnp.int32)
    places = jnp.stack([long_place, decoder.astype(jnp.int32)])
    offsets = ENC_MOST - np.arange(LINE)
    hits = jnp.where(decoder, bucket_hits(offsets, True), bucket_hits(offsets, False))
    lines = jnp.dot(bias_table, hits.T, precision=HIGHEST).reshape(PAIRS, 2, LINE)

    capacity = 5 * row_count // (2 * experts)
    padded = -(-capacity // 8) * 8
    first_chunk = padded // 16 * 8
    chunk_sizes = (first_chunk, padded - first_chunk)
    picked = [
        (routing[:, k : k + 1] == jnp.arange(experts, dtype=jnp.int32)[None, :]).astype(F32)
        for k in range(2)
    ]
    before = jnp.asarray(np.tril(np.ones((row_count, row_count)), -1), BF16)
    counts = dot(before, jnp.concatenate(picked, axis=1).astype(BF16))
    totals = jnp.sum(picked[0], axis=0, keepdims=True)
    slot_first = jnp.sum(picked[0] * counts[:, :experts], axis=1)
    slot_second = jnp.sum(picked[1] * (counts[:, experts:] + totals), axis=1)
    code_first = routing[:, 0] * padded + slot_first.astype(jnp.int32)
    code_second = routing[:, 1] * padded + slot_second.astype(jnp.int32)
    chunk_codes = []
    offset = 0
    for size in chunk_sizes:
        chunk_codes.append(
            (np.arange(experts)[:, None] * padded + offset + np.arange(size)[None, :])
            .reshape(-1)
            .astype(np.int32)
        )
        offset += size

    def spread(first_values, second_values):
        buffers = []
        for codes in chunk_codes:
            hit_first = (codes[:, None] == code_first[None, :]).astype(BF16)
            hit_second = (codes[:, None] == code_second[None, :]).astype(BF16)
            if first_values is second_values:
                buffers.append(dot(hit_first + hit_second, first_values).astype(BF16))
            else:
                buffers.append(
                    (dot(hit_first, first_values) + dot(hit_second, second_values)).astype(BF16)
                )
        return buffers

    def collect(buffers, code, first=0):
        total = None
        for codes, buffer in zip(chunk_codes[first:], buffers):
            part = dot((code[:, None] == codes[None, :]).astype(BF16), buffer)
            total = part if total is None else total + part
        return total

    normed_in = rms_norm(start_rows, gain_rows[0]).astype(BF16)
    project = dot(normed_in, qkv_weight).astype(BF16)
    query, keys, values = (project, 0), (project, PAIRS), (project, 2 * PAIRS)
    context, lse = attend(query, keys, values, places, lines)
    first_half = start_rows + dot(context, out_weight)
    normed_half = rms_norm(first_half, gain_rows[1])
    rounded_half = normed_half.astype(BF16)

    first_rows = jnp.where(decoder, cot, rounded_half)
    sent = spread(first_rows, first_rows)
    arrived_one = [exchange(part, experts) for part in sent]
    returned_one = []
    for k in range(2):
        part, piece = together(arrived_one[k], pieces[k])
        part = expert_forward(part, expert_first, expert_second)
        part, pieces[k] = together(part, lax.ppermute(piece, "half", forward))
        if k == 1:
            part, pieces[2] = together(part, pieces[2])
        returned_one.append(exchange(part, experts))
    returned_one[1], pieces[2] = together(
        returned_one[1], lax.ppermute(pieces[2], "half", forward)
    )
    both_weights = jnp.concatenate(pieces)
    memory_proj, memory_value = both_weights[:, :D], both_weights[:, D:]
    enc_gates = gate_pair(normed_half, router_weight, *picked)
    enc_first = collect(returned_one, code_first)
    enc_second = collect(returned_one, code_second)
    encoded = first_half + enc_gates[0] * enc_first + enc_gates[1] * enc_second
    memory = rms_norm(encoded, gain_rows[2]).astype(BF16)
    memory_in = lax.ppermute(memory, "half", forward)

    cross_query = dot(rounded_half, proj_weight).astype(BF16)
    memory_both = dot(memory_in, both_weights).astype(BF16)
    memory_keys, memory_values = (memory_both, 0), (memory_both, PAIRS)
    cross_context, cross_lse = attend(
        (cross_query, 0), memory_keys, memory_values, places, None
    )
    second_half = first_half + dot(cross_context, value_weight)
    normed_second = rms_norm(second_half, gain_rows[2])
    dec_gates = gate_pair(normed_second, router_weight, *picked)

    rounded_second = normed_second.astype(BF16)
    arrived_two = [exchange(part, experts) for part in spread(rounded_second, rounded_second)]
    all_codes = np.concatenate(chunk_codes)
    gate_rows = jnp.sum(
        jnp.where(all_codes[:, None] == code_first[None, :], dec_gates[0][:, 0][None, :], 0.0)
        + jnp.where(all_codes[:, None] == code_second[None, :], dec_gates[1][:, 0][None, :], 0.0),
        axis=1,
    )
    edge = experts * chunk_sizes[0]

    def exchange_lines(lines):
        parts = []
        for line in lines:
            parts += [line[:edge].reshape(experts, -1), line[edge:].reshape(experts, -1)]
        moved = lax.all_gather(jnp.concatenate(parts, axis=1), "expert", axis=0)
        moved = lax.dynamic_index_in_dim(moved, lax.axis_index("expert"), 1, keepdims=False)
        results = []
        first = 0
        for _ in lines:
            halves = []
            for size in chunk_sizes:
                halves.append(moved[:, first : first + size].reshape(-1))
                first += size
            results.append(jnp.concatenate(halves))
        return results

    actives_two = []
    returned_two = []
    gate_grads = []
    for part, grad_part in zip(arrived_two, arrived_one):
        grad_arrived, active, line = expert_both(part, grad_part, expert_first, expert_second)
        gate_grads.append(line[:, 0])
        actives_two.append(active)
        returned_two.append(exchange(grad_arrived, experts))
    first_parts, line_grads = together(
        [collect(returned_two[:1], code) for code in (code_first, code_second)],
        jnp.concatenate(gate_grads),
    )
    line_grads, arrived_gates = exchange_lines([line_grads, gate_rows])

    def collect_line(line, code):
        return jnp.sum(
            jnp.where(code[:, None] == all_codes[None, :], line[None, :], 0.0), axis=1, keepdims=True
        )

    def router_back(gates, grad_first, grad_second):
        pulled = gates[0] * gates[1] * (grad_first - grad_second)
        grad_logits = pulled * (picked[0] - picked[1])
        return grad_logits, jnp.dot(grad_logits, router_weight.T, precision=HIGHEST)

    dec_logits, dec_normed = router_back(
        dec_gates, collect_line(line_grads, code_first), collect_line(line_grads, code_second)
    )
    dec_normed = (
        dec_normed
        + dec_gates[0] * (first_parts[0] + collect(returned_two[1:], code_first, 1))
        + dec_gates[1] * (first_parts[1] + collect(returned_two[1:], code_second, 1))
    )
    pulled_rows, gain_dec_moe = rms_back(dec_normed, second_half, gain_rows[2])
    grad_second_half = cot_f + pulled_rows

    rounded_grad = grad_second_half.astype(BF16)
    grad_cross_context = dot_nt(rounded_grad, value_weight).astype(BF16)
    grad_cross_query, grad_memory_keys, grad_memory_values = attend_back(
        (cross_query, 0),
        memory_keys,
        memory_values,
        grad_cross_context,
        cross_lse,
        places,
        None,
    )
    key_part = dot_nt(grad_memory_keys, memory_proj)
    value_part, key_part = together(dot_nt(grad_memory_values, memory_value), key_part)
    grad_memory, actives_two = together((key_part + value_part).astype(BF16), actives_two)
    produced_two = [dot(active, expert_second).astype(BF16) for active in actives_two]
    grad_memory, grad_memory_keys, grad_memory_values, produced_two = together(
        lax.ppermute(grad_memory, "half", backward),
        grad_memory_keys,
        grad_memory_values,
        produced_two,
    )
    back_keys = lax.ppermute(grad_memory_keys, "half", backward)
    grad_memory = grad_memory.astype(F32)
    pulled_rows, gain_cross = rms_back(
        dot_nt(grad_cross_query, proj_weight), first_half, gain_rows[1]
    )
    grad_first_dec = grad_second_half + pulled_rows

    pulled_rows, gain_memory = rms_back(grad_memory, encoded, gain_rows[2])
    grad_encoded = cot_f + pulled_rows
    grad_gate_first = jnp.sum(grad_encoded * enc_first, axis=1, keepdims=True)
    grad_gate_second = jnp.sum(grad_encoded * enc_second, axis=1, keepdims=True)
    sent = spread(
        (enc_gates[0] * grad_encoded).astype(BF16), (enc_gates[1] * grad_encoded).astype(BF16)
    )
    normed_sharded = jnp.swapaxes(
        normed_in.reshape(row_count, 2, lax.axis_size("expert"), -1), 1, 2
    ).reshape(row_count, D)
    back_keys, grad_memory_values = together(back_keys, grad_memory_values)
    back_values = lax.ppermute(grad_memory_values, "half", backward)
    grad_proj = dot_tn(
        jnp.where(decoder, rounded_half, memory), jnp.where(decoder, grad_cross_query, back_keys)
    ).astype(BF16)
    sent = [jnp.where(decoder, produced, part) for produced, part in zip(produced_two, sent)]
    flags = jnp.stack([decoder.astype(jnp.int32), group])
    scales = jnp.where(decoder, arrived_gates, 1.0)[:, None]
    scales = [scales[:edge], scales[edge:]]
    proj_kept, proj_sent = group_halves(grad_proj, group)
    sent[1], normed_sharded, proj_kept, proj_sent, flags, scales = together(
        sent[1], normed_sharded, proj_kept, proj_sent, flags, scales
    )
    early = [(proj_kept, lax.ppermute(proj_sent, "group", SWAP))]
    arrived_three = [exchange(part, experts) for part in sent]
    most = max(part.shape[0] for part in arrived_one)
    kept = None
    returned_three = []
    for k, scale in enumerate(scales):
        grad_arrived, kept = expert_back(
            flags,
            arrived_one[k],
            arrived_two[k],
            arrived_three[k],
            scale,
            expert_first,
            expert_second,
            kept,
            k,
            most,
        )
        if k == 0:
            grad_arrived, back_values, early = together(grad_arrived, back_values, early)
            arrived_three[1], back_values = together(arrived_three[1], back_values)
            grad_value = dot_tn(
                jnp.where(decoder, cross_context, memory),
                jnp.where(decoder, rounded_grad, back_values),
            )
            early.append(group_parts(grad_value.astype(BF16), group))
        else:
            grad_arrived, early, kept, returned_three[0], arrived_three = together(
                grad_arrived, early, kept, returned_three[0], arrived_three
            )
        returned_three.append(exchange(grad_arrived, experts))

    expert_rows, expert_grad_rows, actives, keep_halves, send_halves = [
        part.reshape(2 * most, -1) for part in kept
    ]
    first_group = group == 0
    half_ff = FF // 2
    in_cuts = (0, 256, 512, 640, 768, 896, D)
    out_cuts = (0, half_ff // 4, half_ff // 2, half_ff)

    def cut(values, cuts):
        return [[values[first:last]] for first, last in zip(cuts[:-1], cuts[1:])]

    first_in = dot_tn(expert_rows[:, : in_cuts[1]], send_halves).astype(BF16)
    rest_in = dot_tn(expert_rows[:, in_cuts[1] :], send_halves).astype(BF16)
    sends = [[first_in]] + cut(rest_in, [place - in_cuts[1] for place in in_cuts[1:]])

    def swapped(parts):
        return [lax.ppermute(part, "group", SWAP) for part in parts]

    gots = [swapped(sends[0])]
    early = jnp.concatenate([mine + other for mine, other in early], axis=1)
    early = with_layout_constraint(early, Layout((0, 1)))
    returned_three[1], sends, gots, early = together(returned_three[1], sends, gots, early)
    early = expert_scatter(early)

    enc_logits, enc_normed = router_back(enc_gates, grad_gate_first, grad_gate_second)
    enc_normed = enc_normed + collect(returned_three, code_first) + collect(returned_three, code_second)
    pulled_rows, gain_enc_moe = rms_back(enc_normed, first_half, gain_rows[1])
    grad_first = jnp.where(decoder, grad_first_dec, grad_encoded + pulled_rows)

    rounded_grad = grad_first.astype(BF16)
    grad_context = dot_nt(rounded_grad, out_weight).astype(BF16)
    gots.append(swapped(sends[1]))
    halves = [
        attend_back(query, keys, values, grad_context, lse, places, lines, 0, PAIRS // 2)
    ]
    halves[0], gots, sends[2], early, grad_context = together(
        halves[0], gots, sends[2], early, grad_context
    )
    early = expert_gather(early)
    gots.append(swapped(sends[2]))
    halves.append(
        attend_back(query, keys, values, grad_context, lse, places, lines, PAIRS // 2, PAIRS // 2)
    )
    halves, gots, kept, arrived_three = together(
        halves, gots, (actives, expert_grad_rows), arrived_three
    )
    late_first = dot_tn(normed_sharded, jnp.concatenate(halves[0][:3], axis=1))
    late_first, halves, sends[3], kept, rounded_grad, early = together(
        late_first.astype(BF16), halves, sends[3], kept, rounded_grad, early
    )
    late_first = expert_scatter(late_first)
    gots.append(swapped(sends[3]))
    grad_project = jnp.concatenate(
        [half[part] for part in range(3) for half in halves], axis=1
    )
    grad_lines = jnp.concatenate([half[3] for half in halves])

    grad_table = jnp.dot(grad_lines.reshape(H, LINE), hits, precision=HIGHEST)
    grad_router = lax.dot_general(
        jnp.where(decoder, normed_second, normed_half),
        jnp.where(decoder, dec_logits, enc_logits),
        (((0,), (0,)), ((), ())),
        precision=HIGHEST,
    )
    grad_normed = dot_nt(grad_project, qkv_weight)
    grad_normed, gots, sends[4] = together(grad_normed, gots, sends[4])
    gots.append(swapped(sends[4]))
    pulled_rows, gain_self = rms_back(grad_normed, start_rows, gain_rows[0])
    grad_starts = grad_first + pulled_rows
    gain_grads = jnp.stack(
        [
            gain_self,
            jnp.where(decoder, gain_cross, gain_enc_moe),
            jnp.where(decoder, gain_dec_moe, gain_memory),
        ]
    )
    table_rows = jnp.pad(grad_table.reshape(2, -1), ((0, 0), (0, (D - H * NBKT) // 2)))
    small = jnp.concatenate([grad_router, gain_grads.T, table_rows.reshape(D, 1)], axis=1)
    small = jnp.pad(small, ((0, 0), (0, 128 - small.shape[1])))
    late_second = jnp.concatenate(
        [
            dot_tn(normed_sharded, jnp.concatenate(halves[1][:3], axis=1)).astype(BF16),
            shard_rows(small),
            shard_rows(dot_tn(context, rounded_grad)),
        ],
        axis=1,
    )
    late_second, gots, sends[5] = together(late_second, gots, sends[5])
    gots.append(swapped(sends[5]))
    late_second = expert_scatter(late_second)
    keep_in = dot_tn(expert_rows, keep_halves)
    keep_in, gots, late_first, kept = together(keep_in, gots, late_first, kept)
    actives, expert_grad_rows = kept
    send_out = dot_tn(
        jnp.where(first_group, actives[:, half_ff:], actives[:, :half_ff]), expert_grad_rows
    ).astype(BF16)
    out_sends = cut(send_out, out_cuts)
    out_sends, gots, late_first, kept = together(out_sends, gots, late_first, kept)
    late_first = group_swap(late_first, group)
    grad_expert_in = add_pieces(keep_in, [part[0] for part in gots], BLOCK)
    grad_expert_in, late_first, out_sends, kept, first_got = together(
        grad_expert_in, late_first, out_sends, kept, swapped(out_sends[0])
    )
    late_first = expert_gather(late_first)
    out_gots = [first_got, swapped(out_sends[1])]
    actives, expert_grad_rows = kept
    keep_out = dot_tn(
        jnp.where(first_group, actives[:, :half_ff], actives[:, half_ff:]), expert_grad_rows
    )
    keep_out, out_gots, out_sends = together(keep_out, out_gots, out_sends)
    late_second, out_gots, out_sends, arrived_three = together(
        late_second, out_gots, out_sends, arrived_three
    )
    late_second = group_swap(late_second, group)
    late_second, out_sends, arrived_three = together(late_second, out_sends, arrived_three)
    late_second = expert_gather(late_second)
    last_got, late_first = together(swapped(out_sends[2]), late_first)
    out_gots.append(last_got)
    decoded = (
        second_half
        + dec_gates[0] * collect(arrived_three, code_first)
        + dec_gates[1] * collect(arrived_three, code_second)
    )
    result = jnp.where(decoder, decoded, encoded)

    result = result.astype(BF16)
    grad_expert_out = add_pieces(keep_out, [part[0] for part in out_gots], half_ff // 4)
    small = late_second[:, 3 * D // 2 : 3 * D // 2 + 128].astype(F32)
    small_table = small[: H * NBKT // 2, experts + 3].reshape(H // 2, NBKT)
    return (
        result[None],
        grad_starts.astype(BF16)[None],
        small[:, experts : experts + 3].T[None],
        small_table[None],
        interleave(late_second, 1, interleave(late_first, 0))[None],
        late_second[:, 3 * D // 2 + 128 :].astype(F32)[None],
        early[:, :D].astype(F32)[None],
        early[:, D:].astype(F32)[None],
        small[:, :experts][None],
        grad_expert_in[None, None],
        grad_expert_out[None, None],
    )


def solution(mesh):
    in_specs = (
        P("half", ("expert", "group"), None),
        P("half", ("expert", "group"), None),
        P(("expert", "group")),
        P("half", ("expert", "group"), None),
        P("half", None, None),
        P("half", None, None),
        P("half", None, None),
        P("half", None, None),
        P("half", None, None),
        P("half", None, None),
        P("half", None, None),
        P("half", "expert", None, None),
        P("half", "expert", None, None),
    )
    out_specs = (
        P("half", ("expert", "group"), None),
        P("half", ("expert", "group"), None),
        P("half", None, "group"),
        P("half", "group", None),
        P("half", "group", None),
        P("half", "group", None),
        P("half", "group", None),
        P("half", "group", None),
        P("half", "group", None),
        P("half", "expert", None, "group"),
        P("half", "expert", "group", None),
    )
    return jax.shard_map(
        per_device, mesh=mesh, in_specs=in_specs, out_specs=out_specs, check_vma=False
    )
```
